256 devices in a mesh: row: 8 (over y_lo, x), col: 32 (over z, y_hi, core).
Axes of the slice: x: 4, y: 4 (y_hi: 2, y_lo: 2; y = y_hi * 2 + y_lo), z: 8, core: 2. Of those that a mesh axis runs over, the one named last changes fastest.
Arguments:
- pair: bfloat16 [512, 512, 128], P('row', 'col'), may hold values from -6 to 6
- residue_mask: int32 [512], replicated, may hold values 0 or 1
- in_gain: float32 [2, 128], replicated, may hold values from 0.25 to 1.75
- in_bias: float32 [2, 128], replicated, may hold values from -3 to 3
- proj_weight: bfloat16 [2, 128, 512], replicated, may hold values from -0.5 to 0.5
- gate_weight: bfloat16 [2, 128, 128], replicated, may hold values from -0.5 to 0.5
- out_gain: float32 [2, 128], replicated, may hold values from 0.25 to 1.75
- out_bias: float32 [2, 128], replicated, may hold values from -3 to 3
- out_weight: bfloat16 [2, 128, 128], replicated, may hold values from -0.5 to 0.5
Outputs:
- updated: bfloat16 [512, 512, 128], P('row', 'col')
The draws below stay inside these ranges and needn't reach their ends.
All inputs are finite; a program needn't handle non-finite values.
Results may differ from the reference program's by a relative error of at most 0.012.
Values may be sent and summed in bfloat16 or wider, within the bound.
A program may use at most 128 MiB of HBM per device.

```python
import jax
import jax.numpy as jnp
from jax import lax

C = 128
H = 128
N = 512


def plant(array, stream_key, smallest, high):
    index_at = [jax.random.randint(jax.random.fold_in(stream_key, axis), (), 0, length) for axis, length in enumerate(array.shape)]
    main_axis = array.shape.index(max(array.shape))
    beside = index_at[:main_axis] + [(index_at[main_axis] + 1) % array.shape[main_axis]] + index_at[main_axis + 1:]
    return array.at[tuple(index_at)].set(smallest).at[tuple(beside)].set(high)


def levels(stream_key, shape, split, low, top_value):
    loudness = 1.0
    for dim, parts in split:
        draws = jax.random.uniform(jax.random.fold_in(jax.random.fold_in(stream_key, 6), dim), (parts,), jnp.float32, low / len(split), top_value / len(split))
        loudness = loudness * jnp.repeat(jnp.exp(draws), shape[dim] // parts).reshape((-1,) + (1,) * (len(shape) - 1 - dim))
    return loudness


def normal_values(key, dims, scale, reach, split=(), dtype=jnp.bfloat16):
    loudness = levels(key, dims, split, -0.22, 0.18) if split else 1.0
    values = jax.random.normal(key, dims, jnp.float32) * scale * loudness
    return jnp.minimum(jnp.maximum(values, -reach), reach).astype(dtype)


def setup_inputs(seed: int = 0) -> dict:
    key_of = jax.random.split(jax.random.key(seed), 10)
    pair = normal_values(key_of[0], (N, N, C), 1.0, 6.0, ((0, 8), (1, 32)))
    residue_mask = plant((jax.random.randint(key_of[1], (N,), 0, 8) < 7).astype(jnp.int32), jax.random.fold_in(key_of[1], 1), 0, 1)
    in_gain = jnp.clip(1.0 + 0.15 * jax.random.normal(key_of[2], (2, C), jnp.float32), 0.25, 1.75)
    in_bias = normal_values(key_of[3], (2, C), 0.5, 3.0, (), jnp.float32)
    proj_weight = normal_values(key_of[4], (2, C, 4 * H), C ** -0.5, 0.5)
    gate_weight = normal_values(key_of[5], (2, C, C), C ** -0.5, 0.5)
    out_gain = jnp.clip(1.0 + 0.15 * jax.random.normal(key_of[6], (2, H), jnp.float32), 0.25, 1.75)
    out_bias = normal_values(key_of[7], (2, H), 0.5, 3.0, (), jnp.float32)
    out_weight = normal_values(key_of[8], (2, H, C), H ** -0.5, 0.5)
    return {"pair": pair, "residue_mask": residue_mask, "in_gain": in_gain, "in_bias": in_bias, "proj_weight": proj_weight, "gate_weight": gate_weight, "out_gain": out_gain, "out_bias": out_bias, "out_weight": out_weight}


def layer_norm(values, gain, bias):
    center = values - lax.optimization_barrier(jnp.mean(values, axis=-1, keepdims=True))
    spread = lax.optimization_barrier(jnp.mean(center * center, axis=-1, keepdims=True))
    return center * lax.rsqrt(spread + 1e-05) * gain + bias

def factors(tile, mask_rows, mask_cols, gain, bias, w_proj, w_gate):
    rows_here, cols_here, width = tile.shape
    normed = layer_norm(tile.astype(jnp.float32), gain, bias).astype(jnp.bfloat16)
    flat = normed.reshape(rows_here * cols_here, width)
    proj = jnp.dot(flat, w_proj, preferred_element_type=jnp.float32).reshape(rows_here, cols_here, 4 * H)
    masking = (mask_rows[:, None] * mask_cols[None, :])[:, :, None]
    left = (jax.nn.sigmoid(proj[..., :H]) * proj[..., H:2 * H] * masking).astype(jnp.bfloat16)
    right = (jax.nn.sigmoid(proj[..., 2 * H:3 * H]) * proj[..., 3 * H:] * masking).astype(jnp.bfloat16)
    gated = jax.nn.sigmoid(jnp.dot(flat, w_gate, preferred_element_type=jnp.float32)).reshape(rows_here, cols_here, width)
    return (left, right, gated)

def block(current, mask, gain, bias, w_proj, w_gate, o_gain, o_bias, w_out, incoming):
    step_rows = min(N, 128)
    count = N // step_rows

    def rowwork(args):
        tile, mask_rows = args
        return factors(tile, mask_rows, mask, gain, bias, w_proj, w_gate)
    left, right, gated = lax.map(rowwork, (current.reshape(count, step_rows, N, C), mask.reshape(count, step_rows)))
    left = left.reshape(N, N, H).astype(jnp.float32)
    right = right.reshape(N, N, H).astype(jnp.float32)
    gated = gated.reshape(N, N, C)
    if incoming:
        mixed = jnp.einsum('kic,kjc->ijc', left, right, precision=lax.Precision.HIGHEST)
    else:
        mixed = jnp.einsum('ikc,jkc->ijc', left, right, precision=lax.Precision.HIGHEST)
    normed = layer_norm(mixed, o_gain, o_bias).astype(jnp.bfloat16)
    update = jnp.dot(normed.reshape(N * N, H), w_out, preferred_element_type=jnp.float32).reshape(N, N, C)
    return (current.astype(jnp.float32) + gated * update).astype(jnp.bfloat16)

def reference(pair, residue_mask, in_gain, in_bias, proj_weight, gate_weight, out_gain, out_bias, out_weight):
    mask = residue_mask.astype(jnp.float32)
    current = pair
    for layer in range(2):
        current = block(current, mask, in_gain[layer], in_bias[layer], proj_weight[layer], gate_weight[layer], out_gain[layer], out_bias[layer], out_weight[layer], layer == 1)
    return current
```

```python
import jax
import jax.numpy as jnp
from jax import lax
from jax.experimental import pallas as pl
from jax.experimental.pallas import tpu as pltpu
from jax.sharding import PartitionSpec as P

MESH = pl.DeviceIdType.MESH
F32 = jnp.float32
BF16 = jnp.bfloat16
ROWS, COLS = 8, 32
TR, TC = 64, 16
CH = 128
POS = TR * TC


def kernel(
    pair_hbm, mask_hbm, gain_hbm, bias_hbm, wp_hbm, wg_hbm, ogain_hbm, obias_hbm, wo_hbm,
    out_ref,
    pair_ref, mask_in, gain_ref, bias_ref, wp_ref, wg_ref, ogain_ref, obias_ref, wo_ref,
    wide, cur, gate, stage, masks, means, rstds, normed, wpt, wgt, wot, gains,
    tile, recv1, recv2, back1, back2, swap1, swap2, mine_r, mine_l, outgoing,
    load_sem, hop_sem, send_sem, in_sem, swap_send, swap_recv, ret_send, ret_recv,
):
    row = lax.axis_index("row")
    col = lax.axis_index("col")
    core = lax.rem(col, 2)
    sibling = col + 1 - 2 * core
    x, y_lo = lax.rem(row, 4), row // 4
    z, y_hi = col // 4, lax.rem(col // 2, 2)

    def diagonal(depth):
        return lax.rem(x - depth + 8, 4)

    def channel_of(depth):
        key = diagonal(depth)
        return (lax.rem(key, 2) * 4 + key // 2 * 2 + y_lo) * 16 + depth * 2 + y_hi

    own = channel_of(z)
    colour_here = lax.rem(diagonal(z), 2)
    loads = [
        pltpu.make_async_copy(src, dst, load_sem.at[n])
        for n, (src, dst) in enumerate([
            (pair_hbm, pair_ref), (mask_hbm, mask_in), (gain_hbm, gain_ref), (bias_hbm, bias_ref), (wp_hbm, wp_ref),
            (wg_hbm, wg_ref), (ogain_hbm, ogain_ref), (obias_hbm, obias_ref), (wo_hbm, wo_ref),
        ])
    ]
    for load in loads:
        load.start()

    barrier = pltpu.get_barrier_semaphore()

    @pl.loop(1, ROWS)
    def _(d):
        pl.semaphore_signal(barrier, inc=1, device_id=(lax.rem(row + d, ROWS), col), device_id_type=MESH)

    @pl.loop(1, COLS)
    def _(d):
        pl.semaphore_signal(barrier, inc=1, device_id=(row, lax.rem(col + d, COLS)), device_id_type=MESH)

    def second_hop():
        pl.semaphore_wait(barrier, ROWS - 1 + COLS - 1)

        @pl.loop(1, COLS)
        def _(d):
            pl.semaphore_signal(hop_sem, inc=1, device_id=(row, lax.rem(col + d, COLS)), device_id_type=MESH)

    order = [(b, g, e) for b in range(2) for g in range(4) for e in range(2)]

    def make_masks():
        lane = lax.broadcasted_iota(jnp.int32, (8, CH), 1)
        mask = mask_in[...].astype(F32)
        number = lax.broadcasted_iota(jnp.int32, (8, 512), 1)
        sub = lax.broadcasted_iota(jnp.int32, (8, 512), 0)
        even_b = jnp.sum(jnp.where(number == TC * col + 2 * sub, mask, 0.0), axis=1, keepdims=True)
        odd_b = jnp.sum(jnp.where(number == TC * col + 2 * sub + 1, mask, 0.0), axis=1, keepdims=True)
        mask_b = jnp.where(lane < 64, even_b, odd_b)
        lane_n = lax.broadcasted_iota(jnp.int32, (512, CH), 1)
        row_n = lax.broadcasted_iota(jnp.int32, (512, CH), 0)
        a_of = ((lane_n // 16) % 4) * 16 + ((lane_n // 8) % 2) + 2 * (lane_n % 8)
        pick = jnp.where(row_n == TR * row + a_of, 1.0, 0.0).astype(BF16)
        mask_a = jnp.dot(jnp.broadcast_to(mask, (8, 512)).astype(BF16), pick, preferred_element_type=F32)
        masks[...] = mask_a * mask_b

    def spread_out(ref, layer, n):
        gains[layer, n] = jnp.broadcast_to(ref[layer : layer + 1, :], (CH, CH)).T

    def prepare(layer):
        turned = wp_ref[layer].astype(F32).T.astype(BF16)
        for g in range(8):
            for q in range(4):
                wpt[layer, g, 16 * q : 16 * q + 16, :] = turned[128 * q + 16 * g : 128 * q + 16 * g + 16]
        spread_out(gain_ref, layer, 0)
        spread_out(bias_ref, layer, 1)

    def prepare_out(layer):
        wgt[layer] = wg_ref[layer].astype(F32).T.astype(BF16)
        wot[layer] = wo_ref[layer].astype(F32).T.astype(BF16)
        spread_out(ogain_ref, layer, 2)
        spread_out(obias_ref, layer, 3)

    def normalize(layer, s, values):
        center = values - jnp.mean(values, axis=0, keepdims=True)
        spread = jnp.mean(center * center, axis=0, keepdims=True)
        scaled = center * lax.rsqrt(spread + 1e-05) * gains[layer, 0] + gains[layer, 1]
        normed[:, CH * s : CH * s + CH] = scaled.astype(BF16)
        cur[s] = values

    def send(src, dst, to_row, to_col, send_sem, recv_sem, here):
        def local():
            pltpu.make_async_copy(src, dst, recv_sem).start()

        def remote():
            pltpu.make_async_remote_copy(
                src_ref=src, dst_ref=dst, send_sem=send_sem, recv_sem=recv_sem,
                device_id=(to_row, to_col), device_id_type=MESH,
            ).start()

        if here is None:
            remote()
        else:
            pl.when(here)(local)
            pl.when(jnp.logical_not(here))(remote)

    def sent(buffer, sem, home):
        count = buffer.shape[0]

        @pl.when(home)
        def _():
            part = buffer.at[pl.ds(0, count - 1)]
            pltpu.make_async_copy(part, part, sem).wait()

        @pl.when(jnp.logical_not(home))
        def _():
            pltpu.make_async_copy(buffer, buffer, sem).wait()

    def arrived(buffer, sem):
        pltpu.make_async_copy(buffer, buffer, sem).wait()

    def scatter(layer):
        to_core = y_lo if layer == 0 else col // 16
        slot = x * COLS + col if layer == 0 else row * 16 + lax.rem(col, 16)
        dst = (recv1 if layer == 0 else recv2).at[slot]
        depths = [lax.rem(z + d, 8) for d in range(8)]
        lows = [y_lo, 1 - y_lo]
        highs = [y_hi, 1 - y_hi]

        def key_of(depth, colour, turn):
            return colour + 2 * lax.rem(diagonal(depth) // 2 + turn // 2, 2)

        @pl.loop(0, 8)
        def _(g):
            colour, turn = g // 4, lax.rem(g, 4)
            key = key_of(z, colour, turn)
            low = lax.rem(y_lo + turn, 2)
            block = colour * 4 + key // 2 * 2 + low
            proj = jnp.dot(wpt[layer, block], normed[...], preferred_element_type=F32)
            left = jax.nn.sigmoid(proj[0:16]) * proj[16:32]
            right = jax.nn.sigmoid(proj[32:48]) * proj[48:64]
            for s in range(8):
                keep = masks[s : s + 1, :]
                stage[pl.ds(s, 16, stride=16), :] = left[:, CH * s : CH * s + CH] * keep
                stage[pl.ds(s + 8, 16, stride=16), :] = right[:, CH * s : CH * s + CH] * keep
            first = block * 16
            tile[pl.ds(first, 16)] = stage[0:256, :].reshape(16, 16, CH).astype(BF16)
            to_rows = [low * 4 + lax.rem(key + z + d, 4) for d in range(4)]

            def direct(dz, dh, here=None):
                send(
                    tile.at[first + depths[dz] * 2 + highs[dh]], dst,
                    to_rows[dz % 4], depths[dz] * 4 + highs[dh] * 2 + to_core,
                    send_sem.at[layer], in_sem.at[layer], here,
                )

            for n, (dh, dz) in enumerate([(dh, dz) for dh in range(2) for dz in (0, 3, 6, 1, 4, 7, 2, 5)]):
                here = jnp.logical_and(g == 4 * colour_here, to_core == core) if n == 0 else None
                direct(dz, dh, here)

        return to_core == core

    def make_gate(layer):
        for s in range(8):
            part = jnp.dot(wgt[layer], normed[:, CH * s : CH * s + CH], preferred_element_type=F32)
            gate[s] = jax.nn.sigmoid(part)

    def merge(first, second):
        low = lax.broadcasted_iota(jnp.int32, first.shape, 2) < 64
        even = jnp.where(low, first, pltpu.roll(second, 64, 2))
        odd = jnp.where(low, pltpu.roll(first, 64, 2), second)
        return even, odd

    def gather(layer):
        recv, width, pairs = (recv1, 32, 2) if layer == 0 else (recv2, 16, 4)
        for p in range(pairs):
            first = recv[2 * p * width : (2 * p + 1) * width].astype(F32)
            second = recv[(2 * p + 1) * width : (2 * p + 2) * width].astype(F32)
            even, odd = merge(first, second)
            left = jnp.concatenate([even[:, :8], odd[:, :8]], axis=1).reshape(width * 16, CH)
            right = jnp.concatenate([even[:, 8:], odd[:, 8:]], axis=1).reshape(width * 16, CH)
            if layer == 0:
                mine_l[0:512, 128 * p : 128 * p + 128] = left.astype(BF16)
                mine_r[128 * p : 128 * p + 128, :] = right.T.astype(BF16)
            else:
                mine_l[512:768, 128 * p : 128 * p + 128] = left.astype(BF16)
                mine_r[:, 128 * p : 128 * p + 128] = right.astype(BF16)

    def quadrant(layer, q, right, dst):
        if layer == 0:
            mixed = jnp.dot(right, mine_l[0:512, 0:256], preferred_element_type=F32)
        else:
            mixed = lax.dot_general(right, mine_l[512:768, :], (((1,), (1,)), ((), ())), preferred_element_type=F32)
        for p in range(2):
            block = mixed[:, 128 * p : 128 * p + 128].reshape(16, 16, CH)
            even, odd = merge(block[:, :8], block[:, 8:])
            base = q * 64 + p * 32
            outgoing[base : base + 16] = even.astype(BF16)
            outgoing[base + 16 : base + 32] = odd.astype(BF16)
        side = core if q == 0 else 1 - core
        z_low = lax.rem(z, 4)
        cells = [
            (dz, lax.rem(z_low + dz, 4) * 4 + (y_hi if dy == 0 else 1 - y_hi) * 2 + (core if dc == 0 else 1 - core))
            for dy in range(2) for dc in range(2) for dz in (0, 2, 1, 3)
        ]

        @pl.loop(0, 4)
        def _(d):
            lines = [lax.rem(x + d + n, 4) for n in range(4)]
            for n, (dz, cell) in enumerate(cells):
                r = lines[dz]
                here = None
                if n == 0:
                    here = jnp.logical_and(d == 0, jnp.logical_and(y_lo == core, z // 4 == side))
                src = outgoing.at[q * 64 + r * 16 + cell]

                send(
                    src, dst, core * 4 + r, side * 16 + cell,
                    ret_send.at[layer], ret_recv.at[2 * layer + colour_here], here,
                )

    def multiply(layer):
        back = (back1 if layer == 0 else back2).at[own]
        swap = swap1 if layer == 0 else swap2
        gather(layer)
        exchange = pltpu.make_async_remote_copy(
            src_ref=mine_r, dst_ref=swap, send_sem=swap_send.at[layer], recv_sem=swap_recv.at[layer],
            device_id=(row, sibling), device_id_type=MESH,
        )
        exchange.start()
        quadrant(layer, 0, mine_r[...], back)
        exchange.wait_recv()
        quadrant(layer, 1, swap[...], back)
        exchange.wait_send()

    def finish(layer):
        back = back1 if layer == 0 else back2
        halves = []
        for colour in range(2):
            arrived(back.at[pl.ds(64 * colour, 64)], ret_recv.at[2 * layer + colour])
            total = jnp.zeros((8, CH), F32)
            for g in range(4 * colour, 4 * colour + 4):
                part = back[16 * g : 16 * g + 16].astype(F32)
                wide[128 * g : 128 * g + 128, :] = part.reshape(128, CH)
                total = total + jnp.sum(part, axis=0)
            mean = total * (1.0 / 64)
            total = jnp.zeros((8, CH), F32)
            for g in range(4 * colour, 4 * colour + 4):
                part = wide[128 * g : 128 * g + 128, :].reshape(16, 8, CH) - mean[None]
                total = total + jnp.sum(part * part, axis=0)
            halves.append((mean, total))
        (mean0, total0), (mean1, total1) = halves
        apart = 0.5 * (mean0 - mean1)
        means[...] = 0.5 * (mean0 + mean1)
        rstds[...] = lax.rsqrt((total0 + total1) * (1.0 / CH) + apart * apart + 1e-05)

    def updated(layer, s):
        mixed = wide[pl.ds(s, CH, stride=8), :]
        out_normed = (mixed - means[s : s + 1, :]) * rstds[s : s + 1, :] * gains[layer, 2] + gains[layer, 3]
        update = jnp.dot(wot[layer], out_normed.astype(BF16), preferred_element_type=F32)
        return cur[s] + gate[s] * update

    for load in loads:
        load.wait()
    prepare(0)
    make_masks()
    second_hop()
    wide[...] = pair_ref[...].astype(F32).reshape(POS, CH)
    for s in range(8):
        rows = [wide[pl.ds(256 * g + 16 * e + 2 * s + b, 8, stride=32), :] for b, g, e in order]
        normalize(0, s, jnp.concatenate(rows, axis=0).T)
    pl.semaphore_wait(hop_sem, COLS - 1)
    home1 = scatter(0)
    prepare_out(0)
    make_gate(0)
    prepare(1)
    prepare_out(1)
    arrived(recv1, in_sem.at[0])
    multiply(0)
    sent(tile, send_sem.at[0], home1)
    finish(0)
    for s in range(8):
        normalize(1, s, updated(0, s).astype(BF16).astype(F32))
    home2 = scatter(1)
    make_gate(1)
    sent(outgoing, ret_send.at[0], home1)
    arrived(recv2, in_sem.at[1])
    multiply(1)
    sent(tile, send_sem.at[1], home2)
    finish(1)
    for s in range(8):
        values = updated(1, s).T
        for n, (b, g, e) in enumerate(order):
            stage[pl.ds(256 * g + 16 * e + 2 * s + b, 8, stride=32), :] = values[8 * n : 8 * n + 8]
    out_ref[...] = stage[...].reshape(TR, TC, CH).astype(BF16)
    sent(outgoing, ret_send.at[1], home1)


def shards(pair, residue_mask, in_gain, in_bias, proj_weight, gate_weight, out_gain, out_bias, out_weight):
    arguments = (
        pair, residue_mask.reshape(1, 512), in_gain, in_bias, proj_weight, gate_weight, out_gain, out_bias, out_weight
    )
    dma = pltpu.SemaphoreType.DMA
    return pl.pallas_call(
        kernel,
        out_shape=pltpu.VMEM((TR, TC, CH), BF16),
        in_specs=[pl.BlockSpec(memory_space=pltpu.HBM)] * 9,
        out_specs=pl.BlockSpec(memory_space=pltpu.VMEM),
        scratch_shapes=[pltpu.VMEM(value.shape, value.dtype) for value in arguments] + [
            pltpu.VMEM((POS, CH), F32),
            pltpu.VMEM((8, CH, CH), F32),
            pltpu.VMEM((8, CH, CH), F32),
            pltpu.VMEM((POS, CH), F32),
            pltpu.VMEM((8, CH), F32),
            pltpu.VMEM((8, CH), F32),
            pltpu.VMEM((8, CH), F32),
            pltpu.VMEM((CH, POS), BF16),
            pltpu.VMEM((2, 8, 64, CH), BF16),
            pltpu.VMEM((2, CH, CH), BF16),
            pltpu.VMEM((2, CH, CH), BF16),
            pltpu.VMEM((2, 4, CH, CH), F32),
            pltpu.VMEM((CH, 16, CH), BF16),
            pltpu.VMEM((CH, 16, CH), BF16),
            pltpu.VMEM((CH, 16, CH), BF16),
            pltpu.VMEM((CH, 8, CH), BF16),
            pltpu.VMEM((CH, 8, CH), BF16),
            pltpu.VMEM((256, 512), BF16),
            pltpu.VMEM((256, 512), BF16),
            pltpu.VMEM((256, 512), BF16),
            pltpu.VMEM((768, 512), BF16),
            pltpu.VMEM((CH, 8, CH), BF16),
            dma((9,)),
            pltpu.SemaphoreType.REGULAR,
            dma((2,)), dma((2,)), dma((2,)), dma((2,)), dma((2,)), dma((4,)),
        ],
        compiler_params=pltpu.CompilerParams(
            collective_id=0, has_side_effects=True, vmem_limit_bytes=48 * 1024 * 1024
        ),
        cost_estimate=pl.CostEstimate(flops=700_000_000, bytes_accessed=4_000_000, transcendentals=1_000_000),
    )(*[pltpu.with_memory_space_constraint(value, pltpu.HBM) for value in arguments])


def solution(mesh):
    placed = (P("row", "col", None), P(), P(), P(), P(), P(), P(), P(), P())
    return jax.shard_map(
        shards, mesh=mesh, in_specs=placed, out_specs=P("row", "col", None), check_vma=False
    )
```

```python
import jax
import jax.numpy as jnp
from jax import lax
from jax.experimental import pallas as pl
from jax.experimental.pallas import tpu as pltpu
from jax.sharding import PartitionSpec as P

MESH = pl.DeviceIdType.MESH
F32 = jnp.float32
BF16 = jnp.bfloat16
ROWS, COLS = 8, 32
TR, TC = 64, 16
CH = 128
POS = TR * TC


def kernel(
    pair_hbm, mask_hbm, gain_hbm, bias_hbm, wp_hbm, wg_hbm, ogain_hbm, obias_hbm, wo_hbm,
    out_ref,
    pair_ref, mask_in, gain_ref, bias_ref, wp_ref, wg_ref, ogain_ref, obias_ref, wo_ref,
    wide, cur, gate, stage, masks, means, rstds, normed, wpt, wgt, wot, gains,
    tile, recv1, recv2, back1, back2, swap1, swap2, mine_r, mine_l, mine_l2, raw_r, outgoing,
    load_sem, hop_sem, send_sem, in_sem, swap_send, swap_recv, ret_send, ret_recv,
):
    row = lax.axis_index("row")
    col = lax.axis_index("col")
    core = lax.rem(col, 2)
    sibling = col + 1 - 2 * core
    x, y_lo = lax.rem(row, 4), row // 4
    z, y_hi = col // 4, lax.rem(col // 2, 2)

    colour_here = lax.rem(x + z, 2)
    own = (colour_here * 8 + z) * 8 + x // 2 * 4 + y_hi * 2 + y_lo
    z_low = lax.rem(z, 4)

    loads = [
        pltpu.make_async_copy(src, dst, load_sem.at[n])
        for n, (src, dst) in enumerate([
            (pair_hbm, pair_ref), (mask_hbm, mask_in), (gain_hbm, gain_ref), (bias_hbm, bias_ref), (wp_hbm, wp_ref),
            (wg_hbm, wg_ref), (ogain_hbm, ogain_ref), (obias_hbm, obias_ref), (wo_hbm, wo_ref),
        ])
    ]
    for load in loads:
        load.start()

    barrier = pltpu.get_barrier_semaphore()

    @pl.loop(1, ROWS)
    def _(d):
        pl.semaphore_signal(barrier, inc=1, device_id=(lax.rem(row + d, ROWS), col), device_id_type=MESH)

    @pl.loop(1, COLS)
    def _(d):
        pl.semaphore_signal(barrier, inc=1, device_id=(row, lax.rem(col + d, COLS)), device_id_type=MESH)

    def second_hop():
        pl.semaphore_wait(barrier, ROWS - 1 + COLS - 1)

        @pl.loop(1, COLS)
        def _(d):
            pl.semaphore_signal(hop_sem, inc=1, device_id=(row, lax.rem(col + d, COLS)), device_id_type=MESH)

    order = [(b, g, e) for b in range(2) for g in range(4) for e in range(2)]

    def make_masks():
        lane = lax.broadcasted_iota(jnp.int32, (8, CH), 1)
        mask = mask_in[...].astype(F32)
        number = lax.broadcasted_iota(jnp.int32, (8, 512), 1)
        sub = lax.broadcasted_iota(jnp.int32, (8, 512), 0)
        even_b = jnp.sum(jnp.where(number == TC * col + 2 * sub, mask, 0.0), axis=1, keepdims=True)
        odd_b = jnp.sum(jnp.where(number == TC * col + 2 * sub + 1, mask, 0.0), axis=1, keepdims=True)
        mask_b = jnp.where(lane < 64, even_b, odd_b)
        lane_n = lax.broadcasted_iota(jnp.int32, (512, CH), 1)
        row_n = lax.broadcasted_iota(jnp.int32, (512, CH), 0)
        a_of = ((lane_n // 16) % 4) * 16 + ((lane_n // 8) % 2) + 2 * (lane_n % 8)
        pick = jnp.where(row_n == TR * row + a_of, 1.0, 0.0).astype(BF16)
        mask_a = jnp.dot(jnp.broadcast_to(mask, (8, 512)).astype(BF16), pick, preferred_element_type=F32)
        masks[...] = mask_a * mask_b

    def spread_out(ref, layer, n):
        gains[layer, n] = jnp.broadcast_to(ref[layer : layer + 1, :], (CH, CH)).T

    def prepare(layer):
        turned = wp_ref[layer].astype(F32).T
        for b in range(16):
            rows = [turned[128 * q + 8 * b : 128 * q + 8 * b + 8] for q in range(4)]
            wpt[layer, b] = jnp.concatenate(rows, axis=0).astype(BF16)
        spread_out(gain_ref, layer, 0)
        spread_out(bias_ref, layer, 1)

    def prepare_out(layer):
        wgt[layer] = wg_ref[layer].astype(F32).T.astype(BF16)
        wot[layer] = wo_ref[layer].astype(F32).T.astype(BF16)
        spread_out(ogain_ref, layer, 2)
        spread_out(obias_ref, layer, 3)

    def normalize(layer, s, values):
        center = values - jnp.mean(values, axis=0, keepdims=True)
        spread = jnp.mean(center * center, axis=0, keepdims=True)
        scaled = center * lax.rsqrt(spread + 1e-05) * gains[layer, 0] + gains[layer, 1]
        normed[:, CH * s : CH * s + CH] = scaled.astype(BF16)
        cur[s] = values

    def send(src, dst, to_row, to_col, send_sem, recv_sem, here):
        def local():
            pltpu.make_async_copy(src, dst, recv_sem).start()

        def remote():
            pltpu.make_async_remote_copy(
                src_ref=src, dst_ref=dst, send_sem=send_sem, recv_sem=recv_sem,
                device_id=(to_row, to_col), device_id_type=MESH,
            ).start()

        if here is None:
            remote()
        else:
            pl.when(here)(local)
            pl.when(jnp.logical_not(here))(remote)

    def sent(buffer, sem, home):
        count = buffer.shape[0]

        @pl.when(home)
        def _():
            part = buffer.at[pl.ds(0, count - 1)]
            pltpu.make_async_copy(part, part, sem).wait()

        @pl.when(jnp.logical_not(home))
        def _():
            pltpu.make_async_copy(buffer, buffer, sem).wait()

    def arrived(buffer, sem):
        pltpu.make_async_copy(buffer, buffer, sem).wait()

    def scatter(layer):
        to_core = y_lo if layer == 0 else col // 16
        corner = y_hi * 2 + core
        slot = z * 16 + x * 4 + corner if layer == 0 else z_low * 32 + row * 4 + corner
        dst = (recv1 if layer == 0 else recv2).at[slot]
        lows = [y_lo, 1 - y_lo]
        highs = [y_hi, 1 - y_hi]
        halves = [x // 2, 1 - x // 2]

        @pl.loop(0, 8)
        def _(g):
            colour, step = g // 4, lax.rem(g, 4)
            depths = [lax.rem(z + 4 + step, 8), lax.rem(z + 3 - step, 8)]
            blocks = [colour * 8 + depth for depth in depths]
            weights = jnp.concatenate([wpt[layer, block] for block in blocks], axis=0)
            proj = jnp.dot(weights, normed[...], preferred_element_type=F32)
            left = jnp.concatenate([jax.nn.sigmoid(proj[n : n + 8]) * proj[n + 8 : n + 16] for n in (0, 32)], axis=0)
            right = jnp.concatenate([jax.nn.sigmoid(proj[n : n + 8]) * proj[n + 8 : n + 16] for n in (16, 48)], axis=0)
            for s in range(8):
                keep = masks[s : s + 1, :]
                stage[pl.ds(s, 16, stride=16), :] = left[:, CH * s : CH * s + CH] * keep
                stage[pl.ds(s + 8, 16, stride=16), :] = right[:, CH * s : CH * s + CH] * keep
            for n, block in enumerate(blocks):
                tile[pl.ds(block * 8, 8)] = stage[128 * n : 128 * n + 128, :].reshape(8, 16, CH).astype(BF16)
            odd = [lax.rem(colour + depth, 2) for depth in depths]
            for dx in (1, 0):
                for dh in (1, 0):
                    for dl in (1, 0):
                        for n in range(2):
                            here = None
                            if n == 1 and dx + dh + dl == 0:
                                here = jnp.logical_and(g == 4 * colour_here + 3, to_core == core)
                            send(
                                tile.at[blocks[n] * 8 + halves[dx] * 4 + highs[dh] * 2 + lows[dl]], dst,
                                lows[dl] * 4 + halves[dx] * 2 + odd[n], depths[n] * 4 + highs[dh] * 2 + to_core,
                                send_sem.at[layer], in_sem.at[8 * layer + z], here,
                            )

        return to_core == core

    def make_gate(layer):
        for s in range(8):
            part = jnp.dot(wgt[layer], normed[:, CH * s : CH * s + CH], preferred_element_type=F32)
            gate[s] = jax.nn.sigmoid(part)

    def merge(first, second):
        low = lax.broadcasted_iota(jnp.int32, first.shape, 2) < 64
        even = jnp.where(low, first, pltpu.roll(second, 64, 2))
        odd = jnp.where(low, pltpu.roll(first, 64, 2), second)
        return even, odd

    def far_first(step, same):
        falling = (z_low < 2) == same
        return jnp.where(falling, 3 - step, step)

    def gather(layer):
        for step in range(8 if layer == 0 else 4):
            if layer == 0:
                recv, width, pairs = recv1, 16, 2
                place = lax.rem(z + (4, 5, 3, 6, 2, 7, 1, 0)[step], 8)
                sem = in_sem.at[place]
            else:
                recv, width, pairs = recv2, 32, 4
                place = far_first(step, z // 4 == core)
                sem = in_sem.at[8 + core * 4 + place]
            arrived(recv.at[pl.ds(place * width, width)], sem)
            rows = pl.ds(pl.multiple_of(place * 64, 64), 64)
            for p in range(pairs):
                first = recv[pl.ds(place * width + 8 * p, 4)].astype(F32)
                second = recv[pl.ds(place * width + 8 * p + 4, 4)].astype(F32)
                even, odd = merge(first, second)
                left = jnp.concatenate([even[:, :8], odd[:, :8]], axis=1).reshape(64, CH)
                right = jnp.concatenate([even[:, 8:], odd[:, 8:]], axis=1).reshape(64, CH)
                if layer == 0:
                    mine_l[rows, 128 * p : 128 * p + 128] = left.astype(BF16)
                    raw_r[rows, 128 * p : 128 * p + 128] = right
                else:
                    mine_l2[rows, 128 * p : 128 * p + 128] = left.astype(BF16)
                    mine_r[rows, 128 * p : 128 * p + 128] = right.astype(BF16)
        if layer == 0:
            for p in range(2):
                mine_r[128 * p : 128 * p + 128, :] = raw_r[:, 128 * p : 128 * p + 128].T.astype(BF16)

    def quadrant(layer, q, right, dst):
        if layer == 0:
            mixed = jnp.dot(right, mine_l[...], preferred_element_type=F32)
        else:
            mixed = lax.dot_general(right, mine_l2[...], (((1,), (1,)), ((), ())), preferred_element_type=F32)
        for p in range(2):
            block = mixed[:, 128 * p : 128 * p + 128].reshape(16, 16, CH)
            even, odd = merge(block[:, :8], block[:, 8:])
            base = q * 64 + p * 32
            outgoing[base : base + 16] = even.astype(BF16)
            outgoing[base + 16 : base + 32] = odd.astype(BF16)
        side = core if q == 0 else 1 - core
        lines = [lax.rem(x + n, 4) for n in range(4)]
        corners = [(y_hi if dy == 0 else 1 - y_hi) * 2 + (core if dc == 0 else 1 - core) for dy in range(2) for dc in range(2)]

        @pl.loop(0, 4)
        def _(step):
            depth = far_first(step, z // 4 == side)
            for corner in (3, 2, 1, 0):
                for dx in (2, 1, 3, 0):
                    here = None
                    if corner == 0 and dx == 0:
                        here = jnp.logical_and(y_lo == core, side * 4 + depth == z)
                    cell = depth * 4 + corners[corner]
                    send(
                        outgoing.at[q * 64 + lines[dx] * 16 + cell], dst, core * 4 + lines[dx], side * 16 + cell,
                        ret_send.at[layer], ret_recv.at[2 * layer + colour_here], here,
                    )

    def multiply(layer):
        back = (back1 if layer == 0 else back2).at[own]
        swap = swap1 if layer == 0 else swap2
        gather(layer)
        exchange = pltpu.make_async_remote_copy(
            src_ref=mine_r, dst_ref=swap, send_sem=swap_send.at[layer], recv_sem=swap_recv.at[layer],
            device_id=(row, sibling), device_id_type=MESH,
        )
        exchange.start()
        quadrant(layer, 0, mine_r[...], back)
        exchange.wait_recv()
        quadrant(layer, 1, swap[...], back)
        exchange.wait_send()

    def finish(layer):
        back = back1 if layer == 0 else back2
        halves = []
        for colour in range(2):
            arrived(back.at[pl.ds(64 * colour, 64)], ret_recv.at[2 * layer + colour])
            total = jnp.zeros((8, CH), F32)
            for g in range(4 * colour, 4 * colour + 4):
                part = back[16 * g : 16 * g + 16].astype(F32)
                wide[128 * g : 128 * g + 128, :] = part.reshape(128, CH)
                total = total + jnp.sum(part, axis=0)
            mean = total * (1.0 / 64)
            total = jnp.zeros((8, CH), F32)
            for g in range(4 * colour, 4 * colour + 4):
                part = wide[128 * g : 128 * g + 128, :].reshape(16, 8, CH) - mean[None]
                total = total + jnp.sum(part * part, axis=0)
            halves.append((mean, total))
        (mean0, total0), (mean1, total1) = halves
        apart = 0.5 * (mean0 - mean1)
        means[...] = 0.5 * (mean0 + mean1)
        rstds[...] = lax.rsqrt((total0 + total1) * (1.0 / CH) + apart * apart + 1e-05)

    def updated(layer, s):
        mixed = wide[pl.ds(s, CH, stride=8), :]
        out_normed = (mixed - means[s : s + 1, :]) * rstds[s : s + 1, :] * gains[layer, 2] + gains[layer, 3]
        update = jnp.dot(wot[layer], out_normed.astype(BF16), preferred_element_type=F32)
        return cur[s] + gate[s] * update

    for load in loads:
        load.wait()
    prepare(0)
    make_masks()
    second_hop()
    wide[...] = pair_ref[...].astype(F32).reshape(POS, CH)
    for s in range(8):
        rows = [wide[pl.ds(256 * g + 16 * e + 2 * s + b, 8, stride=32), :] for b, g, e in order]
        normalize(0, s, jnp.concatenate(rows, axis=0).T)
    pl.semaphore_wait(hop_sem, COLS - 1)
    home1 = scatter(0)
    multiply(0)
    prepare_out(0)
    make_gate(0)
    prepare(1)
    prepare_out(1)
    sent(tile, send_sem.at[0], home1)
    finish(0)
    for s in range(8):
        normalize(1, s, updated(0, s).astype(BF16).astype(F32))
    home2 = scatter(1)
    sent(outgoing, ret_send.at[0], home1)
    multiply(1)
    make_gate(1)
    sent(tile, send_sem.at[1], home2)
    finish(1)
    for s in range(8):
        values = updated(1, s).T
        for n, (b, g, e) in enumerate(order):
            stage[pl.ds(256 * g + 16 * e + 2 * s + b, 8, stride=32), :] = values[8 * n : 8 * n + 8]
    out_ref[...] = stage[...].reshape(TR, TC, CH).astype(BF16)
    sent(outgoing, ret_send.at[1], home1)


def shards(pair, residue_mask, in_gain, in_bias, proj_weight, gate_weight, out_gain, out_bias, out_weight):
    arguments = (
        pair, residue_mask.reshape(1, 512), in_gain, in_bias, proj_weight, gate_weight, out_gain, out_bias, out_weight
    )
    dma = pltpu.SemaphoreType.DMA
    return pl.pallas_call(
        kernel,
        out_shape=pltpu.VMEM((TR, TC, CH), BF16),
        in_specs=[pl.BlockSpec(memory_space=pltpu.HBM)] * 9,
        out_specs=pl.BlockSpec(memory_space=pltpu.VMEM),
        scratch_shapes=[pltpu.VMEM(value.shape, value.dtype) for value in arguments] + [
            pltpu.VMEM((POS, CH), F32),
            pltpu.VMEM((8, CH, CH), F32),
            pltpu.VMEM((8, CH, CH), F32),
            pltpu.VMEM((POS, CH), F32),
            pltpu.VMEM((8, CH), F32),
            pltpu.VMEM((8, CH), F32),
            pltpu.VMEM((8, CH), F32),
            pltpu.VMEM((CH, POS), BF16),
            pltpu.VMEM((2, 16, 32, CH), BF16),
            pltpu.VMEM((2, CH, CH), BF16),
            pltpu.VMEM((2, CH, CH), BF16),
            pltpu.VMEM((2, 4, CH, CH), F32),
            pltpu.VMEM((CH, 16, CH), BF16),
            pltpu.VMEM((CH, 16, CH), BF16),
            pltpu.VMEM((CH, 16, CH), BF16),
            pltpu.VMEM((CH, 8, CH), BF16),
            pltpu.VMEM((CH, 8, CH), BF16),
            pltpu.VMEM((256, 512), BF16),
            pltpu.VMEM((256, 512), BF16),
            pltpu.VMEM((256, 512), BF16),
            pltpu.VMEM((512, 256), BF16),
            pltpu.VMEM((256, 512), BF16),
            pltpu.VMEM((512, 256), F32),
            pltpu.VMEM((CH, 8, CH), BF16),
            dma((9,)),
            pltpu.SemaphoreType.REGULAR,
            dma((2,)), dma((16,)), dma((2,)), dma((2,)), dma((2,)), dma((4,)),
        ],
        compiler_params=pltpu.CompilerParams(
            collective_id=0, has_side_effects=True, vmem_limit_bytes=48 * 1024 * 1024
        ),
        cost_estimate=pl.CostEstimate(flops=700_000_000, bytes_accessed=4_000_000, transcendentals=1_000_000),
    )(*[pltpu.with_memory_space_constraint(value, pltpu.HBM) for value in arguments])


def solution(mesh):
    placed = (P("row", "col", None), P(), P(), P(), P(), P(), P(), P(), P())
    return jax.shard_map(
        shards, mesh=mesh, in_specs=placed, out_specs=P("row", "col", None), check_vma=False
    )
```

```python
import jax
import jax.numpy as jnp
from jax import lax
from jax.experimental import pallas as pl
from jax.experimental.pallas import tpu as pltpu
from jax.sharding import PartitionSpec as P

MESH = pl.DeviceIdType.MESH
F32 = jnp.float32
BF16 = jnp.bfloat16
ROWS, COLS = 8, 32
TR, TC = 64, 16
CH = 128
POS = TR * TC


def kernel(
    pair_hbm, mask_hbm, gain_hbm, bias_hbm, wp_hbm, wg_hbm, ogain_hbm, obias_hbm, wo_hbm,
    out_ref,
    pair_ref, mask_in, gain_ref, bias_ref, wp_ref, wg_ref, ogain_ref, obias_ref, wo_ref,
    wide, cur, gate, stage, masks, means, rstds, normed, wpt, wgt, wot, gains,
    tile, recv1, recv2, back1, back2, swap1, swap2, mine_r, mine_l, mine_l2, raw_r, outgoing,
    load_sem, hop_sem, send_sem, in_sem, swap_send, swap_recv, ret_send, ret_recv,
):
    row = lax.axis_index("row")
    col = lax.axis_index("col")
    core = lax.rem(col, 2)
    sibling = col + 1 - 2 * core
    x, y_lo = lax.rem(row, 4), row // 4
    z, y_hi = col // 4, lax.rem(col // 2, 2)

    colour_here = lax.rem(x + z, 2)
    own = (colour_here * 8 + z) * 8 + x // 2 * 4 + y_hi * 2 + y_lo
    z_low = lax.rem(z, 4)

    loads = [
        pltpu.make_async_copy(src, dst, load_sem.at[n])
        for n, (src, dst) in enumerate([
            (pair_hbm, pair_ref), (mask_hbm, mask_in), (gain_hbm, gain_ref), (bias_hbm, bias_ref), (wp_hbm, wp_ref),
            (wg_hbm, wg_ref), (ogain_hbm, ogain_ref), (obias_hbm, obias_ref), (wo_hbm, wo_ref),
        ])
    ]
    for load in loads:
        load.start()

    barrier = pltpu.get_barrier_semaphore()

    @pl.loop(1, ROWS)
    def _(d):
        pl.semaphore_signal(barrier, inc=1, device_id=(lax.rem(row + d, ROWS), col), device_id_type=MESH)

    @pl.loop(1, COLS)
    def _(d):
        pl.semaphore_signal(barrier, inc=1, device_id=(row, lax.rem(col + d, COLS)), device_id_type=MESH)

    def second_hop():
        pl.semaphore_wait(barrier, ROWS - 1 + COLS - 1)

        @pl.loop(1, COLS)
        def _(d):
            pl.semaphore_signal(hop_sem, inc=1, device_id=(row, lax.rem(col + d, COLS)), device_id_type=MESH)

    order = [(b, g, e) for b in range(2) for g in range(4) for e in range(2)]

    def make_masks():
        lane = lax.broadcasted_iota(jnp.int32, (8, CH), 1)
        mask = mask_in[...].astype(F32)
        number = lax.broadcasted_iota(jnp.int32, (8, 512), 1)
        sub = lax.broadcasted_iota(jnp.int32, (8, 512), 0)
        even_b = jnp.sum(jnp.where(number == TC * col + 2 * sub, mask, 0.0), axis=1, keepdims=True)
        odd_b = jnp.sum(jnp.where(number == TC * col + 2 * sub + 1, mask, 0.0), axis=1, keepdims=True)
        mask_b = jnp.where(lane < 64, even_b, odd_b)
        lane_n = lax.broadcasted_iota(jnp.int32, (512, CH), 1)
        row_n = lax.broadcasted_iota(jnp.int32, (512, CH), 0)
        a_of = ((lane_n // 16) % 4) * 16 + ((lane_n // 8) % 2) + 2 * (lane_n % 8)
        pick = jnp.where(row_n == TR * row + a_of, 1.0, 0.0).astype(BF16)
        mask_a = jnp.dot(jnp.broadcast_to(mask, (8, 512)).astype(BF16), pick, preferred_element_type=F32)
        masks[...] = mask_a * mask_b

    def spread_out(ref, layer, n):
        gains[layer, n] = jnp.broadcast_to(ref[layer : layer + 1, :], (CH, CH)).T

    def prepare(layer):
        turned = wp_ref[layer].astype(F32).T
        for b in range(16):
            rows = [turned[128 * q + 8 * b : 128 * q + 8 * b + 8] for q in range(4)]
            wpt[layer, b] = jnp.concatenate(rows, axis=0).astype(BF16)
        spread_out(gain_ref, layer, 0)
        spread_out(bias_ref, layer, 1)

    def prepare_out(layer):
        wgt[layer] = wg_ref[layer].astype(F32).T.astype(BF16)
        wot[layer] = wo_ref[layer].astype(F32).T.astype(BF16)
        spread_out(ogain_ref, layer, 2)
        spread_out(obias_ref, layer, 3)

    def normalize(layer, s, values):
        center = values - jnp.mean(values, axis=0, keepdims=True)
        spread = jnp.mean(center * center, axis=0, keepdims=True)
        scaled = center * lax.rsqrt(spread + 1e-05) * gains[layer, 0] + gains[layer, 1]
        normed[:, CH * s : CH * s + CH] = scaled.astype(BF16)
        cur[s] = values

    def send(src, dst, to_row, to_col, send_sem, recv_sem, here):
        def local():
            pltpu.make_async_copy(src, dst, recv_sem).start()

        def remote():
            pltpu.make_async_remote_copy(
                src_ref=src, dst_ref=dst, send_sem=send_sem, recv_sem=recv_sem,
                device_id=(to_row, to_col), device_id_type=MESH,
            ).start()

        if here is None:
            remote()
        else:
            pl.when(here)(local)
            pl.when(jnp.logical_not(here))(remote)

    def sent(buffer, sem, home):
        count = buffer.shape[0]

        @pl.when(home)
        def _():
            part = buffer.at[pl.ds(0, count - 1)]
            pltpu.make_async_copy(part, part, sem).wait()

        @pl.when(jnp.logical_not(home))
        def _():
            pltpu.make_async_copy(buffer, buffer, sem).wait()

    def arrived(buffer, sem):
        pltpu.make_async_copy(buffer, buffer, sem).wait()

    def scatter(layer):
        to_core = y_lo if layer == 0 else col // 16
        corner = y_hi * 2 + core
        slot = z * 16 + x * 4 + corner if layer == 0 else z_low * 32 + row * 4 + corner
        dst = (recv1 if layer == 0 else recv2).at[slot]
        lows = [y_lo, 1 - y_lo]
        highs = [y_hi, 1 - y_hi]
        halves = [x // 2, 1 - x // 2]

        @pl.loop(0, 8)
        def _(g):
            colour, step = g // 4, lax.rem(g, 4)
            ahead = jnp.where(step == 0, 3, jnp.where(step == 1, 4, 4 - step))
            depths = [lax.rem(z + ahead, 8), lax.rem(z + jnp.where(step == 1, 0, 8 - ahead), 8)]
            blocks = [colour * 8 + depth for depth in depths]
            weights = jnp.concatenate([wpt[layer, block] for block in blocks], axis=0)
            proj = jnp.dot(weights, normed[...], preferred_element_type=F32)
            left = jnp.concatenate([jax.nn.sigmoid(proj[n : n + 8]) * proj[n + 8 : n + 16] for n in (0, 32)], axis=0)
            right = jnp.concatenate([jax.nn.sigmoid(proj[n : n + 8]) * proj[n + 8 : n + 16] for n in (16, 48)], axis=0)
            for s in range(8):
                keep = masks[s : s + 1, :]
                stage[pl.ds(s, 16, stride=16), :] = left[:, CH * s : CH * s + CH] * keep
                stage[pl.ds(s + 8, 16, stride=16), :] = right[:, CH * s : CH * s + CH] * keep
            for n, block in enumerate(blocks):
                tile[pl.ds(block * 8, 8)] = stage[128 * n : 128 * n + 128, :].reshape(8, 16, CH).astype(BF16)
            odd = [lax.rem(colour + depth, 2) for depth in depths]
            for dx in (1, 0):
                for dh in (1, 0):
                    for dl in (1, 0):
                        for n in range(2):
                            here = None
                            if n == 1 and dx + dh + dl == 0:
                                here = jnp.logical_and(g == 4 * colour_here + 1, to_core == core)
                            send(
                                tile.at[blocks[n] * 8 + halves[dx] * 4 + highs[dh] * 2 + lows[dl]], dst,
                                lows[dl] * 4 + halves[dx] * 2 + odd[n], depths[n] * 4 + highs[dh] * 2 + to_core,
                                send_sem.at[layer], in_sem.at[8 * layer + z], here,
                            )

        return to_core == core

    def make_gate(layer):
        for s in range(8):
            part = jnp.dot(wgt[layer], normed[:, CH * s : CH * s + CH], preferred_element_type=F32)
            gate[s] = jax.nn.sigmoid(part)

    def merge(first, second):
        low = lax.broadcasted_iota(jnp.int32, first.shape, 2) < 64
        even = jnp.where(low, first, pltpu.roll(second, 64, 2))
        odd = jnp.where(low, pltpu.roll(first, 64, 2), second)
        return even, odd

    def far_first(step, same):
        falling = (z_low < 2) == same
        return jnp.where(falling, 3 - step, step)

    def gather(layer):
        for step in range(8 if layer == 0 else 4):
            if layer == 0:
                recv, width, pairs = recv1, 16, 2
                place = lax.rem(z + (5, 3, 4, 0, 6, 2, 7, 1)[step], 8)
                sem = in_sem.at[place]
            else:
                recv, width, pairs = recv2, 32, 4
                place = far_first(step, z // 4 == core)
                sem = in_sem.at[8 + core * 4 + place]
            arrived(recv.at[pl.ds(place * width, width)], sem)
            rows = pl.ds(64 * step if layer == 0 else pl.multiple_of(place * 64, 64), 64)
            for p in range(pairs):
                first = recv[pl.ds(place * width + 8 * p, 4)].astype(F32)
                second = recv[pl.ds(place * width + 8 * p + 4, 4)].astype(F32)
                even, odd = merge(first, second)
                left = jnp.concatenate([even[:, :8], odd[:, :8]], axis=1).reshape(64, CH)
                right = jnp.concatenate([even[:, 8:], odd[:, 8:]], axis=1).reshape(64, CH)
                lanes = slice(128 * p, 128 * p + 128)
                if layer == 0:
                    mine_l[rows, lanes] = left.astype(BF16)
                    raw_r[rows, lanes] = right
                else:
                    mine_l2[rows, lanes] = left.astype(BF16)
                    mine_r[rows, lanes] = right.astype(BF16)
                if layer == 0 and step % 2 == 1:
                    block = slice(64 * step - 64, 64 * step + 64)
                    mine_r[lanes, block] = raw_r[block, lanes].T.astype(BF16)

    def quadrant(layer, q, right, dst):
        side = core if q == 0 else 1 - core
        lines = [lax.rem(x + n, 4) for n in range(4)]
        corners = [(y_hi if dy == 0 else 1 - y_hi) * 2 + (core if dc == 0 else 1 - core) for dy in range(2) for dc in range(2)]

        @pl.loop(0, 4)
        def _(step):
            depth = far_first(step, z // 4 == side)
            rows = right[pl.ds(pl.multiple_of(depth * 64, 64), 64), :]
            if layer == 0:
                mixed = jnp.dot(rows, mine_l[...], preferred_element_type=F32)
            else:
                mixed = lax.dot_general(rows, mine_l2[...], (((1,), (1,)), ((), ())), preferred_element_type=F32)
            base = q * 64 + depth * 16
            for p in range(2):
                block = mixed[:, 128 * p : 128 * p + 128].reshape(4, 16, CH)
                even, odd = merge(block[:, :8], block[:, 8:])
                outgoing[pl.ds(base + 8 * p, 4)] = even.astype(BF16)
                outgoing[pl.ds(base + 8 * p + 4, 4)] = odd.astype(BF16)
            for corner in (3, 2, 1, 0):
                for dx in (2, 1, 3, 0):
                    here = None
                    if corner == 0 and dx == 0:
                        here = jnp.logical_and(y_lo == core, side * 4 + depth == z)
                    send(
                        outgoing.at[base + lines[dx] * 4 + corners[corner]], dst,
                        core * 4 + lines[dx], (side * 4 + depth) * 4 + corners[corner],
                        ret_send.at[layer], ret_recv.at[2 * layer + colour_here], here,
                    )

    def multiply(layer):
        back = (back1 if layer == 0 else back2).at[own]
        swap = swap1 if layer == 0 else swap2
        gather(layer)
        exchange = pltpu.make_async_remote_copy(
            src_ref=mine_r, dst_ref=swap, send_sem=swap_send.at[layer], recv_sem=swap_recv.at[layer],
            device_id=(row, sibling), device_id_type=MESH,
        )
        exchange.start()
        quadrant(layer, 0, mine_r, back)
        exchange.wait_recv()
        quadrant(layer, 1, swap, back)
        exchange.wait_send()

    def finish(layer):
        back = back1 if layer == 0 else back2
        halves = []
        for colour in range(2):
            arrived(back.at[pl.ds(64 * colour, 64)], ret_recv.at[2 * layer + colour])
            total = jnp.zeros((8, CH), F32)
            for g in range(4 * colour, 4 * colour + 4):
                part = back[16 * g : 16 * g + 16].astype(F32)
                wide[128 * g : 128 * g + 128, :] = part.reshape(128, CH)
                total = total + jnp.sum(part, axis=0)
            mean = total * (1.0 / 64)
            total = jnp.zeros((8, CH), F32)
            for g in range(4 * colour, 4 * colour + 4):
                part = wide[128 * g : 128 * g + 128, :].reshape(16, 8, CH) - mean[None]
                total = total + jnp.sum(part * part, axis=0)
            halves.append((mean, total))
        (mean0, total0), (mean1, total1) = halves
        apart = 0.5 * (mean0 - mean1)
        means[...] = 0.5 * (mean0 + mean1)
        rstds[...] = lax.rsqrt((total0 + total1) * (1.0 / CH) + apart * apart + 1e-05)

    def updated(layer, s):
        mixed = wide[pl.ds(s, CH, stride=8), :]
        out_normed = (mixed - means[s : s + 1, :]) * rstds[s : s + 1, :] * gains[layer, 2] + gains[layer, 3]
        update = jnp.dot(wot[layer], out_normed.astype(BF16), preferred_element_type=F32)
        return cur[s] + gate[s] * update

    for load in loads:
        load.wait()
    prepare(0)
    make_masks()
    second_hop()
    wide[...] = pair_ref[...].astype(F32).reshape(POS, CH)
    for s in range(8):
        rows = [wide[pl.ds(256 * g + 16 * e + 2 * s + b, 8, stride=32), :] for b, g, e in order]
        normalize(0, s, jnp.concatenate(rows, axis=0).T)
    pl.semaphore_wait(hop_sem, COLS - 1)
    home1 = scatter(0)
    multiply(0)
    prepare_out(0)
    make_gate(0)
    prepare(1)
    prepare_out(1)
    sent(tile, send_sem.at[0], home1)
    finish(0)
    for s in range(8):
        normalize(1, s, updated(0, s).astype(BF16).astype(F32))
    home2 = scatter(1)
    sent(outgoing, ret_send.at[0], home1)
    multiply(1)
    make_gate(1)
    sent(tile, send_sem.at[1], home2)
    finish(1)
    for s in range(8):
        values = updated(1, s).T
        for n, (b, g, e) in enumerate(order):
            stage[pl.ds(256 * g + 16 * e + 2 * s + b, 8, stride=32), :] = values[8 * n : 8 * n + 8]
    out_ref[...] = stage[...].reshape(TR, TC, CH).astype(BF16)
    sent(outgoing, ret_send.at[1], home1)


def shards(pair, residue_mask, in_gain, in_bias, proj_weight, gate_weight, out_gain, out_bias, out_weight):
    arguments = (
        pair, residue_mask.reshape(1, 512), in_gain, in_bias, proj_weight, gate_weight, out_gain, out_bias, out_weight
    )
    dma = pltpu.SemaphoreType.DMA
    return pl.pallas_call(
        kernel,
        out_shape=pltpu.VMEM((TR, TC, CH), BF16),
        in_specs=[pl.BlockSpec(memory_space=pltpu.HBM)] * 9,
        out_specs=pl.BlockSpec(memory_space=pltpu.VMEM),
        scratch_shapes=[pltpu.VMEM(value.shape, value.dtype) for value in arguments] + [
            pltpu.VMEM((POS, CH), F32),
            pltpu.VMEM((8, CH, CH), F32),
            pltpu.VMEM((8, CH, CH), F32),
            pltpu.VMEM((POS, CH), F32),
            pltpu.VMEM((8, CH), F32),
            pltpu.VMEM((8, CH), F32),
            pltpu.VMEM((8, CH), F32),
            pltpu.VMEM((CH, POS), BF16),
            pltpu.VMEM((2, 16, 32, CH), BF16),
            pltpu.VMEM((2, CH, CH), BF16),
            pltpu.VMEM((2, CH, CH), BF16),
            pltpu.VMEM((2, 4, CH, CH), F32),
            pltpu.VMEM((CH, 16, CH), BF16),
            pltpu.VMEM((CH, 16, CH), BF16),
            pltpu.VMEM((CH, 16, CH), BF16),
            pltpu.VMEM((CH, 8, CH), BF16),
            pltpu.VMEM((CH, 8, CH), BF16),
            pltpu.VMEM((256, 512), BF16),
            pltpu.VMEM((256, 512), BF16),
            pltpu.VMEM((256, 512), BF16),
            pltpu.VMEM((512, 256), BF16),
            pltpu.VMEM((256, 512), BF16),
            pltpu.VMEM((512, 256), F32),
            pltpu.VMEM((CH, 8, CH), BF16),
            dma((9,)),
            pltpu.SemaphoreType.REGULAR,
            dma((2,)), dma((16,)), dma((2,)), dma((2,)), dma((2,)), dma((4,)),
        ],
        compiler_params=pltpu.CompilerParams(
            collective_id=0, has_side_effects=True, vmem_limit_bytes=48 * 1024 * 1024
        ),
        cost_estimate=pl.CostEstimate(flops=700_000_000, bytes_accessed=4_000_000, transcendentals=1_000_000),
    )(*[pltpu.with_memory_space_constraint(value, pltpu.HBM) for value in arguments])


def solution(mesh):
    placed = (P("row", "col", None), P(), P(), P(), P(), P(), P(), P(), P())
    return jax.shard_map(
        shards, mesh=mesh, in_specs=placed, out_specs=P("row", "col", None), check_vma=False
    )
```

```python
import jax
import jax.numpy as jnp
from jax import lax
from jax.experimental import pallas as pl
from jax.experimental.pallas import tpu as pltpu
from jax.sharding import PartitionSpec as P

MESH = pl.DeviceIdType.MESH
F32 = jnp.float32
BF16 = jnp.bfloat16
ROWS, COLS = 8, 32
TR, TC = 64, 16
CH = 128
POS = TR * TC


def kernel(
    pair_hbm, mask_hbm, gain_hbm, bias_hbm, wp_hbm, wg_hbm, ogain_hbm, obias_hbm, wo_hbm,
    out_ref,
    pair_ref, mask_in, gain_ref, bias_ref, wp_ref, wg_ref, ogain_ref, obias_ref, wo_ref,
    wide, cur, gate, stage, masks, means, rstds, normed, wpt, wgt, wot, gains,
    tile, recv1, recv2, back1, back2, swap1, swap2, mine_r, mine_l, mine_l2, raw_r, outgoing, relay,
    load_sem, hop_sem, send_sem, in_sem, swap_send, swap_recv, ret_send, ret_recv, relay_sem, pass_send,
):
    row = lax.axis_index("row")
    col = lax.axis_index("col")
    core = lax.rem(col, 2)
    sibling = col + 1 - 2 * core
    x, y_lo = lax.rem(row, 4), row // 4
    z, y_hi = col // 4, lax.rem(col // 2, 2)

    colour_here = lax.rem(x + z, 2)
    own = (colour_here * 8 + z) * 8 + x // 2 * 4 + y_hi * 2 + y_lo
    z_low = lax.rem(z, 4)
    relay_col = lax.rem(col + 24, 32)
    served_z = lax.rem(z + 2, 8)

    loads = [
        pltpu.make_async_copy(src, dst, load_sem.at[n])
        for n, (src, dst) in enumerate([
            (pair_hbm, pair_ref), (mask_hbm, mask_in), (gain_hbm, gain_ref), (bias_hbm, bias_ref), (wp_hbm, wp_ref),
            (wg_hbm, wg_ref), (ogain_hbm, ogain_ref), (obias_hbm, obias_ref), (wo_hbm, wo_ref),
        ])
    ]
    for load in loads:
        load.start()

    barrier = pltpu.get_barrier_semaphore()

    @pl.loop(1, ROWS)
    def _(d):
        pl.semaphore_signal(barrier, inc=1, device_id=(lax.rem(row + d, ROWS), col), device_id_type=MESH)

    @pl.loop(1, COLS)
    def _(d):
        pl.semaphore_signal(barrier, inc=1, device_id=(row, lax.rem(col + d, COLS)), device_id_type=MESH)

    def second_hop():
        pl.semaphore_wait(barrier, ROWS - 1 + COLS - 1)

        @pl.loop(1, COLS)
        def _(d):
            pl.semaphore_signal(hop_sem, inc=1, device_id=(row, lax.rem(col + d, COLS)), device_id_type=MESH)

    order = [(b, g, e) for b in range(2) for g in range(4) for e in range(2)]

    def make_masks():
        lane = lax.broadcasted_iota(jnp.int32, (8, CH), 1)
        mask = mask_in[...].astype(F32)
        number = lax.broadcasted_iota(jnp.int32, (8, 512), 1)
        sub = lax.broadcasted_iota(jnp.int32, (8, 512), 0)
        even_b = jnp.sum(jnp.where(number == TC * col + 2 * sub, mask, 0.0), axis=1, keepdims=True)
        odd_b = jnp.sum(jnp.where(number == TC * col + 2 * sub + 1, mask, 0.0), axis=1, keepdims=True)
        mask_b = jnp.where(lane < 64, even_b, odd_b)
        lane_n = lax.broadcasted_iota(jnp.int32, (512, CH), 1)
        row_n = lax.broadcasted_iota(jnp.int32, (512, CH), 0)
        a_of = ((lane_n // 16) % 4) * 16 + ((lane_n // 8) % 2) + 2 * (lane_n % 8)
        pick = jnp.where(row_n == TR * row + a_of, 1.0, 0.0).astype(BF16)
        mask_a = jnp.dot(jnp.broadcast_to(mask, (8, 512)).astype(BF16), pick, preferred_element_type=F32)
        masks[...] = mask_a * mask_b

    def spread_out(ref, layer, n):
        gains[layer, n] = jnp.broadcast_to(ref[layer : layer + 1, :], (CH, CH)).T

    def prepare(layer):
        turned = wp_ref[layer].astype(F32).T
        for b in range(16):
            rows = [turned[128 * q + 8 * b : 128 * q + 8 * b + 8] for q in range(4)]
            wpt[layer, b] = jnp.concatenate(rows, axis=0).astype(BF16)
        spread_out(gain_ref, layer, 0)
        spread_out(bias_ref, layer, 1)

    def prepare_out(layer):
        wgt[layer] = wg_ref[layer].astype(F32).T.astype(BF16)
        wot[layer] = wo_ref[layer].astype(F32).T.astype(BF16)
        spread_out(ogain_ref, layer, 2)
        spread_out(obias_ref, layer, 3)

    def normalize(layer, s, values):
        center = values - jnp.mean(values, axis=0, keepdims=True)
        spread = jnp.mean(center * center, axis=0, keepdims=True)
        scaled = center * lax.rsqrt(spread + 1e-05) * gains[layer, 0] + gains[layer, 1]
        normed[:, CH * s : CH * s + CH] = scaled.astype(BF16)
        cur[s] = values

    def send(src, dst, to_row, to_col, send_sem, recv_sem, here):
        def local():
            pltpu.make_async_copy(src, dst, recv_sem).start()

        def remote():
            pltpu.make_async_remote_copy(
                src_ref=src, dst_ref=dst, send_sem=send_sem, recv_sem=recv_sem,
                device_id=(to_row, to_col), device_id_type=MESH,
            ).start()

        if here is None:
            remote()
        else:
            pl.when(here)(local)
            pl.when(jnp.logical_not(here))(remote)

    def sent(buffer, sem, home):
        count = buffer.shape[0]

        @pl.when(home)
        def _():
            part = buffer.at[pl.ds(0, count - 1)]
            pltpu.make_async_copy(part, part, sem).wait()

        @pl.when(jnp.logical_not(home))
        def _():
            pltpu.make_async_copy(buffer, buffer, sem).wait()

    def arrived(buffer, sem):
        pltpu.make_async_copy(buffer, buffer, sem).wait()

    def scatter(layer):
        to_core = y_lo if layer == 0 else col // 16
        corner = y_hi * 2 + core
        slot = z * 16 + x * 4 + corner if layer == 0 else z_low * 32 + row * 4 + corner
        dst = (recv1 if layer == 0 else recv2).at[slot]
        lows = [y_lo, 1 - y_lo]
        highs = [y_hi, 1 - y_hi]
        halves = [x // 2, 1 - x // 2]

        @pl.loop(0, 8)
        def _(g):
            colour = jnp.where(g == 0, 1, g // 5)
            step = jnp.where(g == 0, 1, jnp.where(g < 5, g - 1, jnp.where(g == 5, 0, g - 4)))
            ahead = jnp.where(step == 0, 3, jnp.where(step == 1, 4, 4 - step))
            depths = [lax.rem(z + ahead, 8), lax.rem(z + jnp.where(step == 1, 0, 8 - ahead), 8)]
            blocks = [colour * 8 + depth for depth in depths]
            weights = jnp.concatenate([wpt[layer, block] for block in blocks], axis=0)
            proj = jnp.dot(weights, normed[...], preferred_element_type=F32)
            left = jnp.concatenate([jax.nn.sigmoid(proj[n : n + 8]) * proj[n + 8 : n + 16] for n in (0, 32)], axis=0)
            right = jnp.concatenate([jax.nn.sigmoid(proj[n : n + 8]) * proj[n + 8 : n + 16] for n in (16, 48)], axis=0)
            for s in range(8):
                keep = masks[s : s + 1, :]
                stage[pl.ds(s, 16, stride=16), :] = left[:, CH * s : CH * s + CH] * keep
                stage[pl.ds(s + 8, 16, stride=16), :] = right[:, CH * s : CH * s + CH] * keep
            for n, block in enumerate(blocks):
                tile[pl.ds(block * 8, 8)] = stage[128 * n : 128 * n + 128, :].reshape(8, 16, CH).astype(BF16)
            odd = [lax.rem(colour + depth, 2) for depth in depths]
            for dx in (1, 0):
                for dh in (1, 0):
                    for dl in (1, 0):
                        for n in range(2):
                            here = None
                            if n == 1 and dx + dh + dl == 0:
                                here = jnp.logical_and(jnp.logical_and(step == 1, colour == colour_here), to_core == core)
                            src = tile.at[blocks[n] * 8 + halves[dx] * 4 + highs[dh] * 2 + lows[dl]]

                            def straight():
                                send(
                                    src, dst,
                                    lows[dl] * 4 + halves[dx] * 2 + odd[n], depths[n] * 4 + highs[dh] * 2 + to_core,
                                    send_sem.at[layer], in_sem.at[8 * layer + z], here,
                                )

                            def around():
                                send(
                                    src, relay.at[layer, dx * 4 + dh * 2 + dl], row, relay_col,
                                    send_sem.at[layer], relay_sem.at[layer], None,
                                )

                            if n == 0:
                                pl.when(g == 0)(around)
                                pl.when(g > 0)(straight)
                            else:
                                straight()

        held = relay.at[layer]
        arrived(held, relay_sem.at[layer])
        served_slot = served_z * 16 + x * 4 + corner if layer == 0 else lax.rem(served_z, 4) * 32 + row * 4 + corner
        served_core = y_lo if layer == 0 else served_z // 4
        beyond = lax.rem(z + 6, 8)
        for dx in (1, 0):
            for dh in (1, 0):
                for dl in (1, 0):
                    send(
                        held.at[dx * 4 + dh * 2 + dl], (recv1 if layer == 0 else recv2).at[served_slot],
                        lows[dl] * 4 + halves[dx] * 2 + lax.rem(1 + z, 2), beyond * 4 + highs[dh] * 2 + served_core,
                        pass_send.at[layer], in_sem.at[8 * layer + served_z], None,
                    )

        return to_core == core

    def make_gate(layer):
        for s in range(8):
            part = jnp.dot(wgt[layer], normed[:, CH * s : CH * s + CH], preferred_element_type=F32)
            gate[s] = jax.nn.sigmoid(part)

    def merge(first, second):
        low = lax.broadcasted_iota(jnp.int32, first.shape, 2) < 64
        even = jnp.where(low, first, pltpu.roll(second, 64, 2))
        odd = jnp.where(low, pltpu.roll(first, 64, 2), second)
        return even, odd

    def far_first(step, same):
        falling = (z_low < 2) == same
        return jnp.where(falling, 3 - step, step)

    def gather(layer):
        for step in range(8 if layer == 0 else 4):
            if layer == 0:
                recv, width, pairs = recv1, 16, 2
                place = lax.rem(z + (5, 3, 0, 6, 2, 7, 1, 4)[step], 8)
                sem = in_sem.at[place]
            else:
                recv, width, pairs = recv2, 32, 4
                place = far_first(step, z // 4 == core)
                sem = in_sem.at[8 + core * 4 + place]
            arrived(recv.at[pl.ds(place * width, width)], sem)
            rows = pl.ds(64 * step if layer == 0 else pl.multiple_of(place * 64, 64), 64)
            for p in range(pairs):
                first = recv[pl.ds(place * width + 8 * p, 4)].astype(F32)
                second = recv[pl.ds(place * width + 8 * p + 4, 4)].astype(F32)
                even, odd = merge(first, second)
                left = jnp.concatenate([even[:, :8], odd[:, :8]], axis=1).reshape(64, CH)
                right = jnp.concatenate([even[:, 8:], odd[:, 8:]], axis=1).reshape(64, CH)
                lanes = slice(128 * p, 128 * p + 128)
                if layer == 0:
                    mine_l[rows, lanes] = left.astype(BF16)
                    raw_r[rows, lanes] = right
                else:
                    mine_l2[rows, lanes] = left.astype(BF16)
                    mine_r[rows, lanes] = right.astype(BF16)
                if layer == 0 and step % 2 == 1:
                    block = slice(64 * step - 64, 64 * step + 64)
                    mine_r[lanes, block] = raw_r[block, lanes].T.astype(BF16)

    def quadrant(layer, q, right, dst):
        side = core if q == 0 else 1 - core
        lines = [lax.rem(x + n, 4) for n in range(4)]
        corners = [(y_hi if dy == 0 else 1 - y_hi) * 2 + (core if dc == 0 else 1 - core) for dy in range(2) for dc in range(2)]

        @pl.loop(0, 4)
        def _(step):
            depth = far_first(step, z // 4 == side)
            rows = right[pl.ds(pl.multiple_of(depth * 64, 64), 64), :]
            if layer == 0:
                mixed = jnp.dot(rows, mine_l[...], preferred_element_type=F32)
            else:
                mixed = lax.dot_general(rows, mine_l2[...], (((1,), (1,)), ((), ())), preferred_element_type=F32)
            base = q * 64 + depth * 16
            for p in range(2):
                block = mixed[:, 128 * p : 128 * p + 128].reshape(4, 16, CH)
                even, odd = merge(block[:, :8], block[:, 8:])
                outgoing[pl.ds(base + 8 * p, 4)] = even.astype(BF16)
                outgoing[pl.ds(base + 8 * p + 4, 4)] = odd.astype(BF16)
            for corner in (3, 2, 1, 0):
                for dx in (2, 1, 3, 0):
                    here = None
                    if corner == 0 and dx == 0:
                        here = jnp.logical_and(y_lo == core, side * 4 + depth == z)
                    send(
                        outgoing.at[base + lines[dx] * 4 + corners[corner]], dst,
                        core * 4 + lines[dx], (side * 4 + depth) * 4 + corners[corner],
                        ret_send.at[layer], ret_recv.at[2 * layer + colour_here], here,
                    )

    def multiply(layer):
        back = (back1 if layer == 0 else back2).at[own]
        swap = swap1 if layer == 0 else swap2
        gather(layer)
        exchange = pltpu.make_async_remote_copy(
            src_ref=mine_r, dst_ref=swap, send_sem=swap_send.at[layer], recv_sem=swap_recv.at[layer],
            device_id=(row, sibling), device_id_type=MESH,
        )
        exchange.start()
        quadrant(layer, 0, mine_r, back)
        exchange.wait_recv()
        quadrant(layer, 1, swap, back)
        exchange.wait_send()

    def finish(layer):
        back = back1 if layer == 0 else back2
        halves = []
        for colour in range(2):
            arrived(back.at[pl.ds(64 * colour, 64)], ret_recv.at[2 * layer + colour])
            total = jnp.zeros((8, CH), F32)
            for g in range(4 * colour, 4 * colour + 4):
                part = back[16 * g : 16 * g + 16].astype(F32)
                wide[128 * g : 128 * g + 128, :] = part.reshape(128, CH)
                total = total + jnp.sum(part, axis=0)
            mean = total * (1.0 / 64)
            total = jnp.zeros((8, CH), F32)
            for g in range(4 * colour, 4 * colour + 4):
                part = wide[128 * g : 128 * g + 128, :].reshape(16, 8, CH) - mean[None]
                total = total + jnp.sum(part * part, axis=0)
            halves.append((mean, total))
        (mean0, total0), (mean1, total1) = halves
        apart = 0.5 * (mean0 - mean1)
        means[...] = 0.5 * (mean0 + mean1)
        rstds[...] = lax.rsqrt((total0 + total1) * (1.0 / CH) + apart * apart + 1e-05)

    def updated(layer, s):
        mixed = wide[pl.ds(s, CH, stride=8), :]
        out_normed = (mixed - means[s : s + 1, :]) * rstds[s : s + 1, :] * gains[layer, 2] + gains[layer, 3]
        update = jnp.dot(wot[layer], out_normed.astype(BF16), preferred_element_type=F32)
        return cur[s] + gate[s] * update

    for load in loads:
        load.wait()
    prepare(0)
    make_masks()
    second_hop()
    wide[...] = pair_ref[...].astype(F32).reshape(POS, CH)
    for s in range(8):
        rows = [wide[pl.ds(256 * g + 16 * e + 2 * s + b, 8, stride=32), :] for b, g, e in order]
        normalize(0, s, jnp.concatenate(rows, axis=0).T)
    pl.semaphore_wait(hop_sem, COLS - 1)
    home1 = scatter(0)
    multiply(0)
    prepare_out(0)
    make_gate(0)
    prepare(1)
    prepare_out(1)
    sent(tile, send_sem.at[0], home1)
    finish(0)
    for s in range(8):
        normalize(1, s, updated(0, s).astype(BF16).astype(F32))
    home2 = scatter(1)
    sent(outgoing, ret_send.at[0], home1)
    multiply(1)
    make_gate(1)
    sent(tile, send_sem.at[1], home2)
    finish(1)
    for s in range(8):
        values = updated(1, s).T
        for n, (b, g, e) in enumerate(order):
            stage[pl.ds(256 * g + 16 * e + 2 * s + b, 8, stride=32), :] = values[8 * n : 8 * n + 8]
    out_ref[...] = stage[...].reshape(TR, TC, CH).astype(BF16)
    sent(outgoing, ret_send.at[1], home1)
    for layer in range(2):
        arrived(relay.at[layer], pass_send.at[layer])


def shards(pair, residue_mask, in_gain, in_bias, proj_weight, gate_weight, out_gain, out_bias, out_weight):
    arguments = (
        pair, residue_mask.reshape(1, 512), in_gain, in_bias, proj_weight, gate_weight, out_gain, out_bias, out_weight
    )
    dma = pltpu.SemaphoreType.DMA
    return pl.pallas_call(
        kernel,
        out_shape=pltpu.VMEM((TR, TC, CH), BF16),
        in_specs=[pl.BlockSpec(memory_space=pltpu.HBM)] * 9,
        out_specs=pl.BlockSpec(memory_space=pltpu.VMEM),
        scratch_shapes=[pltpu.VMEM(value.shape, value.dtype) for value in arguments] + [
            pltpu.VMEM((POS, CH), F32),
            pltpu.VMEM((8, CH, CH), F32),
            pltpu.VMEM((8, CH, CH), F32),
            pltpu.VMEM((POS, CH), F32),
            pltpu.VMEM((8, CH), F32),
            pltpu.VMEM((8, CH), F32),
            pltpu.VMEM((8, CH), F32),
            pltpu.VMEM((CH, POS), BF16),
            pltpu.VMEM((2, 16, 32, CH), BF16),
            pltpu.VMEM((2, CH, CH), BF16),
            pltpu.VMEM((2, CH, CH), BF16),
            pltpu.VMEM((2, 4, CH, CH), F32),
            pltpu.VMEM((CH, 16, CH), BF16),
            pltpu.VMEM((CH, 16, CH), BF16),
            pltpu.VMEM((CH, 16, CH), BF16),
            pltpu.VMEM((CH, 8, CH), BF16),
            pltpu.VMEM((CH, 8, CH), BF16),
            pltpu.VMEM((256, 512), BF16),
            pltpu.VMEM((256, 512), BF16),
            pltpu.VMEM((256, 512), BF16),
            pltpu.VMEM((512, 256), BF16),
            pltpu.VMEM((256, 512), BF16),
            pltpu.VMEM((512, 256), F32),
            pltpu.VMEM((CH, 8, CH), BF16),
            pltpu.VMEM((2, 8, 16, CH), BF16),
            dma((9,)),
            pltpu.SemaphoreType.REGULAR,
            dma((2,)), dma((16,)), dma((2,)), dma((2,)), dma((2,)), dma((4,)), dma((2,)), dma((2,)),
        ],
        compiler_params=pltpu.CompilerParams(
            collective_id=0, has_side_effects=True, vmem_limit_bytes=48 * 1024 * 1024
        ),
        cost_estimate=pl.CostEstimate(flops=700_000_000, bytes_accessed=4_000_000, transcendentals=1_000_000),
    )(*[pltpu.with_memory_space_constraint(value, pltpu.HBM) for value in arguments])


def solution(mesh):
    placed = (P("row", "col", None), P(), P(), P(), P(), P(), P(), P(), P())
    return jax.shard_map(
        shards, mesh=mesh, in_specs=placed, out_specs=P("row", "col", None), check_vma=False
    )
```

```python
import jax
import jax.numpy as jnp
from jax import lax
from jax.experimental import pallas as pl
from jax.experimental.pallas import tpu as pltpu
from jax.sharding import PartitionSpec as P

MESH = pl.DeviceIdType.MESH
F32 = jnp.float32
BF16 = jnp.bfloat16
ROWS, COLS = 8, 32
TR, TC = 64, 16
CH = 128
POS = TR * TC


def kernel(
    pair_hbm, mask_hbm, gain_hbm, bias_hbm, wp_hbm, wg_hbm, ogain_hbm, obias_hbm, wo_hbm,
    out_ref,
    pair_ref, mask_in, gain_ref, bias_ref, wp_ref, wg_ref, ogain_ref, obias_ref, wo_ref,
    wide, cur, gate, stage, masks, means, rstds, normed, wpt, wgt, wot, gains,
    tile, recv1, recv2, back1, back2, swap1, swap2, mine_r, mine_l, mine_l2, raw_r, outgoing,
    load_sem, hop_sem, send_sem, in_sem, swap_send, swap_recv, ret_send, ret_recv,
):
    row = lax.axis_index("row")
    col = lax.axis_index("col")
    core = lax.rem(col, 2)
    sibling = col + 1 - 2 * core
    x, y_lo = lax.rem(row, 4), row // 4
    z, y_hi = col // 4, lax.rem(col // 2, 2)

    colour_here = lax.rem(x + z, 2)
    own = (colour_here * 8 + z) * 8 + x // 2 * 4 + y_hi * 2 + y_lo
    z_low = lax.rem(z, 4)

    loads = [
        pltpu.make_async_copy(src, dst, load_sem.at[n])
        for n, (src, dst) in enumerate([
            (pair_hbm, pair_ref), (mask_hbm, mask_in), (gain_hbm, gain_ref), (bias_hbm, bias_ref), (wp_hbm, wp_ref),
            (wg_hbm, wg_ref), (ogain_hbm, ogain_ref), (obias_hbm, obias_ref), (wo_hbm, wo_ref),
        ])
    ]
    for load in loads:
        load.start()

    barrier = pltpu.get_barrier_semaphore()

    @pl.loop(1, ROWS)
    def _(d):
        pl.semaphore_signal(barrier, inc=1, device_id=(lax.rem(row + d, ROWS), col), device_id_type=MESH)

    @pl.loop(1, COLS)
    def _(d):
        pl.semaphore_signal(barrier, inc=1, device_id=(row, lax.rem(col + d, COLS)), device_id_type=MESH)

    def second_hop():
        pl.semaphore_wait(barrier, ROWS - 1 + COLS - 1)

        @pl.loop(1, COLS)
        def _(d):
            pl.semaphore_signal(hop_sem, inc=1, device_id=(row, lax.rem(col + d, COLS)), device_id_type=MESH)

    order = [(b, g, e) for b in range(2) for g in range(4) for e in range(2)]

    def make_masks():
        lane = lax.broadcasted_iota(jnp.int32, (8, CH), 1)
        mask = mask_in[...].astype(F32)
        number = lax.broadcasted_iota(jnp.int32, (8, 512), 1)
        sub = lax.broadcasted_iota(jnp.int32, (8, 512), 0)
        even_b = jnp.sum(jnp.where(number == TC * col + 2 * sub, mask, 0.0), axis=1, keepdims=True)
        odd_b = jnp.sum(jnp.where(number == TC * col + 2 * sub + 1, mask, 0.0), axis=1, keepdims=True)
        mask_b = jnp.where(lane < 64, even_b, odd_b)
        place = lax.broadcasted_iota(jnp.int32, (1, CH), 1)
        place = place - jnp.where(place >= 64, 64, 0)
        a_of = 16 * (place // 16) + (place // 8) % 2 + 2 * (place % 8)
        pick = jnp.where(lax.broadcasted_iota(jnp.int32, (512, CH), 0) == TR * row + a_of, 1.0, 0.0).astype(BF16)
        mask_a = jnp.dot(jnp.broadcast_to(mask, (8, 512)).astype(BF16), pick, preferred_element_type=F32)
        masks[...] = mask_a * mask_b

    def spread_out(ref, layer, n):
        gains[layer, n] = jnp.broadcast_to(ref[layer : layer + 1, :], (CH, CH)).T

    def prepare(layer):
        turned = wp_ref[layer].astype(F32).T
        for b in range(16):
            rows = [turned[128 * q + 8 * b : 128 * q + 8 * b + 8] for q in range(4)]
            wpt[layer, b] = jnp.concatenate(rows, axis=0).astype(BF16)
        spread_out(gain_ref, layer, 0)
        spread_out(bias_ref, layer, 1)

    def prepare_out(layer):
        wgt[layer] = wg_ref[layer].astype(F32).T.astype(BF16)
        wot[layer] = wo_ref[layer].astype(F32).T.astype(BF16)
        spread_out(ogain_ref, layer, 2)
        spread_out(obias_ref, layer, 3)

    def normalize(layer, s, values):
        center = values - jnp.mean(values, axis=0, keepdims=True)
        spread = jnp.mean(center * center, axis=0, keepdims=True)
        scaled = center * lax.rsqrt(spread + 1e-05) * gains[layer, 0] + gains[layer, 1]
        normed[:, CH * s : CH * s + CH] = scaled.astype(BF16)
        cur[s] = values

    def send(src, dst, to_row, to_col, send_sem, recv_sem, here):
        def local():
            pltpu.make_async_copy(src, dst, recv_sem).start()

        def remote():
            pltpu.make_async_remote_copy(
                src_ref=src, dst_ref=dst, send_sem=send_sem, recv_sem=recv_sem,
                device_id=(to_row, to_col), device_id_type=MESH,
            ).start()

        if here is None:
            remote()
        else:
            pl.when(here)(local)
            pl.when(jnp.logical_not(here))(remote)

    def sent(buffer, sem, home):
        count = buffer.shape[0]

        @pl.when(home)
        def _():
            part = buffer.at[pl.ds(0, count - 1)]
            pltpu.make_async_copy(part, part, sem).wait()

        @pl.when(jnp.logical_not(home))
        def _():
            pltpu.make_async_copy(buffer, buffer, sem).wait()

    def arrived(buffer, sem):
        pltpu.make_async_copy(buffer, buffer, sem).wait()

    def scatter(layer):
        to_core = y_lo if layer == 0 else col // 16
        corner = y_hi * 2 + core
        slot = z * 16 + x * 4 + corner if layer == 0 else z_low * 32 + row * 4 + corner
        dst = (recv1 if layer == 0 else recv2).at[slot]
        lows = [y_lo, 1 - y_lo]
        highs = [y_hi, 1 - y_hi]
        halves = [x // 2, 1 - x // 2]

        @pl.loop(0, 8)
        def _(g):
            colour, step = g // 4, lax.rem(g, 4)
            depths = [lax.rem(z + 4 + step, 8), lax.rem(z + 3 - step, 8)]
            blocks = [colour * 8 + depth for depth in depths]
            weights = jnp.concatenate([wpt[layer, block] for block in blocks], axis=0)
            proj = jnp.dot(weights, normed[...], preferred_element_type=F32)
            left = jnp.concatenate([jax.nn.sigmoid(proj[n : n + 8]) * proj[n + 8 : n + 16] for n in (0, 32)], axis=0)
            right = jnp.concatenate([jax.nn.sigmoid(proj[n : n + 8]) * proj[n + 8 : n + 16] for n in (16, 48)], axis=0)
            for s in range(8):
                keep = masks[s : s + 1, :]
                stage[pl.ds(s, 16, stride=16), :] = left[:, CH * s : CH * s + CH] * keep
                stage[pl.ds(s + 8, 16, stride=16), :] = right[:, CH * s : CH * s + CH] * keep
            for n, block in enumerate(blocks):
                tile[pl.ds(block * 8, 8)] = stage[128 * n : 128 * n + 128, :].reshape(8, 16, CH).astype(BF16)
            odd = [lax.rem(colour + depth, 2) for depth in depths]
            for dx in (1, 0):
                for dh in (1, 0):
                    for dl in (1, 0):
                        for n in range(2):
                            here = None
                            if n == 1 and dx + dh + dl == 0:
                                here = jnp.logical_and(g == 4 * colour_here + 3, to_core == core)
                            send(
                                tile.at[blocks[n] * 8 + halves[dx] * 4 + highs[dh] * 2 + lows[dl]], dst,
                                lows[dl] * 4 + halves[dx] * 2 + odd[n], depths[n] * 4 + highs[dh] * 2 + to_core,
                                send_sem.at[layer], in_sem.at[8 * layer + z], here,
                            )

        return to_core == core

    def make_gate(layer):
        for s in range(8):
            part = jnp.dot(wgt[layer], normed[:, CH * s : CH * s + CH], preferred_element_type=F32)
            gate[s] = jax.nn.sigmoid(part)

    def merge(first, second):
        low = lax.broadcasted_iota(jnp.int32, first.shape, 2) < 64
        even = jnp.where(low, first, pltpu.roll(second, 64, 2))
        odd = jnp.where(low, pltpu.roll(first, 64, 2), second)
        return even, odd

    def far_first(step, same):
        falling = (z_low < 2) == same
        return jnp.where(falling, 3 - step, step)

    def gather(layer):
        for step in range(8 if layer == 0 else 4):
            if layer == 0:
                recv, width, pairs = recv1, 16, 2
                place = lax.rem(z + (4, 5, 3, 6, 2, 7, 1, 0)[step], 8)
                sem = in_sem.at[place]
            else:
                recv, width, pairs = recv2, 32, 4
                place = far_first(step, z // 4 == core)
                sem = in_sem.at[8 + core * 4 + place]
            arrived(recv.at[pl.ds(place * width, width)], sem)
            rows = pl.ds(64 * step if layer == 0 else pl.multiple_of(place * 64, 64), 64)
            for p in range(pairs):
                first = recv[pl.ds(place * width + 8 * p, 4)].astype(F32)
                second = recv[pl.ds(place * width + 8 * p + 4, 4)].astype(F32)
                even, odd = merge(first, second)
                left = jnp.concatenate([even[:, :8], odd[:, :8]], axis=1).reshape(64, CH)
                right = jnp.concatenate([even[:, 8:], odd[:, 8:]], axis=1).reshape(64, CH)
                lanes = slice(128 * p, 128 * p + 128)
                if layer == 0:
                    mine_l[rows, lanes] = left.astype(BF16)
                    raw_r[rows, lanes] = right
                else:
                    mine_l2[rows, lanes] = left.astype(BF16)
                    mine_r[rows, lanes] = right.astype(BF16)
                if layer == 0 and step % 2 == 1:
                    block = slice(64 * step - 64, 64 * step + 64)
                    mine_r[lanes, block] = raw_r[block, lanes].T.astype(BF16)

    def quadrant(layer, q, right, dst):
        side = core if q == 0 else 1 - core
        lines = [lax.rem(x + n, 4) for n in range(4)]
        corners = [(y_hi if dy == 0 else 1 - y_hi) * 2 + (core if dc == 0 else 1 - core) for dy in range(2) for dc in range(2)]

        @pl.loop(0, 4)
        def _(step):
            depth = far_first(step, z // 4 == side)
            rows = right[pl.ds(pl.multiple_of(depth * 64, 64), 64), :]
            if layer == 0:
                mixed = jnp.dot(rows, mine_l[...], preferred_element_type=F32)
            else:
                mixed = lax.dot_general(rows, mine_l2[...], (((1,), (1,)), ((), ())), preferred_element_type=F32)
            base = q * 64 + depth * 16
            for p in range(2):
                block = mixed[:, 128 * p : 128 * p + 128].reshape(4, 16, CH)
                even, odd = merge(block[:, :8], block[:, 8:])
                outgoing[pl.ds(base + 8 * p, 4)] = even.astype(BF16)
                outgoing[pl.ds(base + 8 * p + 4, 4)] = odd.astype(BF16)
            for corner in (3, 2, 1, 0):
                for dx in (2, 1, 3, 0):
                    here = None
                    if corner == 0 and dx == 0:
                        here = jnp.logical_and(y_lo == core, side * 4 + depth == z)
                    send(
                        outgoing.at[base + lines[dx] * 4 + corners[corner]], dst,
                        core * 4 + lines[dx], (side * 4 + depth) * 4 + corners[corner],
                        ret_send.at[layer], ret_recv.at[2 * layer + colour_here], here,
                    )

    def multiply(layer):
        back = (back1 if layer == 0 else back2).at[own]
        swap = swap1 if layer == 0 else swap2
        gather(layer)
        exchange = pltpu.make_async_remote_copy(
            src_ref=mine_r, dst_ref=swap, send_sem=swap_send.at[layer], recv_sem=swap_recv.at[layer],
            device_id=(row, sibling), device_id_type=MESH,
        )
        exchange.start()
        quadrant(layer, 0, mine_r, back)
        exchange.wait_recv()
        quadrant(layer, 1, swap, back)
        exchange.wait_send()

    def finish(layer):
        back = back1 if layer == 0 else back2
        halves = []
        for colour in range(2):
            arrived(back.at[pl.ds(64 * colour, 64)], ret_recv.at[2 * layer + colour])
            total = jnp.zeros((8, CH), F32)
            for g in range(4 * colour, 4 * colour + 4):
                part = back[16 * g : 16 * g + 16].astype(F32)
                wide[128 * g : 128 * g + 128, :] = part.reshape(128, CH)
                total = total + jnp.sum(part, axis=0)
            mean = total * (1.0 / 64)
            total = jnp.zeros((8, CH), F32)
            for g in range(4 * colour, 4 * colour + 4):
                part = wide[128 * g : 128 * g + 128, :].reshape(16, 8, CH) - mean[None]
                total = total + jnp.sum(part * part, axis=0)
            halves.append((mean, total))
        (mean0, total0), (mean1, total1) = halves
        apart = 0.5 * (mean0 - mean1)
        means[...] = 0.5 * (mean0 + mean1)
        rstds[...] = lax.rsqrt((total0 + total1) * (1.0 / CH) + apart * apart + 1e-05)

    def updated(layer, s):
        mixed = wide[pl.ds(s, CH, stride=8), :]
        out_normed = (mixed - means[s : s + 1, :]) * rstds[s : s + 1, :] * gains[layer, 2] + gains[layer, 3]
        update = jnp.dot(wot[layer], out_normed.astype(BF16), preferred_element_type=F32)
        return cur[s] + gate[s] * update

    loads[1].wait()
    make_masks()
    for n in (2, 3, 4):
        loads[n].wait()
    prepare(0)
    second_hop()
    loads[0].wait()
    wide[...] = pair_ref[...].astype(F32).reshape(POS, CH)
    for s in range(8):
        rows = [wide[pl.ds(256 * g + 16 * e + 2 * s + b, 8, stride=32), :] for b, g, e in order]
        normalize(0, s, jnp.concatenate(rows, axis=0).T)
    pl.semaphore_wait(hop_sem, COLS - 1)
    home1 = scatter(0)
    multiply(0)
    for n in (5, 6, 7, 8):
        loads[n].wait()
    prepare_out(0)
    make_gate(0)
    prepare(1)
    prepare_out(1)
    sent(tile, send_sem.at[0], home1)
    finish(0)
    for s in range(8):
        normalize(1, s, updated(0, s).astype(BF16).astype(F32))
    home2 = scatter(1)
    sent(outgoing, ret_send.at[0], home1)
    multiply(1)
    make_gate(1)
    sent(tile, send_sem.at[1], home2)
    finish(1)
    for s in range(8):
        values = updated(1, s).T
        for n, (b, g, e) in enumerate(order):
            stage[pl.ds(256 * g + 16 * e + 2 * s + b, 8, stride=32), :] = values[8 * n : 8 * n + 8]
    out_ref[...] = stage[...].reshape(TR, TC, CH).astype(BF16)
    sent(outgoing, ret_send.at[1], home1)


def shards(pair, residue_mask, in_gain, in_bias, proj_weight, gate_weight, out_gain, out_bias, out_weight):
    arguments = (
        pair, residue_mask.reshape(1, 512), in_gain, in_bias, proj_weight, gate_weight, out_gain, out_bias, out_weight
    )
    dma = pltpu.SemaphoreType.DMA
    return pl.pallas_call(
        kernel,
        out_shape=pltpu.VMEM((TR, TC, CH), BF16),
        in_specs=[pl.BlockSpec(memory_space=pltpu.HBM)] * 9,
        out_specs=pl.BlockSpec(memory_space=pltpu.VMEM),
        scratch_shapes=[pltpu.VMEM(value.shape, value.dtype) for value in arguments] + [
            pltpu.VMEM((POS, CH), F32),
            pltpu.VMEM((8, CH, CH), F32),
            pltpu.VMEM((8, CH, CH), F32),
            pltpu.VMEM((POS, CH), F32),
            pltpu.VMEM((8, CH), F32),
            pltpu.VMEM((8, CH), F32),
            pltpu.VMEM((8, CH), F32),
            pltpu.VMEM((CH, POS), BF16),
            pltpu.VMEM((2, 16, 32, CH), BF16),
            pltpu.VMEM((2, CH, CH), BF16),
            pltpu.VMEM((2, CH, CH), BF16),
            pltpu.VMEM((2, 4, CH, CH), F32),
            pltpu.VMEM((CH, 16, CH), BF16),
            pltpu.VMEM((CH, 16, CH), BF16),
            pltpu.VMEM((CH, 16, CH), BF16),
            pltpu.VMEM((CH, 8, CH), BF16),
            pltpu.VMEM((CH, 8, CH), BF16),
            pltpu.VMEM((256, 512), BF16),
            pltpu.VMEM((256, 512), BF16),
            pltpu.VMEM((256, 512), BF16),
            pltpu.VMEM((512, 256), BF16),
            pltpu.VMEM((256, 512), BF16),
            pltpu.VMEM((512, 256), F32),
            pltpu.VMEM((CH, 8, CH), BF16),
            dma((9,)),
            pltpu.SemaphoreType.REGULAR,
            dma((2,)), dma((16,)), dma((2,)), dma((2,)), dma((2,)), dma((4,)),
        ],
        compiler_params=pltpu.CompilerParams(
            collective_id=0, has_side_effects=True, vmem_limit_bytes=48 * 1024 * 1024
        ),
        cost_estimate=pl.CostEstimate(flops=700_000_000, bytes_accessed=4_000_000, transcendentals=1_000_000),
    )(*[pltpu.with_memory_space_constraint(value, pltpu.HBM) for value in arguments])


def solution(mesh):
    placed = (P("row", "col", None), P(), P(), P(), P(), P(), P(), P(), P())
    return jax.shard_map(
        shards, mesh=mesh, in_specs=placed, out_specs=P("row", "col", None), check_vma=False
    )
```

```python
import jax
import jax.numpy as jnp
from jax import lax
from jax.experimental import pallas as pl
from jax.experimental.pallas import tpu as pltpu
from jax.sharding import PartitionSpec as P

MESH = pl.DeviceIdType.MESH
F32 = jnp.float32
BF16 = jnp.bfloat16
ROWS, COLS = 8, 32
TR, TC = 64, 16
CH = 128
POS = TR * TC


def kernel(
    pair_hbm, mask_hbm, gain_hbm, bias_hbm, wp_hbm, wg_hbm, ogain_hbm, obias_hbm, wo_hbm,
    out_ref,
    pair_ref, mask_in, gain_ref, bias_ref, wp_ref, wg_ref, ogain_ref, obias_ref, wo_ref,
    wide, cur, gate, stage, masks, means, rstds, normed, wpt, wgt, wot, gains,
    tile, recv1, recv2, back1, back2, swap1, swap2, mine_r, mine_l, mine_l2, raw_r, outgoing,
    load_sem, hop_sem, send_sem, in_sem, swap_send, swap_recv, ret_send, ret_recv,
):
    row = lax.axis_index("row")
    col = lax.axis_index("col")
    core = lax.rem(col, 2)
    sibling = col + 1 - 2 * core
    x, y_lo = lax.rem(row, 4), row // 4
    z, y_hi = col // 4, lax.rem(col // 2, 2)

    own = (y_lo * 8 + z) * 8 + x * 2 + y_hi
    z_low = lax.rem(z, 4)

    loads = [
        pltpu.make_async_copy(src, dst, load_sem.at[n])
        for n, (src, dst) in enumerate([
            (pair_hbm, pair_ref), (mask_hbm, mask_in), (gain_hbm, gain_ref), (bias_hbm, bias_ref), (wp_hbm, wp_ref),
            (wg_hbm, wg_ref), (ogain_hbm, ogain_ref), (obias_hbm, obias_ref), (wo_hbm, wo_ref),
        ])
    ]
    for load in loads:
        load.start()

    barrier = pltpu.get_barrier_semaphore()

    @pl.loop(1, ROWS)
    def _(d):
        pl.semaphore_signal(barrier, inc=1, device_id=(lax.rem(row + d, ROWS), col), device_id_type=MESH)

    @pl.loop(1, COLS)
    def _(d):
        pl.semaphore_signal(barrier, inc=1, device_id=(row, lax.rem(col + d, COLS)), device_id_type=MESH)

    def second_hop():
        pl.semaphore_wait(barrier, ROWS - 1 + COLS - 1)

        @pl.loop(1, COLS)
        def _(d):
            pl.semaphore_signal(hop_sem, inc=1, device_id=(row, lax.rem(col + d, COLS)), device_id_type=MESH)

    order = [(b, g, e) for b in range(2) for g in range(4) for e in range(2)]

    def make_masks():
        lane = lax.broadcasted_iota(jnp.int32, (8, CH), 1)
        mask = mask_in[...].astype(F32)
        number = lax.broadcasted_iota(jnp.int32, (8, 512), 1)
        sub = lax.broadcasted_iota(jnp.int32, (8, 512), 0)
        even_b = jnp.sum(jnp.where(number == TC * col + 2 * sub, mask, 0.0), axis=1, keepdims=True)
        odd_b = jnp.sum(jnp.where(number == TC * col + 2 * sub + 1, mask, 0.0), axis=1, keepdims=True)
        mask_b = jnp.where(lane < 64, even_b, odd_b)
        place = lax.broadcasted_iota(jnp.int32, (1, CH), 1)
        place = place - jnp.where(place >= 64, 64, 0)
        a_of = 16 * (place // 16) + (place // 8) % 2 + 2 * (place % 8)
        pick = jnp.where(lax.broadcasted_iota(jnp.int32, (512, CH), 0) == TR * row + a_of, 1.0, 0.0).astype(BF16)
        mask_a = jnp.dot(jnp.broadcast_to(mask, (8, 512)).astype(BF16), pick, preferred_element_type=F32)
        masks[...] = mask_a * mask_b

    def spread_out(ref, layer, n):
        gains[layer, n] = jnp.broadcast_to(ref[layer : layer + 1, :], (CH, CH)).T

    def prepare(layer):
        turned = wp_ref[layer].astype(F32).T
        for b in range(16):
            rows = [turned[128 * q + 8 * b : 128 * q + 8 * b + 8] for q in range(4)]
            wpt[layer, b] = jnp.concatenate(rows, axis=0).astype(BF16)
        spread_out(gain_ref, layer, 0)
        spread_out(bias_ref, layer, 1)

    def prepare_out(layer):
        wgt[layer] = wg_ref[layer].astype(F32).T.astype(BF16)
        wot[layer] = wo_ref[layer].astype(F32).T.astype(BF16)
        spread_out(ogain_ref, layer, 2)
        spread_out(obias_ref, layer, 3)

    def normalize(layer, s, values):
        center = values - jnp.mean(values, axis=0, keepdims=True)
        spread = jnp.mean(center * center, axis=0, keepdims=True)
        scaled = center * lax.rsqrt(spread + 1e-05) * gains[layer, 0] + gains[layer, 1]
        normed[:, CH * s : CH * s + CH] = scaled.astype(BF16)
        cur[s] = values

    def send(src, dst, to_row, to_col, send_sem, recv_sem, here):
        def local():
            pltpu.make_async_copy(src, dst, recv_sem).start()

        def remote():
            pltpu.make_async_remote_copy(
                src_ref=src, dst_ref=dst, send_sem=send_sem, recv_sem=recv_sem,
                device_id=(to_row, to_col), device_id_type=MESH,
            ).start()

        if here is None:
            remote()
        else:
            pl.when(here)(local)
            pl.when(jnp.logical_not(here))(remote)

    def sent(buffer, sem, home):
        count = buffer.shape[0]

        @pl.when(home)
        def _():
            part = buffer.at[pl.ds(0, count - 1)]
            pltpu.make_async_copy(part, part, sem).wait()

        @pl.when(jnp.logical_not(home))
        def _():
            pltpu.make_async_copy(buffer, buffer, sem).wait()

    def arrived(buffer, sem):
        pltpu.make_async_copy(buffer, buffer, sem).wait()

    def scatter(layer):
        to_core = y_lo if layer == 0 else col // 16
        corner = y_hi * 2 + core
        slot = z * 16 + x * 4 + corner if layer == 0 else z_low * 32 + row * 4 + corner
        dst = (recv1 if layer == 0 else recv2).at[slot]
        highs = [y_hi, 1 - y_hi]
        columns = [lax.rem(x + d, 4) for d in range(4)]

        @pl.loop(0, 8)
        def _(g):
            step, low = g // 2, lax.rem(y_lo + g, 2)
            depths = [lax.rem(z + 4 + step, 8), lax.rem(z + 3 - step, 8)]
            blocks = [low * 8 + depth for depth in depths]
            weights = jnp.concatenate([wpt[layer, block] for block in blocks], axis=0)
            proj = jnp.dot(weights, normed[...], preferred_element_type=F32)
            left = jnp.concatenate([jax.nn.sigmoid(proj[n : n + 8]) * proj[n + 8 : n + 16] for n in (0, 32)], axis=0)
            right = jnp.concatenate([jax.nn.sigmoid(proj[n : n + 8]) * proj[n + 8 : n + 16] for n in (16, 48)], axis=0)
            for s in range(8):
                keep = masks[s : s + 1, :]
                stage[pl.ds(s, 16, stride=16), :] = left[:, CH * s : CH * s + CH] * keep
                stage[pl.ds(s + 8, 16, stride=16), :] = right[:, CH * s : CH * s + CH] * keep
            for n, block in enumerate(blocks):
                tile[pl.ds(block * 8, 8)] = stage[128 * n : 128 * n + 128, :].reshape(8, 16, CH).astype(BF16)
            for dx in (2, 1, 3, 0):
                for dh in (1, 0):
                    for n in range(2):
                        here = None
                        if n == 1 and dx + dh == 0:
                            here = jnp.logical_and(g == 6, to_core == core)
                        send(
                            tile.at[blocks[n] * 8 + columns[dx] * 2 + highs[dh]], dst,
                            low * 4 + columns[dx], depths[n] * 4 + highs[dh] * 2 + to_core,
                            send_sem.at[layer], in_sem.at[8 * layer + z], here,
                        )

        return to_core == core

    def make_gate(layer):
        for s in range(8):
            part = jnp.dot(wgt[layer], normed[:, CH * s : CH * s + CH], preferred_element_type=F32)
            gate[s] = jax.nn.sigmoid(part)

    def merge(first, second):
        low = lax.broadcasted_iota(jnp.int32, first.shape, 2) < 64
        even = jnp.where(low, first, pltpu.roll(second, 64, 2))
        odd = jnp.where(low, pltpu.roll(first, 64, 2), second)
        return even, odd

    def far_first(step, same):
        falling = (z_low < 2) == same
        return jnp.where(falling, 3 - step, step)

    def gather(layer):
        for step in range(8 if layer == 0 else 4):
            if layer == 0:
                recv, width, pairs = recv1, 16, 2
                place = lax.rem(z + (4, 5, 3, 6, 2, 7, 1, 0)[step], 8)
                sem = in_sem.at[place]
            else:
                recv, width, pairs = recv2, 32, 4
                place = far_first(step, z // 4 == core)
                sem = in_sem.at[8 + core * 4 + place]
            arrived(recv.at[pl.ds(place * width, width)], sem)
            rows = pl.ds(64 * step if layer == 0 else pl.multiple_of(place * 64, 64), 64)
            for p in range(pairs):
                first = recv[pl.ds(place * width + 8 * p, 4)].astype(F32)
                second = recv[pl.ds(place * width + 8 * p + 4, 4)].astype(F32)
                even, odd = merge(first, second)
                left = jnp.concatenate([even[:, :8], odd[:, :8]], axis=1).reshape(64, CH)
                right = jnp.concatenate([even[:, 8:], odd[:, 8:]], axis=1).reshape(64, CH)
                lanes = slice(128 * p, 128 * p + 128)
                if layer == 0:
                    mine_l[rows, lanes] = left.astype(BF16)
                    raw_r[rows, lanes] = right
                else:
                    mine_l2[rows, lanes] = left.astype(BF16)
                    mine_r[rows, lanes] = right.astype(BF16)
                if layer == 0 and step % 2 == 1:
                    block = slice(64 * step - 64, 64 * step + 64)
                    mine_r[lanes, block] = raw_r[block, lanes].T.astype(BF16)

    def quadrant(layer, q, right, dst):
        side = core if q == 0 else 1 - core
        lines = [lax.rem(x + n, 4) for n in range(4)]
        corners = [(y_hi if dy == 0 else 1 - y_hi) * 2 + (core if dc == 0 else 1 - core) for dy in range(2) for dc in range(2)]

        @pl.loop(0, 4)
        def _(step):
            depth = far_first(step, z // 4 == side)
            rows = right[pl.ds(pl.multiple_of(depth * 64, 64), 64), :]
            if layer == 0:
                mixed = jnp.dot(rows, mine_l[...], preferred_element_type=F32)
            else:
                mixed = lax.dot_general(rows, mine_l2[...], (((1,), (1,)), ((), ())), preferred_element_type=F32)
            base = q * 64 + depth * 16
            for p in range(2):
                block = mixed[:, 128 * p : 128 * p + 128].reshape(4, 16, CH)
                even, odd = merge(block[:, :8], block[:, 8:])
                outgoing[pl.ds(base + 8 * p, 4)] = even.astype(BF16)
                outgoing[pl.ds(base + 8 * p + 4, 4)] = odd.astype(BF16)
            for corner in (3, 2, 1, 0):
                for dx in (2, 1, 3, 0):
                    here = None
                    if corner == 0 and dx == 0:
                        here = jnp.logical_and(y_lo == core, side * 4 + depth == z)
                    send(
                        outgoing.at[base + lines[dx] * 4 + corners[corner]], dst,
                        core * 4 + lines[dx], (side * 4 + depth) * 4 + corners[corner],
                        ret_send.at[layer], ret_recv.at[2 * layer + y_lo], here,
                    )

    def multiply(layer):
        back = (back1 if layer == 0 else back2).at[own]
        swap = swap1 if layer == 0 else swap2
        gather(layer)
        exchange = pltpu.make_async_remote_copy(
            src_ref=mine_r, dst_ref=swap, send_sem=swap_send.at[layer], recv_sem=swap_recv.at[layer],
            device_id=(row, sibling), device_id_type=MESH,
        )
        exchange.start()
        quadrant(layer, 0, mine_r, back)
        exchange.wait_recv()
        quadrant(layer, 1, swap, back)
        exchange.wait_send()

    def finish(layer):
        back = back1 if layer == 0 else back2
        halves = []
        for part_y in range(2):
            arrived(back.at[pl.ds(64 * part_y, 64)], ret_recv.at[2 * layer + part_y])
            total = jnp.zeros((8, CH), F32)
            for g in range(4 * part_y, 4 * part_y + 4):
                part = back[16 * g : 16 * g + 16].astype(F32)
                wide[128 * g : 128 * g + 128, :] = part.reshape(128, CH)
                total = total + jnp.sum(part, axis=0)
            mean = total * (1.0 / 64)
            total = jnp.zeros((8, CH), F32)
            for g in range(4 * part_y, 4 * part_y + 4):
                part = wide[128 * g : 128 * g + 128, :].reshape(16, 8, CH) - mean[None]
                total = total + jnp.sum(part * part, axis=0)
            halves.append((mean, total))
        (mean0, total0), (mean1, total1) = halves
        apart = 0.5 * (mean0 - mean1)
        means[...] = 0.5 * (mean0 + mean1)
        rstds[...] = lax.rsqrt((total0 + total1) * (1.0 / CH) + apart * apart + 1e-05)

    def updated(layer, s):
        mixed = wide[pl.ds(s, CH, stride=8), :]
        out_normed = (mixed - means[s : s + 1, :]) * rstds[s : s + 1, :] * gains[layer, 2] + gains[layer, 3]
        update = jnp.dot(wot[layer], out_normed.astype(BF16), preferred_element_type=F32)
        return cur[s] + gate[s] * update

    loads[1].wait()
    make_masks()
    for n in (2, 3, 4):
        loads[n].wait()
    prepare(0)
    second_hop()
    loads[0].wait()
    wide[...] = pair_ref[...].astype(F32).reshape(POS, CH)
    for s in range(8):
        rows = [wide[pl.ds(256 * g + 16 * e + 2 * s + b, 8, stride=32), :] for b, g, e in order]
        normalize(0, s, jnp.concatenate(rows, axis=0).T)
    pl.semaphore_wait(hop_sem, COLS - 1)
    home1 = scatter(0)
    multiply(0)
    for n in (5, 6, 7, 8):
        loads[n].wait()
    prepare_out(0)
    make_gate(0)
    prepare(1)
    prepare_out(1)
    sent(tile, send_sem.at[0], home1)
    finish(0)
    for s in range(8):
        normalize(1, s, updated(0, s).astype(BF16).astype(F32))
    home2 = scatter(1)
    sent(outgoing, ret_send.at[0], home1)
    multiply(1)
    make_gate(1)
    sent(tile, send_sem.at[1], home2)
    finish(1)
    for s in range(8):
        values = updated(1, s).T
        for n, (b, g, e) in enumerate(order):
            stage[pl.ds(256 * g + 16 * e + 2 * s + b, 8, stride=32), :] = values[8 * n : 8 * n + 8]
    out_ref[...] = stage[...].reshape(TR, TC, CH).astype(BF16)
    sent(outgoing, ret_send.at[1], home1)


def shards(pair, residue_mask, in_gain, in_bias, proj_weight, gate_weight, out_gain, out_bias, out_weight):
    arguments = (
        pair, residue_mask.reshape(1, 512), in_gain, in_bias, proj_weight, gate_weight, out_gain, out_bias, out_weight
    )
    dma = pltpu.SemaphoreType.DMA
    return pl.pallas_call(
        kernel,
        out_shape=pltpu.VMEM((TR, TC, CH), BF16),
        in_specs=[pl.BlockSpec(memory_space=pltpu.HBM)] * 9,
        out_specs=pl.BlockSpec(memory_space=pltpu.VMEM),
        scratch_shapes=[pltpu.VMEM(value.shape, value.dtype) for value in arguments] + [
            pltpu.VMEM((POS, CH), F32),
            pltpu.VMEM((8, CH, CH), F32),
            pltpu.VMEM((8, CH, CH), F32),
            pltpu.VMEM((POS, CH), F32),
            pltpu.VMEM((8, CH), F32),
            pltpu.VMEM((8, CH), F32),
            pltpu.VMEM((8, CH), F32),
            pltpu.VMEM((CH, POS), BF16),
            pltpu.VMEM((2, 16, 32, CH), BF16),
            pltpu.VMEM((2, CH, CH), BF16),
            pltpu.VMEM((2, CH, CH), BF16),
            pltpu.VMEM((2, 4, CH, CH), F32),
            pltpu.VMEM((CH, 16, CH), BF16),
            pltpu.VMEM((CH, 16, CH), BF16),
            pltpu.VMEM((CH, 16, CH), BF16),
            pltpu.VMEM((CH, 8, CH), BF16),
            pltpu.VMEM((CH, 8, CH), BF16),
            pltpu.VMEM((256, 512), BF16),
            pltpu.VMEM((256, 512), BF16),
            pltpu.VMEM((256, 512), BF16),
            pltpu.VMEM((512, 256), BF16),
            pltpu.VMEM((256, 512), BF16),
            pltpu.VMEM((512, 256), F32),
            pltpu.VMEM((CH, 8, CH), BF16),
            dma((9,)),
            pltpu.SemaphoreType.REGULAR,
            dma((2,)), dma((16,)), dma((2,)), dma((2,)), dma((2,)), dma((4,)),
        ],
        compiler_params=pltpu.CompilerParams(
            collective_id=0, has_side_effects=True, vmem_limit_bytes=48 * 1024 * 1024
        ),
        cost_estimate=pl.CostEstimate(flops=700_000_000, bytes_accessed=4_000_000, transcendentals=1_000_000),
    )(*[pltpu.with_memory_space_constraint(value, pltpu.HBM) for value in arguments])


def solution(mesh):
    placed = (P("row", "col", None), P(), P(), P(), P(), P(), P(), P(), P())
    return jax.shard_map(
        shards, mesh=mesh, in_specs=placed, out_specs=P("row", "col", None), check_vma=False
    )
```

```python
import jax
import jax.numpy as jnp
from jax import lax
from jax.experimental import pallas as pl
from jax.experimental.pallas import tpu as pltpu
from jax.sharding import PartitionSpec as P

MESH = pl.DeviceIdType.MESH
F32 = jnp.float32
BF16 = jnp.bfloat16
ROWS, COLS = 8, 32
TR, TC = 64, 16
CH = 128
POS = TR * TC


def kernel(
    pair_hbm, mask_hbm, gain_hbm, bias_hbm, wp_hbm, wg_hbm, ogain_hbm, obias_hbm, wo_hbm,
    out_ref,
    pair_ref, mask_in, gain_ref, bias_ref, wp_ref, wg_ref, ogain_ref, obias_ref, wo_ref,
    wide, cur, gate, stage, masks, means, rstds, normed, wpt, wgt, wot, gains,
    tile, recv1, recv2, back1, back2, swap1, swap2, mine_r, mine_l, mine_l2, raw_r, outgoing,
    load_sem, hop_sem, send_sem, in_sem, swap_send, swap_recv, ret_send, ret_recv,
):
    row = lax.axis_index("row")
    col = lax.axis_index("col")
    core = lax.rem(col, 2)
    sibling = col + 1 - 2 * core
    x, y_lo = lax.rem(row, 4), row // 4
    z, y_hi = col // 4, lax.rem(col // 2, 2)

    z_low = lax.rem(z, 4)
    colour_here = lax.rem(x + 4 - z_low, 4)
    own = (colour_here * 4 + z_low) * 8 + z // 4 * 4 + y_hi * 2 + y_lo

    loads = [
        pltpu.make_async_copy(src, dst, load_sem.at[n])
        for n, (src, dst) in enumerate([
            (pair_hbm, pair_ref), (mask_hbm, mask_in), (gain_hbm, gain_ref), (bias_hbm, bias_ref), (wp_hbm, wp_ref),
            (wg_hbm, wg_ref), (ogain_hbm, ogain_ref), (obias_hbm, obias_ref), (wo_hbm, wo_ref),
        ])
    ]
    for load in loads:
        load.start()

    barrier = pltpu.get_barrier_semaphore()

    @pl.loop(1, ROWS)
    def _(d):
        pl.semaphore_signal(barrier, inc=1, device_id=(lax.rem(row + d, ROWS), col), device_id_type=MESH)

    @pl.loop(1, COLS)
    def _(d):
        pl.semaphore_signal(barrier, inc=1, device_id=(row, lax.rem(col + d, COLS)), device_id_type=MESH)

    def second_hop():
        pl.semaphore_wait(barrier, ROWS - 1 + COLS - 1)

        @pl.loop(1, COLS)
        def _(d):
            pl.semaphore_signal(hop_sem, inc=1, device_id=(row, lax.rem(col + d, COLS)), device_id_type=MESH)

    order = [(b, g, e) for b in range(2) for g in range(4) for e in range(2)]

    def make_masks():
        lane = lax.broadcasted_iota(jnp.int32, (8, CH), 1)
        mask = mask_in[...].astype(F32)
        number = lax.broadcasted_iota(jnp.int32, (8, 512), 1)
        sub = lax.broadcasted_iota(jnp.int32, (8, 512), 0)
        even_b = jnp.sum(jnp.where(number == TC * col + 2 * sub, mask, 0.0), axis=1, keepdims=True)
        odd_b = jnp.sum(jnp.where(number == TC * col + 2 * sub + 1, mask, 0.0), axis=1, keepdims=True)
        mask_b = jnp.where(lane < 64, even_b, odd_b)
        place = lax.broadcasted_iota(jnp.int32, (1, CH), 1)
        place = place - jnp.where(place >= 64, 64, 0)
        a_of = 16 * (place // 16) + (place // 8) % 2 + 2 * (place % 8)
        pick = jnp.where(lax.broadcasted_iota(jnp.int32, (512, CH), 0) == TR * row + a_of, 1.0, 0.0).astype(BF16)
        mask_a = jnp.dot(jnp.broadcast_to(mask, (8, 512)).astype(BF16), pick, preferred_element_type=F32)
        masks[...] = mask_a * mask_b

    def spread_out(ref, layer, n):
        gains[layer, n] = jnp.broadcast_to(ref[layer : layer + 1, :], (CH, CH)).T

    def prepare(layer):
        turned = wp_ref[layer].astype(F32).T
        for b in range(16):
            rows = [turned[128 * q + 8 * b : 128 * q + 8 * b + 8] for q in range(4)]
            wpt[layer, b] = jnp.concatenate(rows, axis=0).astype(BF16)
        spread_out(gain_ref, layer, 0)
        spread_out(bias_ref, layer, 1)

    def prepare_out(layer):
        wgt[layer] = wg_ref[layer].astype(F32).T.astype(BF16)
        wot[layer] = wo_ref[layer].astype(F32).T.astype(BF16)
        spread_out(ogain_ref, layer, 2)
        spread_out(obias_ref, layer, 3)

    def normalize(layer, s, values):
        center = values - jnp.mean(values, axis=0, keepdims=True)
        spread = jnp.mean(center * center, axis=0, keepdims=True)
        scaled = center * lax.rsqrt(spread + 1e-05) * gains[layer, 0] + gains[layer, 1]
        normed[:, CH * s : CH * s + CH] = scaled.astype(BF16)
        cur[s] = values

    def send(src, dst, to_row, to_col, send_sem, recv_sem, here):
        def local():
            pltpu.make_async_copy(src, dst, recv_sem).start()

        def remote():
            pltpu.make_async_remote_copy(
                src_ref=src, dst_ref=dst, send_sem=send_sem, recv_sem=recv_sem,
                device_id=(to_row, to_col), device_id_type=MESH,
            ).start()

        if here is None:
            remote()
        else:
            pl.when(here)(local)
            pl.when(jnp.logical_not(here))(remote)

    def sent(buffer, sem, home):
        count = buffer.shape[0]

        @pl.when(home)
        def _():
            part = buffer.at[pl.ds(0, count - 1)]
            pltpu.make_async_copy(part, part, sem).wait()

        @pl.when(jnp.logical_not(home))
        def _():
            pltpu.make_async_copy(buffer, buffer, sem).wait()

    def arrived(buffer, sem):
        pltpu.make_async_copy(buffer, buffer, sem).wait()

    def scatter(layer):
        to_core = y_lo if layer == 0 else col // 16
        corner = y_hi * 2 + core
        slot = z * 16 + x * 4 + corner if layer == 0 else z_low * 32 + row * 4 + corner
        dst = (recv1 if layer == 0 else recv2).at[slot]
        lows = [y_lo, 1 - y_lo]
        highs = [y_hi, 1 - y_hi]
        sides = [z // 4, 1 - z // 4]

        @pl.loop(0, 8)
        def _(g):
            colour, step = g // 2, lax.rem(g, 2)
            depths = [lax.rem(z_low + 3 - step, 4), lax.rem(z_low + step, 4)]
            blocks = [colour * 4 + depth for depth in depths]
            weights = jnp.concatenate([wpt[layer, block] for block in blocks], axis=0)
            proj = jnp.dot(weights, normed[...], preferred_element_type=F32)
            left = jnp.concatenate([jax.nn.sigmoid(proj[n : n + 8]) * proj[n + 8 : n + 16] for n in (0, 32)], axis=0)
            right = jnp.concatenate([jax.nn.sigmoid(proj[n : n + 8]) * proj[n + 8 : n + 16] for n in (16, 48)], axis=0)
            for s in range(8):
                keep = masks[s : s + 1, :]
                stage[pl.ds(s, 16, stride=16), :] = left[:, CH * s : CH * s + CH] * keep
                stage[pl.ds(s + 8, 16, stride=16), :] = right[:, CH * s : CH * s + CH] * keep
            for n, block in enumerate(blocks):
                tile[pl.ds(block * 8, 8)] = stage[128 * n : 128 * n + 128, :].reshape(8, 16, CH).astype(BF16)
            columns = [lax.rem(colour + depth, 4) for depth in depths]
            for dz in (1, 0):
                for dh in (1, 0):
                    for dl in (1, 0):
                        for n in range(2):
                            here = None
                            if n == 1 and dz + dh + dl == 0:
                                here = jnp.logical_and(g == 2 * colour_here, to_core == core)
                            send(
                                tile.at[blocks[n] * 8 + sides[dz] * 4 + highs[dh] * 2 + lows[dl]], dst,
                                lows[dl] * 4 + columns[n], (sides[dz] * 4 + depths[n]) * 4 + highs[dh] * 2 + to_core,
                                send_sem.at[layer], in_sem.at[8 * layer + z], here,
                            )

        return to_core == core

    def make_gate(layer):
        for s in range(8):
            part = jnp.dot(wgt[layer], normed[:, CH * s : CH * s + CH], preferred_element_type=F32)
            gate[s] = jax.nn.sigmoid(part)

    def merge(first, second):
        low = lax.broadcasted_iota(jnp.int32, first.shape, 2) < 64
        even = jnp.where(low, first, pltpu.roll(second, 64, 2))
        odd = jnp.where(low, pltpu.roll(first, 64, 2), second)
        return even, odd

    def far_first(step, same):
        falling = (z_low < 2) == same
        return jnp.where(falling, 3 - step, step)

    def gather(layer):
        for step in range(8 if layer == 0 else 4):
            if layer == 0:
                recv, width, pairs = recv1, 16, 2
                place = lax.rem(z + (5, 1, 4, 0, 6, 2, 7, 3)[step], 8)
                sem = in_sem.at[place]
            else:
                recv, width, pairs = recv2, 32, 4
                place = lax.rem(z_low + (1, 0, 2, 3)[step], 4)
                sem = in_sem.at[8 + core * 4 + place]
            arrived(recv.at[pl.ds(place * width, width)], sem)
            rows = pl.ds(64 * step if layer == 0 else pl.multiple_of(place * 64, 64), 64)
            for p in range(pairs):
                first = recv[pl.ds(place * width + 8 * p, 4)].astype(F32)
                second = recv[pl.ds(place * width + 8 * p + 4, 4)].astype(F32)
                even, odd = merge(first, second)
                left = jnp.concatenate([even[:, :8], odd[:, :8]], axis=1).reshape(64, CH)
                right = jnp.concatenate([even[:, 8:], odd[:, 8:]], axis=1).reshape(64, CH)
                lanes = slice(128 * p, 128 * p + 128)
                if layer == 0:
                    mine_l[rows, lanes] = left.astype(BF16)
                    raw_r[rows, lanes] = right
                else:
                    mine_l2[rows, lanes] = left.astype(BF16)
                    mine_r[rows, lanes] = right.astype(BF16)
                if layer == 0 and step % 2 == 1:
                    block = slice(64 * step - 64, 64 * step + 64)
                    mine_r[lanes, block] = raw_r[block, lanes].T.astype(BF16)

    def quadrant(layer, q, right, dst):
        side = core if q == 0 else 1 - core
        lines = [lax.rem(x + n, 4) for n in range(4)]
        corners = [(y_hi if dy == 0 else 1 - y_hi) * 2 + (core if dc == 0 else 1 - core) for dy in range(2) for dc in range(2)]

        @pl.loop(0, 4)
        def _(step):
            depth = far_first(step, z // 4 == side)
            rows = right[pl.ds(pl.multiple_of(depth * 64, 64), 64), :]
            if layer == 0:
                mixed = jnp.dot(rows, mine_l[...], preferred_element_type=F32)
            else:
                mixed = lax.dot_general(rows, mine_l2[...], (((1,), (1,)), ((), ())), preferred_element_type=F32)
            base = q * 64 + depth * 16
            for p in range(2):
                block = mixed[:, 128 * p : 128 * p + 128].reshape(4, 16, CH)
                even, odd = merge(block[:, :8], block[:, 8:])
                outgoing[pl.ds(base + 8 * p, 4)] = even.astype(BF16)
                outgoing[pl.ds(base + 8 * p + 4, 4)] = odd.astype(BF16)
            for corner in (3, 2, 1, 0):
                for dx in (2, 1, 3, 0):
                    here = None
                    if corner == 0 and dx == 0:
                        here = jnp.logical_and(y_lo == core, side * 4 + depth == z)
                    send(
                        outgoing.at[base + lines[dx] * 4 + corners[corner]], dst,
                        core * 4 + lines[dx], (side * 4 + depth) * 4 + corners[corner],
                        ret_send.at[layer], ret_recv.at[2 * layer + colour_here // 2], here,
                    )

    def multiply(layer):
        back = (back1 if layer == 0 else back2).at[own]
        swap = swap1 if layer == 0 else swap2
        gather(layer)
        exchange = pltpu.make_async_remote_copy(
            src_ref=mine_r, dst_ref=swap, send_sem=swap_send.at[layer], recv_sem=swap_recv.at[layer],
            device_id=(row, sibling), device_id_type=MESH,
        )
        exchange.start()
        quadrant(layer, 0, mine_r, back)
        exchange.wait_recv()
        quadrant(layer, 1, swap, back)
        exchange.wait_send()

    def finish(layer):
        back = back1 if layer == 0 else back2
        halves = []
        for colour in range(2):
            arrived(back.at[pl.ds(64 * colour, 64)], ret_recv.at[2 * layer + colour])
            total = jnp.zeros((8, CH), F32)
            for g in range(4 * colour, 4 * colour + 4):
                part = back[16 * g : 16 * g + 16].astype(F32)
                wide[128 * g : 128 * g + 128, :] = part.reshape(128, CH)
                total = total + jnp.sum(part, axis=0)
            mean = total * (1.0 / 64)
            total = jnp.zeros((8, CH), F32)
            for g in range(4 * colour, 4 * colour + 4):
                part = wide[128 * g : 128 * g + 128, :].reshape(16, 8, CH) - mean[None]
                total = total + jnp.sum(part * part, axis=0)
            halves.append((mean, total))
        (mean0, total0), (mean1, total1) = halves
        apart = 0.5 * (mean0 - mean1)
        means[...] = 0.5 * (mean0 + mean1)
        rstds[...] = lax.rsqrt((total0 + total1) * (1.0 / CH) + apart * apart + 1e-05)

    def updated(layer, s):
        mixed = wide[pl.ds(s, CH, stride=8), :]
        out_normed = (mixed - means[s : s + 1, :]) * rstds[s : s + 1, :] * gains[layer, 2] + gains[layer, 3]
        update = jnp.dot(wot[layer], out_normed.astype(BF16), preferred_element_type=F32)
        return cur[s] + gate[s] * update

    loads[1].wait()
    make_masks()
    for n in (2, 3, 4):
        loads[n].wait()
    prepare(0)
    second_hop()
    loads[0].wait()
    wide[...] = pair_ref[...].astype(F32).reshape(POS, CH)
    for s in range(8):
        rows = [wide[pl.ds(256 * g + 16 * e + 2 * s + b, 8, stride=32), :] for b, g, e in order]
        normalize(0, s, jnp.concatenate(rows, axis=0).T)
    pl.semaphore_wait(hop_sem, COLS - 1)
    home1 = scatter(0)
    multiply(0)
    for n in (5, 6, 7, 8):
        loads[n].wait()
    prepare_out(0)
    make_gate(0)
    prepare(1)
    prepare_out(1)
    sent(tile, send_sem.at[0], home1)
    finish(0)
    for s in range(8):
        normalize(1, s, updated(0, s).astype(BF16).astype(F32))
    home2 = scatter(1)
    sent(outgoing, ret_send.at[0], home1)
    multiply(1)
    make_gate(1)
    sent(tile, send_sem.at[1], home2)
    finish(1)
    for s in range(8):
        values = updated(1, s).T
        for n, (b, g, e) in enumerate(order):
            stage[pl.ds(256 * g + 16 * e + 2 * s + b, 8, stride=32), :] = values[8 * n : 8 * n + 8]
    out_ref[...] = stage[...].reshape(TR, TC, CH).astype(BF16)
    sent(outgoing, ret_send.at[1], home1)


def shards(pair, residue_mask, in_gain, in_bias, proj_weight, gate_weight, out_gain, out_bias, out_weight):
    arguments = (
        pair, residue_mask.reshape(1, 512), in_gain, in_bias, proj_weight, gate_weight, out_gain, out_bias, out_weight
    )
    dma = pltpu.SemaphoreType.DMA
    return pl.pallas_call(
        kernel,
        out_shape=pltpu.VMEM((TR, TC, CH), BF16),
        in_specs=[pl.BlockSpec(memory_space=pltpu.HBM)] * 9,
        out_specs=pl.BlockSpec(memory_space=pltpu.VMEM),
        scratch_shapes=[pltpu.VMEM(value.shape, value.dtype) for value in arguments] + [
            pltpu.VMEM((POS, CH), F32),
            pltpu.VMEM((8, CH, CH), F32),
            pltpu.VMEM((8, CH, CH), F32),
            pltpu.VMEM((POS, CH), F32),
            pltpu.VMEM((8, CH), F32),
            pltpu.VMEM((8, CH), F32),
            pltpu.VMEM((8, CH), F32),
            pltpu.VMEM((CH, POS), BF16),
            pltpu.VMEM((2, 16, 32, CH), BF16),
            pltpu.VMEM((2, CH, CH), BF16),
            pltpu.VMEM((2, CH, CH), BF16),
            pltpu.VMEM((2, 4, CH, CH), F32),
            pltpu.VMEM((CH, 16, CH), BF16),
            pltpu.VMEM((CH, 16, CH), BF16),
            pltpu.VMEM((CH, 16, CH), BF16),
            pltpu.VMEM((CH, 8, CH), BF16),
            pltpu.VMEM((CH, 8, CH), BF16),
            pltpu.VMEM((256, 512), BF16),
            pltpu.VMEM((256, 512), BF16),
            pltpu.VMEM((256, 512), BF16),
            pltpu.VMEM((512, 256), BF16),
            pltpu.VMEM((256, 512), BF16),
            pltpu.VMEM((512, 256), F32),
            pltpu.VMEM((CH, 8, CH), BF16),
            dma((9,)),
            pltpu.SemaphoreType.REGULAR,
            dma((2,)), dma((16,)), dma((2,)), dma((2,)), dma((2,)), dma((4,)),
        ],
        compiler_params=pltpu.CompilerParams(
            collective_id=0, has_side_effects=True, vmem_limit_bytes=48 * 1024 * 1024
        ),
        cost_estimate=pl.CostEstimate(flops=700_000_000, bytes_accessed=4_000_000, transcendentals=1_000_000),
    )(*[pltpu.with_memory_space_constraint(value, pltpu.HBM) for value in arguments])


def solution(mesh):
    placed = (P("row", "col", None), P(), P(), P(), P(), P(), P(), P(), P())
    return jax.shard_map(
        shards, mesh=mesh, in_specs=placed, out_specs=P("row", "col", None), check_vma=False
    )
```

```python
import jax
import jax.numpy as jnp
from jax import lax
from jax.experimental import pallas as pl
from jax.experimental.pallas import tpu as pltpu
from jax.sharding import PartitionSpec as P

MESH = pl.DeviceIdType.MESH
F32 = jnp.float32
BF16 = jnp.bfloat16
ROWS, COLS = 8, 32
TR, TC = 64, 16
CH = 128
POS = TR * TC


def kernel(
    pair_hbm, mask_hbm, gain_hbm, bias_hbm, wp_hbm, wg_hbm, ogain_hbm, obias_hbm, wo_hbm,
    out_ref,
    pair_ref, mask_in, gain_ref, bias_ref, wp_ref, wg_ref, ogain_ref, obias_ref, wo_ref,
    wide, cur, gate, stage, masks, means, rstds, normed, wpt, wgt, wot, gains,
    tile, recv1, recv2, back1, back2, swap1, swap2, mine_r, mine_l, mine_l2, raw_r, outgoing,
    load_sem, hop_sem, send_sem, in_sem, swap_send, swap_recv, ret_send, ret_recv,
):
    row = lax.axis_index("row")
    col = lax.axis_index("col")
    core = lax.rem(col, 2)
    sibling = col + 1 - 2 * core
    x, y_lo = lax.rem(row, 4), row // 4
    z, y_hi = col // 4, lax.rem(col // 2, 2)

    z_low = lax.rem(z, 4)
    colour_here = lax.rem(x + 4 - z_low, 4)
    own = (colour_here * 4 + z_low) * 8 + z // 4 * 4 + y_hi * 2 + y_lo

    loads = [
        pltpu.make_async_copy(src, dst, load_sem.at[n])
        for n, (src, dst) in enumerate([
            (pair_hbm, pair_ref), (mask_hbm, mask_in), (gain_hbm, gain_ref), (bias_hbm, bias_ref), (wp_hbm, wp_ref),
            (wg_hbm, wg_ref), (ogain_hbm, ogain_ref), (obias_hbm, obias_ref), (wo_hbm, wo_ref),
        ])
    ]
    for load in loads:
        load.start()

    barrier = pltpu.get_barrier_semaphore()

    @pl.loop(1, ROWS)
    def _(d):
        pl.semaphore_signal(barrier, inc=1, device_id=(lax.rem(row + d, ROWS), col), device_id_type=MESH)

    @pl.loop(1, COLS)
    def _(d):
        pl.semaphore_signal(barrier, inc=1, device_id=(row, lax.rem(col + d, COLS)), device_id_type=MESH)

    def second_hop():
        pl.semaphore_wait(barrier, ROWS - 1 + COLS - 1)

        @pl.loop(1, COLS)
        def _(d):
            pl.semaphore_signal(hop_sem, inc=1, device_id=(row, lax.rem(col + d, COLS)), device_id_type=MESH)

    order = [(b, g, e) for b in range(2) for g in range(4) for e in range(2)]

    def make_masks():
        lane = lax.broadcasted_iota(jnp.int32, (8, CH), 1)
        mask = mask_in[...].astype(F32)
        number = lax.broadcasted_iota(jnp.int32, (8, 512), 1)
        sub = lax.broadcasted_iota(jnp.int32, (8, 512), 0)
        even_b = jnp.sum(jnp.where(number == TC * col + 2 * sub, mask, 0.0), axis=1, keepdims=True)
        odd_b = jnp.sum(jnp.where(number == TC * col + 2 * sub + 1, mask, 0.0), axis=1, keepdims=True)
        mask_b = jnp.where(lane < 64, even_b, odd_b)
        place = lax.broadcasted_iota(jnp.int32, (1, CH), 1)
        place = place - jnp.where(place >= 64, 64, 0)
        a_of = 16 * (place // 16) + (place // 8) % 2 + 2 * (place % 8)
        pick = jnp.where(lax.broadcasted_iota(jnp.int32, (512, CH), 0) == TR * row + a_of, 1.0, 0.0).astype(BF16)
        mask_a = jnp.dot(jnp.broadcast_to(mask, (8, 512)).astype(BF16), pick, preferred_element_type=F32)
        masks[...] = mask_a * mask_b

    def spread_out(ref, layer, n):
        gains[layer, n] = jnp.broadcast_to(ref[layer : layer + 1, :], (CH, CH)).T

    def prepare(layer):
        turned = wp_ref[layer].astype(F32).T
        for b in range(16):
            rows = [turned[128 * q + 8 * b : 128 * q + 8 * b + 8] for q in range(4)]
            wpt[layer, b] = jnp.concatenate(rows, axis=0).astype(BF16)
        spread_out(gain_ref, layer, 0)
        spread_out(bias_ref, layer, 1)

    def prepare_out(layer):
        wgt[layer] = wg_ref[layer].astype(F32).T.astype(BF16)
        wot[layer] = wo_ref[layer].astype(F32).T.astype(BF16)
        spread_out(ogain_ref, layer, 2)
        spread_out(obias_ref, layer, 3)

    def normalize(layer, s, values):
        center = values - jnp.mean(values, axis=0, keepdims=True)
        spread = jnp.mean(center * center, axis=0, keepdims=True)
        scaled = center * lax.rsqrt(spread + 1e-05) * gains[layer, 0] + gains[layer, 1]
        normed[:, pl.ds(pl.multiple_of(s * CH, CH), CH)] = scaled.astype(BF16)
        cur[s] = values

    def send(src, dst, to_row, to_col, send_sem, recv_sem, here):
        def local():
            pltpu.make_async_copy(src, dst, recv_sem).start()

        def remote():
            pltpu.make_async_remote_copy(
                src_ref=src, dst_ref=dst, send_sem=send_sem, recv_sem=recv_sem,
                device_id=(to_row, to_col), device_id_type=MESH,
            ).start()

        if here is None:
            remote()
        else:
            pl.when(here)(local)
            pl.when(jnp.logical_not(here))(remote)

    def sent(buffer, sem, home):
        count = buffer.shape[0]

        @pl.when(home)
        def _():
            part = buffer.at[pl.ds(0, count - 1)]
            pltpu.make_async_copy(part, part, sem).wait()

        @pl.when(jnp.logical_not(home))
        def _():
            pltpu.make_async_copy(buffer, buffer, sem).wait()

    def arrived(buffer, sem):
        pltpu.make_async_copy(buffer, buffer, sem).wait()

    def scatter(layer):
        to_core = y_lo if layer == 0 else col // 16
        corner = y_hi * 2 + core
        slot = z * 16 + x * 4 + corner if layer == 0 else z_low * 32 + row * 4 + corner
        dst = (recv1 if layer == 0 else recv2).at[slot]
        lows = [y_lo, 1 - y_lo]
        highs = [y_hi, 1 - y_hi]
        sides = [z // 4, 1 - z // 4]

        @pl.loop(0, 8)
        def _(g):
            colour, step = g // 2, lax.rem(g, 2)
            depths = [lax.rem(z_low + 3 - step, 4), lax.rem(z_low + step, 4)]
            blocks = [colour * 4 + depth for depth in depths]
            weights = jnp.concatenate([wpt[layer, block] for block in blocks], axis=0)
            proj = jnp.dot(weights, normed[...], preferred_element_type=F32)
            left = jnp.concatenate([jax.nn.sigmoid(proj[n : n + 8]) * proj[n + 8 : n + 16] for n in (0, 32)], axis=0)
            right = jnp.concatenate([jax.nn.sigmoid(proj[n : n + 8]) * proj[n + 8 : n + 16] for n in (16, 48)], axis=0)
            for s in range(8):
                keep = masks[s : s + 1, :]
                stage[pl.ds(s, 16, stride=16), :] = left[:, CH * s : CH * s + CH] * keep
                stage[pl.ds(s + 8, 16, stride=16), :] = right[:, CH * s : CH * s + CH] * keep
            for n, block in enumerate(blocks):
                tile[pl.ds(block * 8, 8)] = stage[128 * n : 128 * n + 128, :].reshape(8, 16, CH).astype(BF16)
            columns = [lax.rem(colour + depth, 4) for depth in depths]
            for dz in (1, 0):
                for dh in (1, 0):
                    for dl in (1, 0):
                        for n in range(2):
                            here = None
                            if n == 1 and dz + dh + dl == 0:
                                here = jnp.logical_and(g == 2 * colour_here, to_core == core)
                            send(
                                tile.at[blocks[n] * 8 + sides[dz] * 4 + highs[dh] * 2 + lows[dl]], dst,
                                lows[dl] * 4 + columns[n], (sides[dz] * 4 + depths[n]) * 4 + highs[dh] * 2 + to_core,
                                send_sem.at[layer], in_sem.at[8 * layer + z], here,
                            )

        return to_core == core

    def make_gate(layer):
        @pl.loop(0, 8)
        def _(s):
            part = normed[:, pl.ds(pl.multiple_of(s * CH, CH), CH)]
            gate[s] = jax.nn.sigmoid(jnp.dot(wgt[layer], part, preferred_element_type=F32))

    def merge(first, second):
        low = lax.broadcasted_iota(jnp.int32, first.shape, 2) < 64
        even = jnp.where(low, first, pltpu.roll(second, 64, 2))
        odd = jnp.where(low, pltpu.roll(first, 64, 2), second)
        return even, odd

    def far_first(step, same):
        falling = (z_low < 2) == same
        return jnp.where(falling, 3 - step, step)

    def gather(layer):
        def collect(recv, width, place, p):
            first = recv[pl.ds(place * width + 8 * p, 4)].astype(F32)
            second = recv[pl.ds(place * width + 8 * p + 4, 4)].astype(F32)
            even, odd = merge(first, second)
            left = jnp.concatenate([even[:, :8], odd[:, :8]], axis=1).reshape(64, CH)
            right = jnp.concatenate([even[:, 8:], odd[:, 8:]], axis=1).reshape(64, CH)
            return left.astype(BF16), right

        @pl.loop(0, 4)
        def _(step):
            low = lax.rem(z_low + jnp.where(step < 2, 1 - step, step), 4)
            if layer == 0:
                block = pl.ds(pl.multiple_of(step * 128, 128), 128)
                for half in range(2):
                    place = low + 4 * half
                    arrived(recv1.at[pl.ds(place * 16, 16)], in_sem.at[place])
                    rows = pl.ds(pl.multiple_of(step * 128 + 64 * half, 64), 64)
                    for p in range(2):
                        mine_l[rows, 128 * p : 128 * p + 128], raw_r[rows, 128 * p : 128 * p + 128] = collect(recv1, 16, place, p)
                for p in range(2):
                    mine_r[128 * p : 128 * p + 128, block] = raw_r[block, 128 * p : 128 * p + 128].T.astype(BF16)
            else:
                arrived(recv2.at[pl.ds(low * 32, 32)], in_sem.at[8 + core * 4 + low])
                rows = pl.ds(pl.multiple_of(low * 64, 64), 64)
                for p in range(4):
                    left, right = collect(recv2, 32, low, p)
                    mine_l2[rows, 128 * p : 128 * p + 128] = left
                    mine_r[rows, 128 * p : 128 * p + 128] = right.astype(BF16)

    def quadrant(layer, q, right, dst):
        side = core if q == 0 else 1 - core
        lines = [lax.rem(x + n, 4) for n in range(4)]
        corners = [(y_hi if dy == 0 else 1 - y_hi) * 2 + (core if dc == 0 else 1 - core) for dy in range(2) for dc in range(2)]

        @pl.loop(0, 4)
        def _(step):
            depth = far_first(step, z // 4 == side)
            rows = right[pl.ds(pl.multiple_of(depth * 64, 64), 64), :]
            if layer == 0:
                mixed = jnp.dot(rows, mine_l[...], preferred_element_type=F32)
            else:
                mixed = lax.dot_general(rows, mine_l2[...], (((1,), (1,)), ((), ())), preferred_element_type=F32)
            base = q * 64 + depth * 16
            for p in range(2):
                block = mixed[:, 128 * p : 128 * p + 128].reshape(4, 16, CH)
                even, odd = merge(block[:, :8], block[:, 8:])
                outgoing[pl.ds(base + 8 * p, 4)] = even.astype(BF16)
                outgoing[pl.ds(base + 8 * p + 4, 4)] = odd.astype(BF16)
            for corner in (3, 2, 1, 0):
                for dx in (2, 1, 3, 0):
                    here = None
                    if corner == 0 and dx == 0:
                        here = jnp.logical_and(y_lo == core, side * 4 + depth == z)
                    send(
                        outgoing.at[base + lines[dx] * 4 + corners[corner]], dst,
                        core * 4 + lines[dx], (side * 4 + depth) * 4 + corners[corner],
                        ret_send.at[layer], ret_recv.at[2 * layer + colour_here // 2], here,
                    )

    def multiply(layer):
        back = (back1 if layer == 0 else back2).at[own]
        swap = swap1 if layer == 0 else swap2
        gather(layer)
        exchange = pltpu.make_async_remote_copy(
            src_ref=mine_r, dst_ref=swap, send_sem=swap_send.at[layer], recv_sem=swap_recv.at[layer],
            device_id=(row, sibling), device_id_type=MESH,
        )
        exchange.start()
        quadrant(layer, 0, mine_r, back)
        exchange.wait_recv()
        quadrant(layer, 1, swap, back)
        exchange.wait_send()

    def finish(layer):
        back = back1 if layer == 0 else back2
        halves = []
        zero = jnp.zeros((8, CH), F32)
        for part in range(2):
            arrived(back.at[pl.ds(64 * part, 64)], ret_recv.at[2 * layer + part])

            def add(g, total):
                values = back[pl.ds(64 * part + 16 * g, 16)].astype(F32)
                wide[pl.ds(pl.multiple_of(512 * part + 128 * g, 128), 128), :] = values.reshape(128, CH)
                return total + jnp.sum(values, axis=0)

            mean = lax.fori_loop(0, 4, add, zero) * (1.0 / 64)

            def vary(g, total):
                values = wide[pl.ds(pl.multiple_of(512 * part + 128 * g, 128), 128), :].reshape(16, 8, CH) - mean[None]
                return total + jnp.sum(values * values, axis=0)

            halves.append((mean, lax.fori_loop(0, 4, vary, zero)))
        (mean0, total0), (mean1, total1) = halves
        apart = 0.5 * (mean0 - mean1)
        means[...] = 0.5 * (mean0 + mean1)
        rstds[...] = lax.rsqrt((total0 + total1) * (1.0 / CH) + apart * apart + 1e-05)

    def updated(layer, s):
        mixed = wide[pl.ds(s, CH, stride=8), :]
        out_normed = (mixed - means[pl.ds(s, 1), :]) * rstds[pl.ds(s, 1), :] * gains[layer, 2] + gains[layer, 3]
        update = jnp.dot(wot[layer], out_normed.astype(BF16), preferred_element_type=F32)
        return cur[s] + gate[s] * update

    loads[1].wait()
    make_masks()
    for n in (2, 3, 4):
        loads[n].wait()
    prepare(0)
    second_hop()
    loads[0].wait()
    wide[...] = pair_ref[...].astype(F32).reshape(POS, CH)
    @pl.loop(0, 8)
    def _(s):
        rows = [wide[pl.ds(256 * g + 16 * e + 2 * s + b, 8, stride=32), :] for b, g, e in order]
        normalize(0, s, jnp.concatenate(rows, axis=0).T)
    pl.semaphore_wait(hop_sem, COLS - 1)
    home1 = scatter(0)
    multiply(0)
    for n in (5, 6, 7, 8):
        loads[n].wait()
    prepare_out(0)
    make_gate(0)
    prepare(1)
    prepare_out(1)
    sent(tile, send_sem.at[0], home1)
    finish(0)
    @pl.loop(0, 8)
    def _(s):
        normalize(1, s, updated(0, s).astype(BF16).astype(F32))
    home2 = scatter(1)
    sent(outgoing, ret_send.at[0], home1)
    multiply(1)
    make_gate(1)
    sent(tile, send_sem.at[1], home2)
    finish(1)
    @pl.loop(0, 8)
    def _(s):
        values = updated(1, s).T
        for n, (b, g, e) in enumerate(order):
            stage[pl.ds(256 * g + 16 * e + 2 * s + b, 8, stride=32), :] = values[8 * n : 8 * n + 8]
    out_ref[...] = stage[...].reshape(TR, TC, CH).astype(BF16)
    sent(outgoing, ret_send.at[1], home1)


def shards(pair, residue_mask, in_gain, in_bias, proj_weight, gate_weight, out_gain, out_bias, out_weight):
    arguments = (
        pair, residue_mask.reshape(1, 512), in_gain, in_bias, proj_weight, gate_weight, out_gain, out_bias, out_weight
    )
    dma = pltpu.SemaphoreType.DMA
    return pl.pallas_call(
        kernel,
        out_shape=pltpu.VMEM((TR, TC, CH), BF16),
        in_specs=[pl.BlockSpec(memory_space=pltpu.HBM)] * 9,
        out_specs=pl.BlockSpec(memory_space=pltpu.VMEM),
        scratch_shapes=[pltpu.VMEM(value.shape, value.dtype) for value in arguments] + [
            pltpu.VMEM((POS, CH), F32),
            pltpu.VMEM((8, CH, CH), F32),
            pltpu.VMEM((8, CH, CH), F32),
            pltpu.VMEM((POS, CH), F32),
            pltpu.VMEM((8, CH), F32),
            pltpu.VMEM((8, CH), F32),
            pltpu.VMEM((8, CH), F32),
            pltpu.VMEM((CH, POS), BF16),
            pltpu.VMEM((2, 16, 32, CH), BF16),
            pltpu.VMEM((2, CH, CH), BF16),
            pltpu.VMEM((2, CH, CH), BF16),
            pltpu.VMEM((2, 4, CH, CH), F32),
            pltpu.VMEM((CH, 16, CH), BF16),
            pltpu.VMEM((CH, 16, CH), BF16),
            pltpu.VMEM((CH, 16, CH), BF16),
            pltpu.VMEM((CH, 8, CH), BF16),
            pltpu.VMEM((CH, 8, CH), BF16),
            pltpu.VMEM((256, 512), BF16),
            pltpu.VMEM((256, 512), BF16),
            pltpu.VMEM((256, 512), BF16),
            pltpu.VMEM((512, 256), BF16),
            pltpu.VMEM((256, 512), BF16),
            pltpu.VMEM((512, 256), F32),
            pltpu.VMEM((CH, 8, CH), BF16),
            dma((9,)),
            pltpu.SemaphoreType.REGULAR,
            dma((2,)), dma((16,)), dma((2,)), dma((2,)), dma((2,)), dma((4,)),
        ],
        compiler_params=pltpu.CompilerParams(
            collective_id=0, has_side_effects=True, vmem_limit_bytes=48 * 1024 * 1024
        ),
        cost_estimate=pl.CostEstimate(flops=700_000_000, bytes_accessed=4_000_000, transcendentals=1_000_000),
    )(*[pltpu.with_memory_space_constraint(value, pltpu.HBM) for value in arguments])


def solution(mesh):
    placed = (P("row", "col", None), P(), P(), P(), P(), P(), P(), P(), P())
    return jax.shard_map(
        shards, mesh=mesh, in_specs=placed, out_specs=P("row", "col", None), check_vma=False
    )
```

```python
import jax
import jax.numpy as jnp
from jax import lax
from jax.experimental import pallas as pl
from jax.experimental.pallas import tpu as pltpu
from jax.sharding import PartitionSpec as P

MESH = pl.DeviceIdType.MESH
F32 = jnp.float32
BF16 = jnp.bfloat16
ROWS, COLS = 8, 32
TR, TC = 64, 16
CH = 128
POS = TR * TC


def kernel(
    pair_hbm, mask_hbm, gain_hbm, bias_hbm, wp_hbm, wg_hbm, ogain_hbm, obias_hbm, wo_hbm,
    out_ref,
    pair_ref, mask_in, gain_ref, bias_ref, wp_ref, wg_ref, ogain_ref, obias_ref, wo_ref,
    wide, cur, gate, stage, masks, means, rstds, normed, wpt, wgt, wot, gains,
    tile, recv1, recv2, back1, back2, swap1, swap2, mine_r, mine_l, mine_l2, raw_r, outgoing,
    load_sem, hop_sem, send_sem, in_sem, swap_send, swap_recv, ret_send, ret_recv,
):
    row = lax.axis_index("row")
    col = lax.axis_index("col")
    core = lax.rem(col, 2)
    sibling = col + 1 - 2 * core
    x, y_lo = lax.rem(row, 4), row // 4
    z, y_hi = col // 4, lax.rem(col // 2, 2)

    z_low = lax.rem(z, 4)
    colour_here = lax.rem(x + 4 - z_low, 4)
    own = (colour_here * 4 + z_low) * 8 + z // 4 * 4 + y_hi * 2 + y_lo

    loads = [
        pltpu.make_async_copy(src, dst, load_sem.at[n])
        for n, (src, dst) in enumerate([
            (pair_hbm, pair_ref), (mask_hbm, mask_in), (gain_hbm, gain_ref), (bias_hbm, bias_ref), (wp_hbm, wp_ref),
            (wg_hbm, wg_ref), (ogain_hbm, ogain_ref), (obias_hbm, obias_ref), (wo_hbm, wo_ref),
        ])
    ]
    for load in loads:
        load.start()

    barrier = pltpu.get_barrier_semaphore()

    @pl.loop(1, ROWS)
    def _(d):
        pl.semaphore_signal(barrier, inc=1, device_id=(lax.rem(row + d, ROWS), col), device_id_type=MESH)

    @pl.loop(1, COLS)
    def _(d):
        pl.semaphore_signal(barrier, inc=1, device_id=(row, lax.rem(col + d, COLS)), device_id_type=MESH)

    def second_hop():
        pl.semaphore_wait(barrier, ROWS - 1 + COLS - 1)

        @pl.loop(1, COLS)
        def _(d):
            pl.semaphore_signal(hop_sem, inc=1, device_id=(row, lax.rem(col + d, COLS)), device_id_type=MESH)

    order = [(b, g, e) for b in range(2) for g in range(4) for e in range(2)]

    def make_masks():
        lane = lax.broadcasted_iota(jnp.int32, (8, CH), 1)
        mask = mask_in[...].astype(F32)
        number = lax.broadcasted_iota(jnp.int32, (8, 512), 1)
        sub = lax.broadcasted_iota(jnp.int32, (8, 512), 0)
        even_b = jnp.sum(jnp.where(number == TC * col + 2 * sub, mask, 0.0), axis=1, keepdims=True)
        odd_b = jnp.sum(jnp.where(number == TC * col + 2 * sub + 1, mask, 0.0), axis=1, keepdims=True)
        mask_b = jnp.where(lane < 64, even_b, odd_b)
        place = lax.broadcasted_iota(jnp.int32, (1, CH), 1)
        place = place - jnp.where(place >= 64, 64, 0)
        a_of = 16 * (place // 16) + (place // 8) % 2 + 2 * (place % 8)
        pick = jnp.where(lax.broadcasted_iota(jnp.int32, (512, CH), 0) == TR * row + a_of, 1.0, 0.0).astype(BF16)
        mask_a = jnp.dot(jnp.broadcast_to(mask, (8, 512)).astype(BF16), pick, preferred_element_type=F32)
        masks[...] = mask_a * mask_b

    def spread_out(ref, layer, n):
        gains[layer, n] = jnp.broadcast_to(ref[layer : layer + 1, :], (CH, CH)).T

    def prepare(layer):
        turned = wp_ref[layer].astype(F32).T
        for b in range(16):
            rows = [turned[128 * q + 8 * b : 128 * q + 8 * b + 8] for q in range(4)]
            wpt[layer, b] = jnp.concatenate(rows, axis=0).astype(BF16)
        spread_out(gain_ref, layer, 0)
        spread_out(bias_ref, layer, 1)

    def prepare_out(layer):
        wgt[layer] = wg_ref[layer].astype(F32).T.astype(BF16)
        wot[layer] = wo_ref[layer].astype(F32).T.astype(BF16)
        spread_out(ogain_ref, layer, 2)
        spread_out(obias_ref, layer, 3)

    def twice(value):
        return jnp.concatenate([value, value], axis=1)

    def normalize(layer, t, values):
        center = values - jnp.mean(values, axis=0, keepdims=True)
        spread = jnp.mean(center * center, axis=0, keepdims=True)
        scaled = center * lax.rsqrt(spread + 1e-05) * twice(gains[layer, 0]) + twice(gains[layer, 1])
        normed[:, 256 * t : 256 * t + 256] = scaled.astype(BF16)
        cur[t] = values

    def send(src, dst, to_row, to_col, send_sem, recv_sem, here):
        def local():
            pltpu.make_async_copy(src, dst, recv_sem).start()

        def remote():
            pltpu.make_async_remote_copy(
                src_ref=src, dst_ref=dst, send_sem=send_sem, recv_sem=recv_sem,
                device_id=(to_row, to_col), device_id_type=MESH,
            ).start()

        if here is None:
            remote()
        else:
            pl.when(here)(local)
            pl.when(jnp.logical_not(here))(remote)

    def sent(buffer, sem, home):
        count = buffer.shape[0]

        @pl.when(home)
        def _():
            part = buffer.at[pl.ds(0, count - 1)]
            pltpu.make_async_copy(part, part, sem).wait()

        @pl.when(jnp.logical_not(home))
        def _():
            pltpu.make_async_copy(buffer, buffer, sem).wait()

    def arrived(buffer, sem):
        pltpu.make_async_copy(buffer, buffer, sem).wait()

    def scatter(layer):
        to_core = y_lo if layer == 0 else col // 16
        corner = y_hi * 2 + core
        slot = z * 16 + x * 4 + corner if layer == 0 else z_low * 32 + row * 4 + corner
        dst = (recv1 if layer == 0 else recv2).at[slot]
        lows = [y_lo, 1 - y_lo]
        highs = [y_hi, 1 - y_hi]
        sides = [z // 4, 1 - z // 4]

        @pl.loop(0, 8)
        def _(g):
            colour, step = g // 2, lax.rem(g, 2)
            depths = [lax.rem(z_low + 3 - step, 4), lax.rem(z_low + step, 4)]
            blocks = [colour * 4 + depth for depth in depths]
            weights = jnp.concatenate([wpt[layer, block] for block in blocks], axis=0)
            proj = jnp.dot(weights, normed[...], preferred_element_type=F32)
            left = jnp.concatenate([jax.nn.sigmoid(proj[n : n + 8]) * proj[n + 8 : n + 16] for n in (0, 32)], axis=0)
            right = jnp.concatenate([jax.nn.sigmoid(proj[n : n + 8]) * proj[n + 8 : n + 16] for n in (16, 48)], axis=0)
            for s in range(8):
                keep = masks[s : s + 1, :]
                stage[pl.ds(s, 16, stride=16), :] = left[:, CH * s : CH * s + CH] * keep
                stage[pl.ds(s + 8, 16, stride=16), :] = right[:, CH * s : CH * s + CH] * keep
            for n, block in enumerate(blocks):
                tile[pl.ds(block * 8, 8)] = stage[128 * n : 128 * n + 128, :].reshape(8, 16, CH).astype(BF16)
            columns = [lax.rem(colour + depth, 4) for depth in depths]
            for dz in (1, 0):
                for dh in (1, 0):
                    for dl in (1, 0):
                        for n in range(2):
                            here = None
                            if n == 1 and dz + dh + dl == 0:
                                here = jnp.logical_and(g == 2 * colour_here, to_core == core)
                            send(
                                tile.at[blocks[n] * 8 + sides[dz] * 4 + highs[dh] * 2 + lows[dl]], dst,
                                lows[dl] * 4 + columns[n], (sides[dz] * 4 + depths[n]) * 4 + highs[dh] * 2 + to_core,
                                send_sem.at[layer], in_sem.at[8 * layer + z], here,
                            )

        return to_core == core

    def make_gate(layer):
        for t in range(4):
            part = jnp.dot(wgt[layer], normed[:, 256 * t : 256 * t + 256], preferred_element_type=F32)
            gate[t] = jax.nn.sigmoid(part)

    def merge(first, second):
        low = lax.broadcasted_iota(jnp.int32, first.shape, 2) < 64
        even = jnp.where(low, first, pltpu.roll(second, 64, 2))
        odd = jnp.where(low, pltpu.roll(first, 64, 2), second)
        return even, odd

    def far_first(step, same):
        falling = (z_low < 2) == same
        return jnp.where(falling, 3 - step, step)

    def gather(layer):
        for step in range(8 if layer == 0 else 4):
            if layer == 0:
                recv, width, pairs = recv1, 16, 2
                place = lax.rem(z + (5, 1, 4, 0, 6, 2, 7, 3)[step], 8)
                sem = in_sem.at[place]
            else:
                recv, width, pairs = recv2, 32, 4
                place = lax.rem(z_low + (1, 0, 2, 3)[step], 4)
                sem = in_sem.at[8 + core * 4 + place]
            arrived(recv.at[pl.ds(place * width, width)], sem)
            rows = pl.ds(64 * step if layer == 0 else pl.multiple_of(place * 64, 64), 64)
            for p in range(pairs):
                first = recv[pl.ds(place * width + 8 * p, 4)].astype(F32)
                second = recv[pl.ds(place * width + 8 * p + 4, 4)].astype(F32)
                even, odd = merge(first, second)
                left = jnp.concatenate([even[:, :8], odd[:, :8]], axis=1).reshape(64, CH)
                right = jnp.concatenate([even[:, 8:], odd[:, 8:]], axis=1).reshape(64, CH)
                lanes = slice(128 * p, 128 * p + 128)
                if layer == 0:
                    mine_l[rows, lanes] = left.astype(BF16)
                    raw_r[rows, lanes] = right
                else:
                    mine_l2[rows, lanes] = left.astype(BF16)
                    mine_r[rows, lanes] = right.astype(BF16)
                if layer == 0 and step % 2 == 1:
                    block = slice(64 * step - 64, 64 * step + 64)
                    mine_r[lanes, block] = raw_r[block, lanes].T.astype(BF16)

    def quadrant(layer, q, right, dst):
        side = core if q == 0 else 1 - core
        lines = [lax.rem(x + n, 4) for n in range(4)]
        corners = [(y_hi if dy == 0 else 1 - y_hi) * 2 + (core if dc == 0 else 1 - core) for dy in range(2) for dc in range(2)]

        @pl.loop(0, 4)
        def _(step):
            depth = far_first(step, z // 4 == side)
            rows = right[pl.ds(pl.multiple_of(depth * 64, 64), 64), :]
            if layer == 0:
                mixed = jnp.dot(rows, mine_l[...], preferred_element_type=F32)
            else:
                mixed = lax.dot_general(rows, mine_l2[...], (((1,), (1,)), ((), ())), preferred_element_type=F32)
            base = q * 64 + depth * 16
            for p in range(2):
                block = mixed[:, 128 * p : 128 * p + 128].reshape(4, 16, CH)
                even, odd = merge(block[:, :8], block[:, 8:])
                outgoing[pl.ds(base + 8 * p, 4)] = even.astype(BF16)
                outgoing[pl.ds(base + 8 * p + 4, 4)] = odd.astype(BF16)
            for corner in (3, 2, 1, 0):
                for dx in (2, 1, 3, 0):
                    here = None
                    if corner == 0 and dx == 0:
                        here = jnp.logical_and(y_lo == core, side * 4 + depth == z)
                    send(
                        outgoing.at[base + lines[dx] * 4 + corners[corner]], dst,
                        core * 4 + lines[dx], (side * 4 + depth) * 4 + corners[corner],
                        ret_send.at[layer], ret_recv.at[2 * layer + colour_here // 2], here,
                    )

    def multiply(layer):
        back = (back1 if layer == 0 else back2).at[own]
        swap = swap1 if layer == 0 else swap2
        gather(layer)
        exchange = pltpu.make_async_remote_copy(
            src_ref=mine_r, dst_ref=swap, send_sem=swap_send.at[layer], recv_sem=swap_recv.at[layer],
            device_id=(row, sibling), device_id_type=MESH,
        )
        exchange.start()
        quadrant(layer, 0, mine_r, back)
        exchange.wait_recv()
        quadrant(layer, 1, swap, back)
        exchange.wait_send()

    def finish(layer):
        back = back1 if layer == 0 else back2
        halves = []
        for colour in range(2):
            arrived(back.at[pl.ds(64 * colour, 64)], ret_recv.at[2 * layer + colour])
            total = jnp.zeros((8, CH), F32)
            for g in range(4 * colour, 4 * colour + 4):
                part = back[16 * g : 16 * g + 16].astype(F32)
                wide[128 * g : 128 * g + 128, :] = part.reshape(128, CH)
                total = total + jnp.sum(part, axis=0)
            mean = total * (1.0 / 64)
            total = jnp.zeros((8, CH), F32)
            for g in range(4 * colour, 4 * colour + 4):
                part = wide[128 * g : 128 * g + 128, :].reshape(16, 8, CH) - mean[None]
                total = total + jnp.sum(part * part, axis=0)
            halves.append((mean, total))
        (mean0, total0), (mean1, total1) = halves
        apart = 0.5 * (mean0 - mean1)
        means[...] = 0.5 * (mean0 + mean1)
        rstds[...] = lax.rsqrt((total0 + total1) * (1.0 / CH) + apart * apart + 1e-05)

    def updated(layer, t):
        pair_of = [2 * t, 2 * t + 1]
        mixed = jnp.concatenate([wide[pl.ds(s, CH, stride=8), :] for s in pair_of], axis=1)
        mean = jnp.concatenate([means[s : s + 1, :] for s in pair_of], axis=1)
        rstd = jnp.concatenate([rstds[s : s + 1, :] for s in pair_of], axis=1)
        out_normed = (mixed - mean) * rstd * twice(gains[layer, 2]) + twice(gains[layer, 3])
        update = jnp.dot(wot[layer], out_normed.astype(BF16), preferred_element_type=F32)
        return cur[t] + gate[t] * update

    loads[1].wait()
    make_masks()
    for n in (2, 3, 4):
        loads[n].wait()
    prepare(0)
    second_hop()
    loads[0].wait()
    wide[...] = pair_ref[...].astype(F32).reshape(POS, CH)
    for t in range(4):
        rows = [
            wide[pl.ds(256 * g + 16 * e + 2 * s + b, 8, stride=32), :] for s in (2 * t, 2 * t + 1) for b, g, e in order
        ]
        normalize(0, t, jnp.concatenate(rows, axis=0).T)
    pl.semaphore_wait(hop_sem, COLS - 1)
    home1 = scatter(0)
    multiply(0)
    for n in (5, 6, 7, 8):
        loads[n].wait()
    prepare_out(0)
    make_gate(0)
    prepare(1)
    prepare_out(1)
    sent(tile, send_sem.at[0], home1)
    finish(0)
    for t in range(4):
        normalize(1, t, updated(0, t).astype(BF16).astype(F32))
    home2 = scatter(1)
    sent(outgoing, ret_send.at[0], home1)
    multiply(1)
    make_gate(1)
    sent(tile, send_sem.at[1], home2)
    finish(1)
    for t in range(4):
        values = updated(1, t).T
        for n, (s, (b, g, e)) in enumerate([(s, place) for s in (2 * t, 2 * t + 1) for place in order]):
            stage[pl.ds(256 * g + 16 * e + 2 * s + b, 8, stride=32), :] = values[8 * n : 8 * n + 8]
    out_ref[...] = stage[...].reshape(TR, TC, CH).astype(BF16)
    sent(outgoing, ret_send.at[1], home1)


def shards(pair, residue_mask, in_gain, in_bias, proj_weight, gate_weight, out_gain, out_bias, out_weight):
    arguments = (
        pair, residue_mask.reshape(1, 512), in_gain, in_bias, proj_weight, gate_weight, out_gain, out_bias, out_weight
    )
    dma = pltpu.SemaphoreType.DMA
    return pl.pallas_call(
        kernel,
        out_shape=pltpu.VMEM((TR, TC, CH), BF16),
        in_specs=[pl.BlockSpec(memory_space=pltpu.HBM)] * 9,
        out_specs=pl.BlockSpec(memory_space=pltpu.VMEM),
        scratch_shapes=[pltpu.VMEM(value.shape, value.dtype) for value in arguments] + [
            pltpu.VMEM((POS, CH), F32),
            pltpu.VMEM((4, CH, 256), F32),
            pltpu.VMEM((4, CH, 256), F32),
            pltpu.VMEM((POS, CH), F32),
            pltpu.VMEM((8, CH), F32),
            pltpu.VMEM((8, CH), F32),
            pltpu.VMEM((8, CH), F32),
            pltpu.VMEM((CH, POS), BF16),
            pltpu.VMEM((2, 16, 32, CH), BF16),
            pltpu.VMEM((2, CH, CH), BF16),
            pltpu.VMEM((2, CH, CH), BF16),
            pltpu.VMEM((2, 4, CH, CH), F32),
            pltpu.VMEM((CH, 16, CH), BF16),
            pltpu.VMEM((CH, 16, CH), BF16),
            pltpu.VMEM((CH, 16, CH), BF16),
            pltpu.VMEM((CH, 8, CH), BF16),
            pltpu.VMEM((CH, 8, CH), BF16),
            pltpu.VMEM((256, 512), BF16),
            pltpu.VMEM((256, 512), BF16),
            pltpu.VMEM((256, 512), BF16),
            pltpu.VMEM((512, 256), BF16),
            pltpu.VMEM((256, 512), BF16),
            pltpu.VMEM((512, 256), F32),
            pltpu.VMEM((CH, 8, CH), BF16),
            dma((9,)),
            pltpu.SemaphoreType.REGULAR,
            dma((2,)), dma((16,)), dma((2,)), dma((2,)), dma((2,)), dma((4,)),
        ],
        compiler_params=pltpu.CompilerParams(
            collective_id=0, has_side_effects=True, vmem_limit_bytes=48 * 1024 * 1024
        ),
        cost_estimate=pl.CostEstimate(flops=700_000_000, bytes_accessed=4_000_000, transcendentals=1_000_000),
    )(*[pltpu.with_memory_space_constraint(value, pltpu.HBM) for value in arguments])


def solution(mesh):
    placed = (P("row", "col", None), P(), P(), P(), P(), P(), P(), P(), P())
    return jax.shard_map(
        shards, mesh=mesh, in_specs=placed, out_specs=P("row", "col", None), check_vma=False
    )
```

```python
import jax
import jax.numpy as jnp
from jax import lax
from jax.experimental import pallas as pl
from jax.experimental.pallas import tpu as pltpu
from jax.sharding import PartitionSpec as P

MESH = pl.DeviceIdType.MESH
F32 = jnp.float32
BF16 = jnp.bfloat16
ROWS, COLS = 8, 32
TR, TC = 64, 16
CH = 128
POS = TR * TC


def kernel(
    pair_hbm, mask_hbm, gain_hbm, bias_hbm, wp_hbm, wg_hbm, ogain_hbm, obias_hbm, wo_hbm,
    out_ref,
    pair_ref, mask_in, gain_ref, bias_ref, wp_ref, wg_ref, ogain_ref, obias_ref, wo_ref,
    wide, cur, gate, stage, masks, means, rstds, normed, wpt, wgt, wot, gains,
    tile, recv1, recv2, back1, back2, swap1, swap2, mine_r, mine_l, mine_l2, raw_r, outgoing,
    load_sem, hop_sem, send_sem, in_sem, swap_send, swap_recv, ret_send, ret_recv,
):
    row = lax.axis_index("row")
    col = lax.axis_index("col")
    core = lax.rem(col, 2)
    sibling = col + 1 - 2 * core
    x, y_lo = lax.rem(row, 4), row // 4
    z, y_hi = col // 4, lax.rem(col // 2, 2)

    z_low = lax.rem(z, 4)
    colour_here = lax.rem(x + 4 - z_low, 4)
    own = (colour_here * 4 + z_low) * 8 + z // 4 * 4 + y_hi * 2 + y_lo

    loads = [
        pltpu.make_async_copy(src, dst, load_sem.at[n])
        for n, (src, dst) in enumerate([
            (pair_hbm, pair_ref), (mask_hbm, mask_in), (gain_hbm, gain_ref), (bias_hbm, bias_ref), (wp_hbm, wp_ref),
            (wg_hbm, wg_ref), (ogain_hbm, ogain_ref), (obias_hbm, obias_ref), (wo_hbm, wo_ref),
        ])
    ]
    for load in loads:
        load.start()

    barrier = pltpu.get_barrier_semaphore()

    @pl.loop(1, ROWS)
    def _(d):
        pl.semaphore_signal(barrier, inc=1, device_id=(lax.rem(row + d, ROWS), col), device_id_type=MESH)

    @pl.loop(1, COLS)
    def _(d):
        pl.semaphore_signal(barrier, inc=1, device_id=(row, lax.rem(col + d, COLS)), device_id_type=MESH)

    def second_hop():
        pl.semaphore_wait(barrier, ROWS - 1 + COLS - 1)

        @pl.loop(1, COLS)
        def _(d):
            pl.semaphore_signal(hop_sem, inc=1, device_id=(row, lax.rem(col + d, COLS)), device_id_type=MESH)

    order = [(b, g, e) for b in range(2) for g in range(4) for e in range(2)]

    def make_masks():
        lane = lax.broadcasted_iota(jnp.int32, (8, CH), 1)
        mask = mask_in[...].astype(F32)
        number = lax.broadcasted_iota(jnp.int32, (8, 512), 1)
        sub = lax.broadcasted_iota(jnp.int32, (8, 512), 0)
        even_b = jnp.sum(jnp.where(number == TC * col + 2 * sub, mask, 0.0), axis=1, keepdims=True)
        odd_b = jnp.sum(jnp.where(number == TC * col + 2 * sub + 1, mask, 0.0), axis=1, keepdims=True)
        mask_b = jnp.where(lane < 64, even_b, odd_b)
        place = lax.broadcasted_iota(jnp.int32, (1, CH), 1)
        place = place - jnp.where(place >= 64, 64, 0)
        a_of = 16 * (place // 16) + (place // 8) % 2 + 2 * (place % 8)
        pick = jnp.where(lax.broadcasted_iota(jnp.int32, (512, CH), 0) == TR * row + a_of, 1.0, 0.0).astype(BF16)
        mask_a = jnp.dot(jnp.broadcast_to(mask, (8, 512)).astype(BF16), pick, preferred_element_type=F32)
        masks[...] = mask_a * mask_b

    def spread_out(ref, layer, n):
        gains[layer, n] = jnp.broadcast_to(ref[layer : layer + 1, :], (CH, CH)).T

    def prepare(layer):
        turned = wp_ref[layer].astype(F32).T
        for b in range(16):
            rows = [turned[128 * q + 8 * b : 128 * q + 8 * b + 8] for q in range(4)]
            wpt[layer, b] = jnp.concatenate(rows, axis=0).astype(BF16)
        spread_out(gain_ref, layer, 0)
        spread_out(bias_ref, layer, 1)

    def prepare_out(layer):
        wgt[layer] = wg_ref[layer].astype(F32).T.astype(BF16)
        wot[layer] = wo_ref[layer].astype(F32).T.astype(BF16)
        spread_out(ogain_ref, layer, 2)
        spread_out(obias_ref, layer, 3)

    def twice(value):
        return jnp.concatenate([value, value], axis=1)

    def normalize(layer, t, values):
        center = values - jnp.mean(values, axis=0, keepdims=True)
        spread = jnp.mean(center * center, axis=0, keepdims=True)
        scaled = center * lax.rsqrt(spread + 1e-05) * twice(gains[layer, 0]) + twice(gains[layer, 1])
        normed[:, 256 * t : 256 * t + 256] = scaled.astype(BF16)
        cur[t] = values

    def send(src, dst, to_row, to_col, send_sem, recv_sem, here):
        def local():
            pltpu.make_async_copy(src, dst, recv_sem).start()

        def remote():
            pltpu.make_async_remote_copy(
                src_ref=src, dst_ref=dst, send_sem=send_sem, recv_sem=recv_sem,
                device_id=(to_row, to_col), device_id_type=MESH,
            ).start()

        if here is None:
            remote()
        else:
            pl.when(here)(local)
            pl.when(jnp.logical_not(here))(remote)

    def sent(buffer, sem, home):
        count = buffer.shape[0]

        @pl.when(home)
        def _():
            part = buffer.at[pl.ds(0, count - 1)]
            pltpu.make_async_copy(part, part, sem).wait()

        @pl.when(jnp.logical_not(home))
        def _():
            pltpu.make_async_copy(buffer, buffer, sem).wait()

    def arrived(buffer, sem):
        pltpu.make_async_copy(buffer, buffer, sem).wait()

    def scatter(layer):
        to_core = y_lo if layer == 0 else col // 16
        corner = y_hi * 2 + core
        slot = z * 16 + x * 4 + corner if layer == 0 else z_low * 32 + row * 4 + corner
        dst = (recv1 if layer == 0 else recv2).at[slot]
        lows = [y_lo, 1 - y_lo]
        highs = [y_hi, 1 - y_hi]
        sides = [z // 4, 1 - z // 4]

        @pl.loop(0, 4)
        def _(colour):
            depths = [lax.rem(z_low + d, 4) for d in (3, 0, 2, 1)]
            blocks = [colour * 4 + depth for depth in depths]
            weights = jnp.concatenate([wpt[layer, block] for block in blocks], axis=0)
            proj = jnp.dot(weights, normed[...], preferred_element_type=F32)
            for n, block in enumerate(blocks):
                part = proj[32 * n : 32 * n + 32]
                left = jax.nn.sigmoid(part[0:8]) * part[8:16]
                right = jax.nn.sigmoid(part[16:24]) * part[24:32]
                for s in range(8):
                    keep = masks[s : s + 1, :]
                    stage[pl.ds(128 * n + s, 8, stride=16), :] = left[:, CH * s : CH * s + CH] * keep
                    stage[pl.ds(128 * n + s + 8, 8, stride=16), :] = right[:, CH * s : CH * s + CH] * keep
                tile[pl.ds(block * 8, 8)] = stage[128 * n : 128 * n + 128, :].reshape(8, 16, CH).astype(BF16)
            columns = [lax.rem(colour + depth, 4) for depth in depths]
            for n in range(4):
                for dz in (1, 0):
                    for dh in (1, 0):
                        for dl in (1, 0):
                            here = None
                            if n == 1 and dz + dh + dl == 0:
                                here = jnp.logical_and(colour == colour_here, to_core == core)
                            send(
                                tile.at[blocks[n] * 8 + sides[dz] * 4 + highs[dh] * 2 + lows[dl]], dst,
                                lows[dl] * 4 + columns[n], (sides[dz] * 4 + depths[n]) * 4 + highs[dh] * 2 + to_core,
                                send_sem.at[layer], in_sem.at[8 * layer + z], here,
                            )

        return to_core == core

    def make_gate(layer):
        for t in range(4):
            part = jnp.dot(wgt[layer], normed[:, 256 * t : 256 * t + 256], preferred_element_type=F32)
            gate[t] = jax.nn.sigmoid(part)

    def merge(first, second):
        low = lax.broadcasted_iota(jnp.int32, first.shape, 2) < 64
        even = jnp.where(low, first, pltpu.roll(second, 64, 2))
        odd = jnp.where(low, pltpu.roll(first, 64, 2), second)
        return even, odd

    def far_first(step, same):
        falling = (z_low < 2) == same
        return jnp.where(falling, 3 - step, step)

    def gather(layer):
        for step in range(8 if layer == 0 else 4):
            if layer == 0:
                recv, width, pairs = recv1, 16, 2
                place = lax.rem(z + (5, 1, 4, 0, 6, 2, 7, 3)[step], 8)
                sem = in_sem.at[place]
            else:
                recv, width, pairs = recv2, 32, 4
                place = lax.rem(z_low + (1, 0, 2, 3)[step], 4)
                sem = in_sem.at[8 + core * 4 + place]
            arrived(recv.at[pl.ds(place * width, width)], sem)
            rows = pl.ds(64 * step if layer == 0 else pl.multiple_of(place * 64, 64), 64)
            for p in range(pairs):
                first = recv[pl.ds(place * width + 8 * p, 4)].astype(F32)
                second = recv[pl.ds(place * width + 8 * p + 4, 4)].astype(F32)
                even, odd = merge(first, second)
                left = jnp.concatenate([even[:, :8], odd[:, :8]], axis=1).reshape(64, CH)
                right = jnp.concatenate([even[:, 8:], odd[:, 8:]], axis=1).reshape(64, CH)
                lanes = slice(128 * p, 128 * p + 128)
                if layer == 0:
                    mine_l[rows, lanes] = left.astype(BF16)
                    raw_r[rows, lanes] = right
                else:
                    mine_l2[rows, lanes] = left.astype(BF16)
                    mine_r[rows, lanes] = right.astype(BF16)
                if layer == 0 and step % 2 == 1:
                    block = slice(64 * step - 64, 64 * step + 64)
                    mine_r[lanes, block] = raw_r[block, lanes].T.astype(BF16)

    def quadrant(layer, q, right, dst):
        side = core if q == 0 else 1 - core
        lines = [lax.rem(x + n, 4) for n in range(4)]
        corners = [(y_hi if dy == 0 else 1 - y_hi) * 2 + (core if dc == 0 else 1 - core) for dy in range(2) for dc in range(2)]

        @pl.loop(0, 4)
        def _(step):
            depth = far_first(step, z // 4 == side)
            rows = right[pl.ds(pl.multiple_of(depth * 64, 64), 64), :]
            if layer == 0:
                mixed = jnp.dot(rows, mine_l[...], preferred_element_type=F32)
            else:
                mixed = lax.dot_general(rows, mine_l2[...], (((1,), (1,)), ((), ())), preferred_element_type=F32)
            base = q * 64 + depth * 16
            for p in range(2):
                block = mixed[:, 128 * p : 128 * p + 128].reshape(4, 16, CH)
                even, odd = merge(block[:, :8], block[:, 8:])
                outgoing[pl.ds(base + 8 * p, 4)] = even.astype(BF16)
                outgoing[pl.ds(base + 8 * p + 4, 4)] = odd.astype(BF16)
            for corner in (3, 2, 1, 0):
                for dx in (2, 1, 3, 0):
                    here = None
                    if corner == 0 and dx == 0:
                        here = jnp.logical_and(y_lo == core, side * 4 + depth == z)
                    send(
                        outgoing.at[base + lines[dx] * 4 + corners[corner]], dst,
                        core * 4 + lines[dx], (side * 4 + depth) * 4 + corners[corner],
                        ret_send.at[layer], ret_recv.at[2 * layer + colour_here // 2], here,
                    )

    def multiply(layer):
        back = (back1 if layer == 0 else back2).at[own]
        swap = swap1 if layer == 0 else swap2
        gather(layer)
        exchange = pltpu.make_async_remote_copy(
            src_ref=mine_r, dst_ref=swap, send_sem=swap_send.at[layer], recv_sem=swap_recv.at[layer],
            device_id=(row, sibling), device_id_type=MESH,
        )
        exchange.start()
        quadrant(layer, 0, mine_r, back)
        exchange.wait_recv()
        quadrant(layer, 1, swap, back)
        exchange.wait_send()

    def finish(layer):
        back = back1 if layer == 0 else back2
        halves = []
        for colour in range(2):
            arrived(back.at[pl.ds(64 * colour, 64)], ret_recv.at[2 * layer + colour])
            total = jnp.zeros((8, CH), F32)
            for g in range(4 * colour, 4 * colour + 4):
                part = back[16 * g : 16 * g + 16].astype(F32)
                wide[128 * g : 128 * g + 128, :] = part.reshape(128, CH)
                total = total + jnp.sum(part, axis=0)
            mean = total * (1.0 / 64)
            total = jnp.zeros((8, CH), F32)
            for g in range(4 * colour, 4 * colour + 4):
                part = wide[128 * g : 128 * g + 128, :].reshape(16, 8, CH) - mean[None]
                total = total + jnp.sum(part * part, axis=0)
            halves.append((mean, total))
        (mean0, total0), (mean1, total1) = halves
        apart = 0.5 * (mean0 - mean1)
        means[...] = 0.5 * (mean0 + mean1)
        rstds[...] = lax.rsqrt((total0 + total1) * (1.0 / CH) + apart * apart + 1e-05)

    def updated(layer, t):
        pair_of = [2 * t, 2 * t + 1]
        mixed = jnp.concatenate([wide[pl.ds(s, CH, stride=8), :] for s in pair_of], axis=1)
        mean = jnp.concatenate([means[s : s + 1, :] for s in pair_of], axis=1)
        rstd = jnp.concatenate([rstds[s : s + 1, :] for s in pair_of], axis=1)
        out_normed = (mixed - mean) * rstd * twice(gains[layer, 2]) + twice(gains[layer, 3])
        update = jnp.dot(wot[layer], out_normed.astype(BF16), preferred_element_type=F32)
        return cur[t] + gate[t] * update

    loads[1].wait()
    make_masks()
    for n in (2, 3, 4):
        loads[n].wait()
    prepare(0)
    second_hop()
    loads[0].wait()
    wide[...] = pair_ref[...].astype(F32).reshape(POS, CH)
    for t in range(4):
        rows = [
            wide[pl.ds(256 * g + 16 * e + 2 * s + b, 8, stride=32), :] for s in (2 * t, 2 * t + 1) for b, g, e in order
        ]
        normalize(0, t, jnp.concatenate(rows, axis=0).T)
    pl.semaphore_wait(hop_sem, COLS - 1)
    home1 = scatter(0)
    multiply(0)
    for n in (5, 6, 7, 8):
        loads[n].wait()
    prepare_out(0)
    make_gate(0)
    prepare(1)
    prepare_out(1)
    sent(tile, send_sem.at[0], home1)
    finish(0)
    for t in range(4):
        normalize(1, t, updated(0, t).astype(BF16).astype(F32))
    home2 = scatter(1)
    sent(outgoing, ret_send.at[0], home1)
    multiply(1)
    make_gate(1)
    sent(tile, send_sem.at[1], home2)
    finish(1)
    for t in range(4):
        values = updated(1, t).T
        for n, (s, (b, g, e)) in enumerate([(s, place) for s in (2 * t, 2 * t + 1) for place in order]):
            stage[pl.ds(256 * g + 16 * e + 2 * s + b, 8, stride=32), :] = values[8 * n : 8 * n + 8]
    out_ref[...] = stage[...].reshape(TR, TC, CH).astype(BF16)
    sent(outgoing, ret_send.at[1], home1)


def shards(pair, residue_mask, in_gain, in_bias, proj_weight, gate_weight, out_gain, out_bias, out_weight):
    arguments = (
        pair, residue_mask.reshape(1, 512), in_gain, in_bias, proj_weight, gate_weight, out_gain, out_bias, out_weight
    )
    dma = pltpu.SemaphoreType.DMA
    return pl.pallas_call(
        kernel,
        out_shape=pltpu.VMEM((TR, TC, CH), BF16),
        in_specs=[pl.BlockSpec(memory_space=pltpu.HBM)] * 9,
        out_specs=pl.BlockSpec(memory_space=pltpu.VMEM),
        scratch_shapes=[pltpu.VMEM(value.shape, value.dtype) for value in arguments] + [
            pltpu.VMEM((POS, CH), F32),
            pltpu.VMEM((4, CH, 256), F32),
            pltpu.VMEM((4, CH, 256), F32),
            pltpu.VMEM((POS, CH), F32),
            pltpu.VMEM((8, CH), F32),
            pltpu.VMEM((8, CH), F32),
            pltpu.VMEM((8, CH), F32),
            pltpu.VMEM((CH, POS), BF16),
            pltpu.VMEM((2, 16, 32, CH), BF16),
            pltpu.VMEM((2, CH, CH), BF16),
            pltpu.VMEM((2, CH, CH), BF16),
            pltpu.VMEM((2, 4, CH, CH), F32),
            pltpu.VMEM((CH, 16, CH), BF16),
            pltpu.VMEM((CH, 16, CH), BF16),
            pltpu.VMEM((CH, 16, CH), BF16),
            pltpu.VMEM((CH, 8, CH), BF16),
            pltpu.VMEM((CH, 8, CH), BF16),
            pltpu.VMEM((256, 512), BF16),
            pltpu.VMEM((256, 512), BF16),
            pltpu.VMEM((256, 512), BF16),
            pltpu.VMEM((512, 256), BF16),
            pltpu.VMEM((256, 512), BF16),
            pltpu.VMEM((512, 256), F32),
            pltpu.VMEM((CH, 8, CH), BF16),
            dma((9,)),
            pltpu.SemaphoreType.REGULAR,
            dma((2,)), dma((16,)), dma((2,)), dma((2,)), dma((2,)), dma((4,)),
        ],
        compiler_params=pltpu.CompilerParams(
            collective_id=0, has_side_effects=True, vmem_limit_bytes=48 * 1024 * 1024
        ),
        cost_estimate=pl.CostEstimate(flops=700_000_000, bytes_accessed=4_000_000, transcendentals=1_000_000),
    )(*[pltpu.with_memory_space_constraint(value, pltpu.HBM) for value in arguments])


def solution(mesh):
    placed = (P("row", "col", None), P(), P(), P(), P(), P(), P(), P(), P())
    return jax.shard_map(
        shards, mesh=mesh, in_specs=placed, out_specs=P("row", "col", None), check_vma=False
    )
```

```python
import jax
import jax.numpy as jnp
from jax import lax
from jax.experimental import pallas as pl
from jax.experimental.pallas import tpu as pltpu
from jax.sharding import PartitionSpec as P

MESH = pl.DeviceIdType.MESH
F32 = jnp.float32
BF16 = jnp.bfloat16
ROWS, COLS = 8, 32
TR, TC = 64, 16
CH = 128
POS = TR * TC


def sigmoid(values):
    return 0.5 * jnp.tanh(0.5 * values) + 0.5


def kernel(
    pair_hbm, mask_hbm, gain_hbm, bias_hbm, wp_hbm, wg_hbm, ogain_hbm, obias_hbm, wo_hbm,
    out_ref,
    pair_ref, mask_in, gain_ref, bias_ref, wp_ref, wg_ref, ogain_ref, obias_ref, wo_ref,
    wide, cur, gate, stage, masks, means, rstds, normed, wpt, proj_all, wgt, wot, gains,
    tile, recv1, recv2, back1, back2, swap1, swap2, mine_r, mine_l, mine_l2, raw_r, outgoing,
    load_sem, hop_sem, send_sem, in_sem, swap_send, swap_recv, ret_send, ret_recv,
):
    row = lax.axis_index("row")
    col = lax.axis_index("col")
    core = lax.rem(col, 2)
    sibling = col + 1 - 2 * core
    x, y_lo = lax.rem(row, 4), row // 4
    z, y_hi = col // 4, lax.rem(col // 2, 2)

    z_low = lax.rem(z, 4)
    colour_here = lax.rem(x + 4 - z_low, 4)
    own = (colour_here * 4 + z_low) * 8 + z // 4 * 4 + y_hi * 2 + y_lo

    loads = [
        pltpu.make_async_copy(src, dst, load_sem.at[n])
        for n, (src, dst) in enumerate([
            (pair_hbm, pair_ref), (mask_hbm, mask_in), (gain_hbm, gain_ref), (bias_hbm, bias_ref), (wp_hbm, wp_ref),
            (wg_hbm, wg_ref), (ogain_hbm, ogain_ref), (obias_hbm, obias_ref), (wo_hbm, wo_ref),
        ])
    ]
    for load in loads:
        load.start()

    barrier = pltpu.get_barrier_semaphore()

    @pl.loop(1, ROWS)
    def _(d):
        pl.semaphore_signal(barrier, inc=1, device_id=(lax.rem(row + d, ROWS), col), device_id_type=MESH)

    @pl.loop(1, COLS)
    def _(d):
        pl.semaphore_signal(barrier, inc=1, device_id=(row, lax.rem(col + d, COLS)), device_id_type=MESH)

    def second_hop():
        pl.semaphore_wait(barrier, ROWS - 1 + COLS - 1)

        @pl.loop(1, COLS)
        def _(d):
            pl.semaphore_signal(hop_sem, inc=1, device_id=(row, lax.rem(col + d, COLS)), device_id_type=MESH)

    order = [(b, g, e) for b in range(2) for g in range(4) for e in range(2)]

    def make_masks():
        lane = lax.broadcasted_iota(jnp.int32, (8, CH), 1)
        mask = mask_in[...].astype(F32)
        number = lax.broadcasted_iota(jnp.int32, (8, 512), 1)
        sub = lax.broadcasted_iota(jnp.int32, (8, 512), 0)
        even_b = jnp.sum(jnp.where(number == TC * col + 2 * sub, mask, 0.0), axis=1, keepdims=True)
        odd_b = jnp.sum(jnp.where(number == TC * col + 2 * sub + 1, mask, 0.0), axis=1, keepdims=True)
        mask_b = jnp.where(lane < 64, even_b, odd_b)
        place = lax.broadcasted_iota(jnp.int32, (1, CH), 1)
        place = place - jnp.where(place >= 64, 64, 0)
        a_of = 16 * (place // 16) + (place // 8) % 2 + 2 * (place % 8)
        pick = jnp.where(lax.broadcasted_iota(jnp.int32, (512, CH), 0) == TR * row + a_of, 1.0, 0.0).astype(BF16)
        mask_a = jnp.dot(jnp.broadcast_to(mask, (8, 512)).astype(BF16), pick, preferred_element_type=F32)
        masks[...] = mask_a * mask_b

    def spread_out(ref, layer, n):
        gains[layer, n] = jnp.broadcast_to(ref[layer : layer + 1, :], (CH, CH)).T

    def prepare(layer):
        turned = wp_ref[layer].astype(F32).T
        for b in range(16):
            rows = [turned[128 * q + 8 * b : 128 * q + 8 * b + 8] for q in range(4)]
            wpt[layer, 32 * b : 32 * b + 32] = jnp.concatenate(rows, axis=0).astype(BF16)
        spread_out(gain_ref, layer, 0)
        spread_out(bias_ref, layer, 1)

    def prepare_out(layer):
        wgt[layer] = wg_ref[layer].astype(F32).T.astype(BF16)
        wot[layer] = wo_ref[layer].astype(F32).T.astype(BF16)
        spread_out(ogain_ref, layer, 2)
        spread_out(obias_ref, layer, 3)

    def twice(value):
        return jnp.concatenate([value, value], axis=1)

    def normalize(layer, t, values):
        center = values - jnp.mean(values, axis=0, keepdims=True)
        spread = jnp.mean(center * center, axis=0, keepdims=True)
        scaled = center * lax.rsqrt(spread + 1e-05) * twice(gains[layer, 0]) + twice(gains[layer, 1])
        part = scaled.astype(BF16)
        normed[:, 256 * t : 256 * t + 256] = part
        proj_all[:, 256 * t : 256 * t + 256] = jnp.dot(wpt[layer], part, preferred_element_type=F32)
        cur[t] = values

    def send(src, dst, to_row, to_col, send_sem, recv_sem, here):
        def local():
            pltpu.make_async_copy(src, dst, recv_sem).start()

        def remote():
            pltpu.make_async_remote_copy(
                src_ref=src, dst_ref=dst, send_sem=send_sem, recv_sem=recv_sem,
                device_id=(to_row, to_col), device_id_type=MESH,
            ).start()

        if here is None:
            remote()
        else:
            pl.when(here)(local)
            pl.when(jnp.logical_not(here))(remote)

    def sent(buffer, sem, home):
        count = buffer.shape[0]

        @pl.when(home)
        def _():
            part = buffer.at[pl.ds(0, count - 1)]
            pltpu.make_async_copy(part, part, sem).wait()

        @pl.when(jnp.logical_not(home))
        def _():
            pltpu.make_async_copy(buffer, buffer, sem).wait()

    def arrived(buffer, sem):
        pltpu.make_async_copy(buffer, buffer, sem).wait()

    def scatter(layer):
        to_core = y_lo if layer == 0 else col // 16
        corner = y_hi * 2 + core
        slot = z * 16 + x * 4 + corner if layer == 0 else z_low * 32 + row * 4 + corner
        dst = (recv1 if layer == 0 else recv2).at[slot]
        lows = [y_lo, 1 - y_lo]
        highs = [y_hi, 1 - y_hi]
        sides = [z // 4, 1 - z // 4]

        @pl.loop(0, 8)
        def _(g):
            colour, step = g // 2, lax.rem(g, 2)
            depths = [lax.rem(z_low + 3 - step, 4), lax.rem(z_low + step, 4)]
            blocks = [colour * 4 + depth for depth in depths]
            for n, block in enumerate(blocks):
                for s in range(8):
                    part = proj_all[pl.ds(pl.multiple_of(block * 32, 32), 32), CH * s : CH * s + CH]
                    keep = masks[s : s + 1, :]
                    stage[pl.ds(128 * n + s, 8, stride=16), :] = sigmoid(part[0:8]) * part[8:16] * keep
                    stage[pl.ds(128 * n + s + 8, 8, stride=16), :] = sigmoid(part[16:24]) * part[24:32] * keep
                tile[pl.ds(block * 8, 8)] = stage[128 * n : 128 * n + 128, :].reshape(8, 16, CH).astype(BF16)
            columns = [lax.rem(colour + depth, 4) for depth in depths]
            for dz in (1, 0):
                for dh in (1, 0):
                    for dl in (1, 0):
                        for n in range(2):
                            here = None
                            if n == 1 and dz + dh + dl == 0:
                                here = jnp.logical_and(g == 2 * colour_here, to_core == core)
                            send(
                                tile.at[blocks[n] * 8 + sides[dz] * 4 + highs[dh] * 2 + lows[dl]], dst,
                                lows[dl] * 4 + columns[n], (sides[dz] * 4 + depths[n]) * 4 + highs[dh] * 2 + to_core,
                                send_sem.at[layer], in_sem.at[8 * layer + z], here,
                            )

        return to_core == core

    def make_gate(layer):
        for t in range(4):
            part = jnp.dot(wgt[layer], normed[:, 256 * t : 256 * t + 256], preferred_element_type=F32)
            gate[t] = sigmoid(part)

    def merge(first, second):
        low = lax.broadcasted_iota(jnp.int32, first.shape, 2) < 64
        even = jnp.where(low, first, pltpu.roll(second, 64, 2))
        odd = jnp.where(low, pltpu.roll(first, 64, 2), second)
        return even, odd

    def far_first(step, same):
        falling = (z_low < 2) == same
        return jnp.where(falling, 3 - step, step)

    def gather(layer):
        for step in range(8 if layer == 0 else 4):
            if layer == 0:
                recv, width, pairs = recv1, 16, 2
                place = lax.rem(z + (5, 1, 4, 0, 6, 2, 7, 3)[step], 8)
                sem = in_sem.at[place]
            else:
                recv, width, pairs = recv2, 32, 4
                place = lax.rem(z_low + (1, 0, 2, 3)[step], 4)
                sem = in_sem.at[8 + core * 4 + place]
            arrived(recv.at[pl.ds(place * width, width)], sem)
            rows = pl.ds(64 * step if layer == 0 else pl.multiple_of(place * 64, 64), 64)
            for p in range(pairs):
                first = recv[pl.ds(place * width + 8 * p, 4)].astype(F32)
                second = recv[pl.ds(place * width + 8 * p + 4, 4)].astype(F32)
                even, odd = merge(first, second)
                left = jnp.concatenate([even[:, :8], odd[:, :8]], axis=1).reshape(64, CH)
                right = jnp.concatenate([even[:, 8:], odd[:, 8:]], axis=1).reshape(64, CH)
                lanes = slice(128 * p, 128 * p + 128)
                if layer == 0:
                    mine_l[rows, lanes] = left.astype(BF16)
                    raw_r[rows, lanes] = right
                else:
                    mine_l2[rows, lanes] = left.astype(BF16)
                    mine_r[rows, lanes] = right.astype(BF16)
                if layer == 0 and step % 2 == 1:
                    block = slice(64 * step - 64, 64 * step + 64)
                    mine_r[lanes, block] = raw_r[block, lanes].T.astype(BF16)

    def quadrant(layer, q, right, dst):
        side = core if q == 0 else 1 - core
        lines = [lax.rem(x + n, 4) for n in range(4)]
        corners = [(y_hi if dy == 0 else 1 - y_hi) * 2 + (core if dc == 0 else 1 - core) for dy in range(2) for dc in range(2)]

        @pl.loop(0, 4)
        def _(step):
            depth = far_first(step, z // 4 == side)
            rows = right[pl.ds(pl.multiple_of(depth * 64, 64), 64), :]
            if layer == 0:
                mixed = jnp.dot(rows, mine_l[...], preferred_element_type=F32)
            else:
                mixed = lax.dot_general(rows, mine_l2[...], (((1,), (1,)), ((), ())), preferred_element_type=F32)
            base = q * 64 + depth * 16
            for p in range(2):
                block = mixed[:, 128 * p : 128 * p + 128].reshape(4, 16, CH)
                even, odd = merge(block[:, :8], block[:, 8:])
                outgoing[pl.ds(base + 8 * p, 4)] = even.astype(BF16)
                outgoing[pl.ds(base + 8 * p + 4, 4)] = odd.astype(BF16)
            for corner in (3, 2, 1, 0):
                for dx in (2, 1, 3, 0):
                    here = None
                    if corner == 0 and dx == 0:
                        here = jnp.logical_and(y_lo == core, side * 4 + depth == z)
                    send(
                        outgoing.at[base + lines[dx] * 4 + corners[corner]], dst,
                        core * 4 + lines[dx], (side * 4 + depth) * 4 + corners[corner],
                        ret_send.at[layer], ret_recv.at[2 * layer + colour_here // 2], here,
                    )

    def multiply(layer):
        back = (back1 if layer == 0 else back2).at[own]
        swap = swap1 if layer == 0 else swap2
        gather(layer)
        exchange = pltpu.make_async_remote_copy(
            src_ref=mine_r, dst_ref=swap, send_sem=swap_send.at[layer], recv_sem=swap_recv.at[layer],
            device_id=(row, sibling), device_id_type=MESH,
        )
        exchange.start()
        quadrant(layer, 0, mine_r, back)
        exchange.wait_recv()
        quadrant(layer, 1, swap, back)
        exchange.wait_send()

    def finish(layer):
        back = back1 if layer == 0 else back2
        halves = []
        for colour in range(2):
            arrived(back.at[pl.ds(64 * colour, 64)], ret_recv.at[2 * layer + colour])
            total = jnp.zeros((8, CH), F32)
            for g in range(4 * colour, 4 * colour + 4):
                part = back[16 * g : 16 * g + 16].astype(F32)
                wide[128 * g : 128 * g + 128, :] = part.reshape(128, CH)
                total = total + jnp.sum(part, axis=0)
            mean = total * (1.0 / 64)
            total = jnp.zeros((8, CH), F32)
            for g in range(4 * colour, 4 * colour + 4):
                part = wide[128 * g : 128 * g + 128, :].reshape(16, 8, CH) - mean[None]
                total = total + jnp.sum(part * part, axis=0)
            halves.append((mean, total))
        (mean0, total0), (mean1, total1) = halves
        apart = 0.5 * (mean0 - mean1)
        means[...] = 0.5 * (mean0 + mean1)
        rstds[...] = lax.rsqrt((total0 + total1) * (1.0 / CH) + apart * apart + 1e-05)

    def updated(layer, t):
        pair_of = [2 * t, 2 * t + 1]
        mixed = jnp.concatenate([wide[pl.ds(s, CH, stride=8), :] for s in pair_of], axis=1)
        mean = jnp.concatenate([means[s : s + 1, :] for s in pair_of], axis=1)
        rstd = jnp.concatenate([rstds[s : s + 1, :] for s in pair_of], axis=1)
        out_normed = (mixed - mean) * rstd * twice(gains[layer, 2]) + twice(gains[layer, 3])
        update = jnp.dot(wot[layer], out_normed.astype(BF16), preferred_element_type=F32)
        return cur[t] + gate[t] * update

    loads[1].wait()
    make_masks()
    for n in (2, 3, 4):
        loads[n].wait()
    prepare(0)
    second_hop()
    loads[0].wait()
    wide[...] = pair_ref[...].astype(F32).reshape(POS, CH)
    for t in range(4):
        rows = [
            wide[pl.ds(256 * g + 16 * e + 2 * s + b, 8, stride=32), :] for s in (2 * t, 2 * t + 1) for b, g, e in order
        ]
        normalize(0, t, jnp.concatenate(rows, axis=0).T)
    pl.semaphore_wait(hop_sem, COLS - 1)
    home1 = scatter(0)
    multiply(0)
    for n in (5, 6, 7, 8):
        loads[n].wait()
    prepare_out(0)
    make_gate(0)
    prepare(1)
    prepare_out(1)
    sent(tile, send_sem.at[0], home1)
    finish(0)
    for t in range(4):
        normalize(1, t, updated(0, t).astype(BF16).astype(F32))
    home2 = scatter(1)
    sent(outgoing, ret_send.at[0], home1)
    multiply(1)
    make_gate(1)
    sent(tile, send_sem.at[1], home2)
    finish(1)
    for t in range(4):
        values = updated(1, t).T
        for n, (s, (b, g, e)) in enumerate([(s, place) for s in (2 * t, 2 * t + 1) for place in order]):
            stage[pl.ds(256 * g + 16 * e + 2 * s + b, 8, stride=32), :] = values[8 * n : 8 * n + 8]
    out_ref[...] = stage[...].reshape(TR, TC, CH).astype(BF16)
    sent(outgoing, ret_send.at[1], home1)


def shards(pair, residue_mask, in_gain, in_bias, proj_weight, gate_weight, out_gain, out_bias, out_weight):
    arguments = (
        pair, residue_mask.reshape(1, 512), in_gain, in_bias, proj_weight, gate_weight, out_gain, out_bias, out_weight
    )
    dma = pltpu.SemaphoreType.DMA
    return pl.pallas_call(
        kernel,
        out_shape=pltpu.VMEM((TR, TC, CH), BF16),
        in_specs=[pl.BlockSpec(memory_space=pltpu.HBM)] * 9,
        out_specs=pl.BlockSpec(memory_space=pltpu.VMEM),
        scratch_shapes=[pltpu.VMEM(value.shape, value.dtype) for value in arguments] + [
            pltpu.VMEM((POS, CH), F32),
            pltpu.VMEM((4, CH, 256), F32),
            pltpu.VMEM((4, CH, 256), F32),
            pltpu.VMEM((POS, CH), F32),
            pltpu.VMEM((8, CH), F32),
            pltpu.VMEM((8, CH), F32),
            pltpu.VMEM((8, CH), F32),
            pltpu.VMEM((CH, POS), BF16),
            pltpu.VMEM((2, 512, CH), BF16),
            pltpu.VMEM((512, POS), F32),
            pltpu.VMEM((2, CH, CH), BF16),
            pltpu.VMEM((2, CH, CH), BF16),
            pltpu.VMEM((2, 4, CH, CH), F32),
            pltpu.VMEM((CH, 16, CH), BF16),
            pltpu.VMEM((CH, 16, CH), BF16),
            pltpu.VMEM((CH, 16, CH), BF16),
            pltpu.VMEM((CH, 8, CH), BF16),
            pltpu.VMEM((CH, 8, CH), BF16),
            pltpu.VMEM((256, 512), BF16),
            pltpu.VMEM((256, 512), BF16),
            pltpu.VMEM((256, 512), BF16),
            pltpu.VMEM((512, 256), BF16),
            pltpu.VMEM((256, 512), BF16),
            pltpu.VMEM((512, 256), F32),
            pltpu.VMEM((CH, 8, CH), BF16),
            dma((9,)),
            pltpu.SemaphoreType.REGULAR,
            dma((2,)), dma((16,)), dma((2,)), dma((2,)), dma((2,)), dma((4,)),
        ],
        compiler_params=pltpu.CompilerParams(
            collective_id=0, has_side_effects=True, vmem_limit_bytes=48 * 1024 * 1024
        ),
        cost_estimate=pl.CostEstimate(flops=700_000_000, bytes_accessed=4_000_000, transcendentals=1_000_000),
    )(*[pltpu.with_memory_space_constraint(value, pltpu.HBM) for value in arguments])


def solution(mesh):
    placed = (P("row", "col", None), P(), P(), P(), P(), P(), P(), P(), P())
    return jax.shard_map(
        shards, mesh=mesh, in_specs=placed, out_specs=P("row", "col", None), check_vma=False
    )
```

```python
import jax
import jax.numpy as jnp
from jax import lax
from jax.experimental import pallas as pl
from jax.experimental.pallas import tpu as pltpu
from jax.sharding import PartitionSpec as P

MESH = pl.DeviceIdType.MESH
F32 = jnp.float32
BF16 = jnp.bfloat16
ROWS, COLS = 8, 32
TR, TC = 64, 16
CH = 128
POS = TR * TC


def sigmoid(values):
    return 0.5 * jnp.tanh(0.5 * values) + 0.5


def kernel(
    pair_hbm, mask_hbm, gain_hbm, bias_hbm, wp_hbm, wg_hbm, ogain_hbm, obias_hbm, wo_hbm,
    out_ref,
    pair_ref, mask_in, gain_ref, bias_ref, wp_ref, wg_ref, ogain_ref, obias_ref, wo_ref,
    wide, cur, gate, stage, masks, means, rstds, normed, wpt, proj_all, wgt, wot, gains,
    tile, recv1, recv2, back1, back2, swap1, swap2, mine_r, mine_l, mine_l2, raw_r, outgoing,
    load_sem, hop_sem, send_sem, in_sem, swap_send, swap_recv, ret_send, ret_recv,
):
    row = lax.axis_index("row")
    col = lax.axis_index("col")
    core = lax.rem(col, 2)
    sibling = col + 1 - 2 * core
    x, y_lo = lax.rem(row, 4), row // 4
    z, y_hi = col // 4, lax.rem(col // 2, 2)

    z_low = lax.rem(z, 4)
    colour_here = lax.rem(x + 4 - z_low, 4)
    own = (colour_here * 4 + z_low) * 8 + z // 4 * 4 + y_hi * 2 + y_lo

    loads = [
        pltpu.make_async_copy(src, dst, load_sem.at[n])
        for n, (src, dst) in enumerate([
            (pair_hbm, pair_ref), (mask_hbm, mask_in), (gain_hbm, gain_ref), (bias_hbm, bias_ref), (wp_hbm, wp_ref),
            (wg_hbm, wg_ref), (ogain_hbm, ogain_ref), (obias_hbm, obias_ref), (wo_hbm, wo_ref),
        ])
    ]
    for load in loads:
        load.start()

    barrier = pltpu.get_barrier_semaphore()

    @pl.loop(1, ROWS)
    def _(d):
        pl.semaphore_signal(barrier, inc=1, device_id=(lax.rem(row + d, ROWS), col), device_id_type=MESH)

    @pl.loop(1, COLS)
    def _(d):
        pl.semaphore_signal(barrier, inc=1, device_id=(row, lax.rem(col + d, COLS)), device_id_type=MESH)

    def second_hop():
        pl.semaphore_wait(barrier, ROWS - 1 + COLS - 1)

        @pl.loop(1, COLS)
        def _(d):
            pl.semaphore_signal(hop_sem, inc=1, device_id=(row, lax.rem(col + d, COLS)), device_id_type=MESH)

    order = [(b, g, e) for b in range(2) for g in range(4) for e in range(2)]

    def make_masks():
        lane = lax.broadcasted_iota(jnp.int32, (8, CH), 1)
        mask = mask_in[...].astype(F32)
        number = lax.broadcasted_iota(jnp.int32, (8, 512), 1)
        sub = lax.broadcasted_iota(jnp.int32, (8, 512), 0)
        even_b = jnp.sum(jnp.where(number == TC * col + 2 * sub, mask, 0.0), axis=1, keepdims=True)
        odd_b = jnp.sum(jnp.where(number == TC * col + 2 * sub + 1, mask, 0.0), axis=1, keepdims=True)
        mask_b = jnp.where(lane < 64, even_b, odd_b)
        place = lax.broadcasted_iota(jnp.int32, (1, CH), 1)
        place = place - jnp.where(place >= 64, 64, 0)
        a_of = 16 * (place // 16) + (place // 8) % 2 + 2 * (place % 8)
        pick = jnp.where(lax.broadcasted_iota(jnp.int32, (512, CH), 0) == TR * row + a_of, 1.0, 0.0).astype(BF16)
        mask_a = jnp.dot(jnp.broadcast_to(mask, (8, 512)).astype(BF16), pick, preferred_element_type=F32)
        masks[...] = mask_a * mask_b

    def spread_out(ref, layer, n):
        gains[layer, n] = jnp.broadcast_to(ref[layer : layer + 1, :], (CH, CH)).T

    def prepare(layer):
        turned = wp_ref[layer].astype(F32).T
        for b in range(16):
            rows = [turned[128 * q + 8 * b : 128 * q + 8 * b + 8] for q in range(4)]
            wpt[layer, 32 * b : 32 * b + 32] = jnp.concatenate(rows, axis=0).astype(BF16)
        spread_out(gain_ref, layer, 0)
        spread_out(bias_ref, layer, 1)

    def prepare_out(layer):
        wgt[layer] = wg_ref[layer].astype(F32).T.astype(BF16)
        wot[layer] = wo_ref[layer].astype(F32).T.astype(BF16)
        spread_out(ogain_ref, layer, 2)
        spread_out(obias_ref, layer, 3)

    def twice(value):
        return jnp.concatenate([value, value], axis=1)

    def normalize(layer, t, values):
        center = values - jnp.mean(values, axis=0, keepdims=True)
        spread = jnp.mean(center * center, axis=0, keepdims=True)
        scaled = center * lax.rsqrt(spread + 1e-05) * twice(gains[layer, 0]) + twice(gains[layer, 1])
        part = scaled.astype(BF16)
        normed[:, 256 * t : 256 * t + 256] = part
        proj_all[:, 256 * t : 256 * t + 256] = jnp.dot(wpt[layer], part, preferred_element_type=F32)
        cur[t] = values

    def send(src, dst, to_row, to_col, send_sem, recv_sem, here):
        def local():
            pltpu.make_async_copy(src, dst, recv_sem).start()

        def remote():
            pltpu.make_async_remote_copy(
                src_ref=src, dst_ref=dst, send_sem=send_sem, recv_sem=recv_sem,
                device_id=(to_row, to_col), device_id_type=MESH,
            ).start()

        if here is None:
            remote()
        else:
            pl.when(here)(local)
            pl.when(jnp.logical_not(here))(remote)

    def sent(buffer, sem, home):
        count = buffer.shape[0]

        @pl.when(home)
        def _():
            part = buffer.at[pl.ds(0, count - 1)]
            pltpu.make_async_copy(part, part, sem).wait()

        @pl.when(jnp.logical_not(home))
        def _():
            pltpu.make_async_copy(buffer, buffer, sem).wait()

    def arrived(buffer, sem):
        pltpu.make_async_copy(buffer, buffer, sem).wait()

    def scatter(layer):
        to_core = y_lo if layer == 0 else col // 16
        corner = y_hi * 2 + core
        slot = z * 16 + x * 4 + corner if layer == 0 else z_low * 32 + row * 4 + corner
        dst = (recv1 if layer == 0 else recv2).at[slot]
        lows = [y_lo, 1 - y_lo]
        highs = [y_hi, 1 - y_hi]
        sides = [z // 4, 1 - z // 4]

        @pl.loop(0, 8)
        def _(g):
            colour, step = g // 2, lax.rem(g, 2)
            depths = [lax.rem(z_low + 3 - step, 4), lax.rem(z_low + step, 4)]
            blocks = [colour * 4 + depth for depth in depths]
            for n, block in enumerate(blocks):
                for s in range(8):
                    part = proj_all[pl.ds(pl.multiple_of(block * 32, 32), 32), CH * s : CH * s + CH]
                    keep = masks[s : s + 1, :]
                    stage[pl.ds(128 * n + s, 8, stride=16), :] = sigmoid(part[0:8]) * part[8:16] * keep
                    stage[pl.ds(128 * n + s + 8, 8, stride=16), :] = sigmoid(part[16:24]) * part[24:32] * keep
                tile[pl.ds(block * 8, 8)] = stage[128 * n : 128 * n + 128, :].reshape(8, 16, CH).astype(BF16)
            columns = [lax.rem(colour + depth, 4) for depth in depths]
            for m in range(16):
                dz, n = 1 - m % 2, m // 2 % 2
                dl, dh = 1 - m // 4 % 2, 1 - m // 8
                here = None
                if n == 1 and dz + dh + dl == 0:
                    here = jnp.logical_and(g == 2 * colour_here, to_core == core)
                send(
                    tile.at[blocks[n] * 8 + sides[dz] * 4 + highs[dh] * 2 + lows[dl]], dst,
                    lows[dl] * 4 + columns[n], (sides[dz] * 4 + depths[n]) * 4 + highs[dh] * 2 + to_core,
                    send_sem.at[layer], in_sem.at[8 * layer + z], here,
                )

        return to_core == core

    def make_gate(layer):
        for t in range(4):
            part = jnp.dot(wgt[layer], normed[:, 256 * t : 256 * t + 256], preferred_element_type=F32)
            gate[t] = sigmoid(part)

    def merge(first, second):
        low = lax.broadcasted_iota(jnp.int32, first.shape, 2) < 64
        even = jnp.where(low, first, pltpu.roll(second, 64, 2))
        odd = jnp.where(low, pltpu.roll(first, 64, 2), second)
        return even, odd

    def gather(layer):
        for step in range(8 if layer == 0 else 4):
            if layer == 0:
                recv, width, pairs = recv1, 16, 2
                place = lax.rem(z + (5, 1, 4, 0, 6, 2, 7, 3)[step], 8)
                sem = in_sem.at[place]
            else:
                recv, width, pairs = recv2, 32, 4
                place = lax.rem(z_low + (1, 0, 2, 3)[step], 4)
                sem = in_sem.at[8 + core * 4 + place]
            arrived(recv.at[pl.ds(place * width, width)], sem)
            rows = pl.ds(64 * step if layer == 0 else pl.multiple_of(place * 64, 64), 64)
            for p in range(pairs):
                first = recv[pl.ds(place * width + 8 * p, 4)].astype(F32)
                second = recv[pl.ds(place * width + 8 * p + 4, 4)].astype(F32)
                even, odd = merge(first, second)
                left = jnp.concatenate([even[:, :8], odd[:, :8]], axis=1).reshape(64, CH)
                right = jnp.concatenate([even[:, 8:], odd[:, 8:]], axis=1).reshape(64, CH)
                lanes = slice(128 * p, 128 * p + 128)
                if layer == 0:
                    mine_l[rows, lanes] = left.astype(BF16)
                    raw_r[rows, lanes] = right
                else:
                    mine_l2[rows, lanes] = left.astype(BF16)
                    mine_r[rows, lanes] = right.astype(BF16)
                if layer == 0 and step % 2 == 1:
                    block = slice(64 * step - 64, 64 * step + 64)
                    mine_r[lanes, block] = raw_r[block, lanes].T.astype(BF16)

    def quadrant(layer, q, right, dst):
        side = core if q == 0 else 1 - core
        lines = [lax.rem(x + n, 4) for n in range(4)]
        floors = [lax.rem(z_low + n, 4) for n in range(4)]

        @pl.loop(0, 4)
        def _(step):
            corner = lax.rem(y_hi + 1 - step // 2, 2) * 2 + lax.rem(core + 1 - lax.rem(step, 2), 2)
            rows = jnp.concatenate(
                [right[pl.ds(pl.multiple_of(64 * n + 16 * corner, 16), 16), :] for n in range(4)], axis=0
            )
            if layer == 0:
                mixed = jnp.dot(rows, mine_l[...], preferred_element_type=F32)
            else:
                mixed = lax.dot_general(rows, mine_l2[...], (((1,), (1,)), ((), ())), preferred_element_type=F32)
            base = q * 64 + corner * 16
            for p in range(2):
                block = mixed[:, 128 * p : 128 * p + 128].reshape(4, 16, CH)
                even, odd = merge(block[:, :8], block[:, 8:])
                outgoing[pl.ds(base + 8 * p, 4)] = even.astype(BF16)
                outgoing[pl.ds(base + 8 * p + 4, 4)] = odd.astype(BF16)
            for n in range(16):
                dx, dz = (2, 1, 3, 0)[(n + n // 4) % 4], (2, 1, 3, 0)[n % 4]
                here = None
                if dx == 0 and dz == 0:
                    here = jnp.logical_and(step == 3, jnp.logical_and(y_lo == core, side == z // 4))
                send(
                    outgoing.at[base + lines[dx] * 4 + floors[dz]], dst,
                    core * 4 + lines[dx], (side * 4 + floors[dz]) * 4 + corner,
                    ret_send.at[layer], ret_recv.at[2 * layer + colour_here // 2], here,
                )

    def multiply(layer):
        back = (back1 if layer == 0 else back2).at[own]
        swap = swap1 if layer == 0 else swap2
        gather(layer)
        exchange = pltpu.make_async_remote_copy(
            src_ref=mine_r, dst_ref=swap, send_sem=swap_send.at[layer], recv_sem=swap_recv.at[layer],
            device_id=(row, sibling), device_id_type=MESH,
        )
        exchange.start()
        quadrant(layer, 0, mine_r, back)
        exchange.wait_recv()
        quadrant(layer, 1, swap, back)
        exchange.wait_send()

    def finish(layer):
        back = back1 if layer == 0 else back2
        halves = []
        for colour in range(2):
            arrived(back.at[pl.ds(64 * colour, 64)], ret_recv.at[2 * layer + colour])
            total = jnp.zeros((8, CH), F32)
            for g in range(4 * colour, 4 * colour + 4):
                part = back[16 * g : 16 * g + 16].astype(F32)
                wide[128 * g : 128 * g + 128, :] = part.reshape(128, CH)
                total = total + jnp.sum(part, axis=0)
            mean = total * (1.0 / 64)
            total = jnp.zeros((8, CH), F32)
            for g in range(4 * colour, 4 * colour + 4):
                part = wide[128 * g : 128 * g + 128, :].reshape(16, 8, CH) - mean[None]
                total = total + jnp.sum(part * part, axis=0)
            halves.append((mean, total))
        (mean0, total0), (mean1, total1) = halves
        apart = 0.5 * (mean0 - mean1)
        means[...] = 0.5 * (mean0 + mean1)
        rstds[...] = lax.rsqrt((total0 + total1) * (1.0 / CH) + apart * apart + 1e-05)

    def updated(layer, t):
        pair_of = [2 * t, 2 * t + 1]
        mixed = jnp.concatenate([wide[pl.ds(s, CH, stride=8), :] for s in pair_of], axis=1)
        mean = jnp.concatenate([means[s : s + 1, :] for s in pair_of], axis=1)
        rstd = jnp.concatenate([rstds[s : s + 1, :] for s in pair_of], axis=1)
        out_normed = (mixed - mean) * rstd * twice(gains[layer, 2]) + twice(gains[layer, 3])
        update = jnp.dot(wot[layer], out_normed.astype(BF16), preferred_element_type=F32)
        return cur[t] + gate[t] * update

    loads[1].wait()
    make_masks()
    for n in (2, 3, 4):
        loads[n].wait()
    prepare(0)
    second_hop()
    loads[0].wait()
    wide[...] = pair_ref[...].astype(F32).reshape(POS, CH)
    for t in range(4):
        rows = [
            wide[pl.ds(256 * g + 16 * e + 2 * s + b, 8, stride=32), :] for s in (2 * t, 2 * t + 1) for b, g, e in order
        ]
        normalize(0, t, jnp.concatenate(rows, axis=0).T)
    pl.semaphore_wait(hop_sem, COLS - 1)
    home1 = scatter(0)
    multiply(0)
    for n in (5, 6, 7, 8):
        loads[n].wait()
    prepare_out(0)
    make_gate(0)
    prepare(1)
    prepare_out(1)
    sent(tile, send_sem.at[0], home1)
    finish(0)
    for t in range(4):
        normalize(1, t, updated(0, t).astype(BF16).astype(F32))
    home2 = scatter(1)
    sent(outgoing, ret_send.at[0], home1)
    multiply(1)
    make_gate(1)
    sent(tile, send_sem.at[1], home2)
    finish(1)
    for t in range(4):
        values = updated(1, t).T
        for n, (s, (b, g, e)) in enumerate([(s, place) for s in (2 * t, 2 * t + 1) for place in order]):
            stage[pl.ds(256 * g + 16 * e + 2 * s + b, 8, stride=32), :] = values[8 * n : 8 * n + 8]
    out_ref[...] = stage[...].reshape(TR, TC, CH).astype(BF16)
    sent(outgoing, ret_send.at[1], home1)


def shards(pair, residue_mask, in_gain, in_bias, proj_weight, gate_weight, out_gain, out_bias, out_weight):
    arguments = (
        pair, residue_mask.reshape(1, 512), in_gain, in_bias, proj_weight, gate_weight, out_gain, out_bias, out_weight
    )
    dma = pltpu.SemaphoreType.DMA
    return pl.pallas_call(
        kernel,
        out_shape=pltpu.VMEM((TR, TC, CH), BF16),
        in_specs=[pl.BlockSpec(memory_space=pltpu.HBM)] * 9,
        out_specs=pl.BlockSpec(memory_space=pltpu.VMEM),
        scratch_shapes=[pltpu.VMEM(value.shape, value.dtype) for value in arguments] + [
            pltpu.VMEM((POS, CH), F32),
            pltpu.VMEM((4, CH, 256), F32),
            pltpu.VMEM((4, CH, 256), F32),
            pltpu.VMEM((POS, CH), F32),
            pltpu.VMEM((8, CH), F32),
            pltpu.VMEM((8, CH), F32),
            pltpu.VMEM((8, CH), F32),
            pltpu.VMEM((CH, POS), BF16),
            pltpu.VMEM((2, 512, CH), BF16),
            pltpu.VMEM((512, POS), F32),
            pltpu.VMEM((2, CH, CH), BF16),
            pltpu.VMEM((2, CH, CH), BF16),
            pltpu.VMEM((2, 4, CH, CH), F32),
            pltpu.VMEM((CH, 16, CH), BF16),
            pltpu.VMEM((CH, 16, CH), BF16),
            pltpu.VMEM((CH, 16, CH), BF16),
            pltpu.VMEM((CH, 8, CH), BF16),
            pltpu.VMEM((CH, 8, CH), BF16),
            pltpu.VMEM((256, 512), BF16),
            pltpu.VMEM((256, 512), BF16),
            pltpu.VMEM((256, 512), BF16),
            pltpu.VMEM((512, 256), BF16),
            pltpu.VMEM((256, 512), BF16),
            pltpu.VMEM((512, 256), F32),
            pltpu.VMEM((CH, 8, CH), BF16),
            dma((9,)),
            pltpu.SemaphoreType.REGULAR,
            dma((2,)), dma((16,)), dma((2,)), dma((2,)), dma((2,)), dma((4,)),
        ],
        compiler_params=pltpu.CompilerParams(
            collective_id=0, has_side_effects=True, vmem_limit_bytes=48 * 1024 * 1024
        ),
        cost_estimate=pl.CostEstimate(flops=700_000_000, bytes_accessed=4_000_000, transcendentals=1_000_000),
    )(*[pltpu.with_memory_space_constraint(value, pltpu.HBM) for value in arguments])


def solution(mesh):
    placed = (P("row", "col", None), P(), P(), P(), P(), P(), P(), P(), P())
    return jax.shard_map(
        shards, mesh=mesh, in_specs=placed, out_specs=P("row", "col", None), check_vma=False
    )
```

```python
import jax
import jax.numpy as jnp
from jax import lax
from jax.experimental import pallas as pl
from jax.experimental.pallas import tpu as pltpu
from jax.sharding import PartitionSpec as P

MESH = pl.DeviceIdType.MESH
F32 = jnp.float32
BF16 = jnp.bfloat16
ROWS, COLS = 8, 32
TR, TC = 64, 16
CH = 128
POS = TR * TC


def sigmoid(values):
    return 0.5 * jnp.tanh(0.5 * values) + 0.5


def kernel(
    pair_hbm, mask_hbm, gain_hbm, bias_hbm, wp_hbm, wg_hbm, ogain_hbm, obias_hbm, wo_hbm,
    out_ref,
    pair_ref, mask_in, gain_ref, bias_ref, wp_ref, wg_ref, ogain_ref, obias_ref, wo_ref,
    wide, cur, gate, stage, masks, means, rstds, normed, wpt, proj_all, wgt, wot, gains,
    tile, recv1, recv2, back1, back2, swap1, swap2, mine_r, mine_l, mine_l2, raw_r, outgoing,
    load_sem, hop_sem, send_sem, in_sem, swap_send, swap_recv, ret_send, ret_recv,
):
    row = lax.axis_index("row")
    col = lax.axis_index("col")
    core = lax.rem(col, 2)
    sibling = col + 1 - 2 * core
    x, y_lo = lax.rem(row, 4), row // 4
    z, y_hi = col // 4, lax.rem(col // 2, 2)

    z_low = lax.rem(z, 4)
    colour_here = lax.rem(x + 4 - z_low, 4)
    own = (colour_here * 4 + z_low) * 8 + z // 4 * 4 + y_hi * 2 + y_lo

    loads = [
        pltpu.make_async_copy(src, dst, load_sem.at[n])
        for n, (src, dst) in enumerate([
            (pair_hbm, pair_ref), (mask_hbm, mask_in), (gain_hbm, gain_ref), (bias_hbm, bias_ref), (wp_hbm, wp_ref),
            (wg_hbm, wg_ref), (ogain_hbm, ogain_ref), (obias_hbm, obias_ref), (wo_hbm, wo_ref),
        ])
    ]
    for load in loads:
        load.start()

    barrier = pltpu.get_barrier_semaphore()

    @pl.loop(1, ROWS)
    def _(d):
        pl.semaphore_signal(barrier, inc=1, device_id=(lax.rem(row + d, ROWS), col), device_id_type=MESH)

    @pl.loop(1, COLS)
    def _(d):
        pl.semaphore_signal(barrier, inc=1, device_id=(row, lax.rem(col + d, COLS)), device_id_type=MESH)

    def second_hop():
        pl.semaphore_wait(barrier, ROWS - 1 + COLS - 1)

        @pl.loop(1, COLS)
        def _(d):
            pl.semaphore_signal(hop_sem, inc=1, device_id=(row, lax.rem(col + d, COLS)), device_id_type=MESH)

    order = [(b, g, e) for b in range(2) for g in range(4) for e in range(2)]

    def make_masks():
        lane = lax.broadcasted_iota(jnp.int32, (8, CH), 1)
        mask = mask_in[...].astype(F32)
        number = lax.broadcasted_iota(jnp.int32, (8, 512), 1)
        sub = lax.broadcasted_iota(jnp.int32, (8, 512), 0)
        even_b = jnp.sum(jnp.where(number == TC * col + 2 * sub, mask, 0.0), axis=1, keepdims=True)
        odd_b = jnp.sum(jnp.where(number == TC * col + 2 * sub + 1, mask, 0.0), axis=1, keepdims=True)
        mask_b = jnp.where(lane < 64, even_b, odd_b)
        place = lax.broadcasted_iota(jnp.int32, (1, CH), 1)
        place = place - jnp.where(place >= 64, 64, 0)
        a_of = 16 * (place // 16) + (place // 8) % 2 + 2 * (place % 8)
        pick = jnp.where(lax.broadcasted_iota(jnp.int32, (512, CH), 0) == TR * row + a_of, 1.0, 0.0).astype(BF16)
        mask_a = jnp.dot(jnp.broadcast_to(mask, (8, 512)).astype(BF16), pick, preferred_element_type=F32)
        masks[...] = mask_a * mask_b

    def spread_out(ref, layer, n):
        gains[layer, n] = jnp.broadcast_to(ref[layer : layer + 1, :], (CH, CH)).T

    def prepare(layer):
        turned = wp_ref[layer].astype(F32).T
        for b in range(16):
            rows = [turned[128 * q + 8 * b : 128 * q + 8 * b + 8] for q in range(4)]
            wpt[layer, 32 * b : 32 * b + 32] = jnp.concatenate(rows, axis=0).astype(BF16)
        spread_out(gain_ref, layer, 0)
        spread_out(bias_ref, layer, 1)

    def prepare_out(layer):
        wgt[layer] = wg_ref[layer].astype(F32).T.astype(BF16)
        wot[layer] = wo_ref[layer].astype(F32).T.astype(BF16)
        spread_out(ogain_ref, layer, 2)
        spread_out(obias_ref, layer, 3)

    def twice(value):
        return jnp.concatenate([value, value], axis=1)

    def normalize(layer, t, values):
        center = values - jnp.mean(values, axis=0, keepdims=True)
        spread = jnp.mean(center * center, axis=0, keepdims=True)
        scaled = center * lax.rsqrt(spread + 1e-05) * twice(gains[layer, 0]) + twice(gains[layer, 1])
        part = scaled.astype(BF16)
        normed[:, 256 * t : 256 * t + 256] = part
        proj_all[:, 256 * t : 256 * t + 256] = jnp.dot(wpt[layer], part, preferred_element_type=F32)
        cur[t] = values

    def send(src, dst, to_row, to_col, send_sem, recv_sem, here):
        def local():
            pltpu.make_async_copy(src, dst, recv_sem).start()

        def remote():
            pltpu.make_async_remote_copy(
                src_ref=src, dst_ref=dst, send_sem=send_sem, recv_sem=recv_sem,
                device_id=(to_row, to_col), device_id_type=MESH,
            ).start()

        if here is None:
            remote()
        else:
            pl.when(here)(local)
            pl.when(jnp.logical_not(here))(remote)

    def sent(buffer, sem, home):
        count = buffer.shape[0]

        @pl.when(home)
        def _():
            part = buffer.at[pl.ds(0, count - 1)]
            pltpu.make_async_copy(part, part, sem).wait()

        @pl.when(jnp.logical_not(home))
        def _():
            pltpu.make_async_copy(buffer, buffer, sem).wait()

    def arrived(buffer, sem):
        pltpu.make_async_copy(buffer, buffer, sem).wait()

    def scatter(layer):
        to_core = y_lo if layer == 0 else col // 16
        corner = y_hi * 2 + core
        slot = z * 16 + x * 4 + corner if layer == 0 else z_low * 32 + row * 4 + corner
        dst = (recv1 if layer == 0 else recv2).at[slot]
        lows = [y_lo, 1 - y_lo]
        highs = [y_hi, 1 - y_hi]

        @pl.loop(0, 4)
        def _(colour):
            blocks = [colour * 4 + lax.rem(z_low + a, 4) for a in range(4)]
            columns = [lax.rem(colour + z_low + a, 4) for a in range(4)]

            def pack(a):
                for s in range(8):
                    part = proj_all[pl.ds(pl.multiple_of(blocks[a] * 32, 32), 32), CH * s : CH * s + CH]
                    keep = masks[s : s + 1, :]
                    stage[pl.ds(128 * a + s, 8, stride=16), :] = sigmoid(part[0:8]) * part[8:16] * keep
                    stage[pl.ds(128 * a + s + 8, 8, stride=16), :] = sigmoid(part[16:24]) * part[24:32] * keep
                tile[pl.ds(blocks[a] * 8, 8)] = stage[128 * a : 128 * a + 128, :].reshape(8, 16, CH).astype(BF16)

            def deliver(shifts):
                for dh in (1, 0):
                    for dl in (1, 0):
                        for shift in shifts:
                            a, depth = shift % 4, lax.rem(z + shift, 8)
                            here = None
                            if shift + dh + dl == 0:
                                here = jnp.logical_and(colour == colour_here, to_core == core)
                            send(
                                tile.at[blocks[a] * 8 + depth // 4 * 4 + highs[dh] * 2 + lows[dl]], dst,
                                lows[dl] * 4 + columns[a], depth * 4 + highs[dh] * 2 + to_core,
                                send_sem.at[layer], in_sem.at[8 * layer + z], here,
                            )

            pack(0)
            pack(3)
            deliver((4, 3))
            pack(1)
            pack(2)
            deliver((5, 2, 6))
            deliver((1, 7, 0))

        return to_core == core

    def make_gate(layer):
        for t in range(4):
            part = jnp.dot(wgt[layer], normed[:, 256 * t : 256 * t + 256], preferred_element_type=F32)
            gate[t] = sigmoid(part)

    def merge(first, second):
        low = lax.broadcasted_iota(jnp.int32, first.shape, 2) < 64
        even = jnp.where(low, first, pltpu.roll(second, 64, 2))
        odd = jnp.where(low, pltpu.roll(first, 64, 2), second)
        return even, odd

    def far_first(step, same):
        falling = (z_low < 2) == same
        return jnp.where(falling, 3 - step, step)

    def gather(layer):
        for step in range(8 if layer == 0 else 4):
            if layer == 0:
                recv, width, pairs = recv1, 16, 2
                place = lax.rem(z + (4, 5, 3, 6, 2, 7, 1, 0)[step], 8)
                sem = in_sem.at[place]
            else:
                recv, width, pairs = recv2, 32, 4
                place = lax.rem(z_low + (1, 0, 2, 3)[step], 4)
                sem = in_sem.at[8 + core * 4 + place]
            arrived(recv.at[pl.ds(place * width, width)], sem)
            rows = pl.ds(64 * step if layer == 0 else pl.multiple_of(place * 64, 64), 64)
            for p in range(pairs):
                first = recv[pl.ds(place * width + 8 * p, 4)].astype(F32)
                second = recv[pl.ds(place * width + 8 * p + 4, 4)].astype(F32)
                even, odd = merge(first, second)
                left = jnp.concatenate([even[:, :8], odd[:, :8]], axis=1).reshape(64, CH)
                right = jnp.concatenate([even[:, 8:], odd[:, 8:]], axis=1).reshape(64, CH)
                lanes = slice(128 * p, 128 * p + 128)
                if layer == 0:
                    mine_l[rows, lanes] = left.astype(BF16)
                    raw_r[rows, lanes] = right
                else:
                    mine_l2[rows, lanes] = left.astype(BF16)
                    mine_r[rows, lanes] = right.astype(BF16)
                if layer == 0 and step % 2 == 1:
                    block = slice(64 * step - 64, 64 * step + 64)
                    mine_r[lanes, block] = raw_r[block, lanes].T.astype(BF16)

    def quadrant(layer, q, right, dst):
        side = core if q == 0 else 1 - core
        lines = [lax.rem(x + n, 4) for n in range(4)]
        corners = [(y_hi if dy == 0 else 1 - y_hi) * 2 + (core if dc == 0 else 1 - core) for dy in range(2) for dc in range(2)]

        @pl.loop(0, 4)
        def _(step):
            depth = far_first(step, z // 4 == side)
            rows = right[pl.ds(pl.multiple_of(depth * 64, 64), 64), :]
            if layer == 0:
                mixed = jnp.dot(rows, mine_l[...], preferred_element_type=F32)
            else:
                mixed = lax.dot_general(rows, mine_l2[...], (((1,), (1,)), ((), ())), preferred_element_type=F32)
            base = q * 64 + depth * 16
            for p in range(2):
                block = mixed[:, 128 * p : 128 * p + 128].reshape(4, 16, CH)
                even, odd = merge(block[:, :8], block[:, 8:])
                outgoing[pl.ds(base + 8 * p, 4)] = even.astype(BF16)
                outgoing[pl.ds(base + 8 * p + 4, 4)] = odd.astype(BF16)
            for corner in (3, 2, 1, 0):
                for dx in (2, 1, 3, 0):
                    here = None
                    if corner == 0 and dx == 0:
                        here = jnp.logical_and(y_lo == core, side * 4 + depth == z)
                    send(
                        outgoing.at[base + lines[dx] * 4 + corners[corner]], dst,
                        core * 4 + lines[dx], (side * 4 + depth) * 4 + corners[corner],
                        ret_send.at[layer], ret_recv.at[2 * layer + colour_here // 2], here,
                    )

    def multiply(layer):
        back = (back1 if layer == 0 else back2).at[own]
        swap = swap1 if layer == 0 else swap2
        gather(layer)
        exchange = pltpu.make_async_remote_copy(
            src_ref=mine_r, dst_ref=swap, send_sem=swap_send.at[layer], recv_sem=swap_recv.at[layer],
            device_id=(row, sibling), device_id_type=MESH,
        )
        exchange.start()
        quadrant(layer, 0, mine_r, back)
        exchange.wait_recv()
        quadrant(layer, 1, swap, back)
        exchange.wait_send()

    def finish(layer):
        back = back1 if layer == 0 else back2
        halves = []
        for colour in range(2):
            arrived(back.at[pl.ds(64 * colour, 64)], ret_recv.at[2 * layer + colour])
            total = jnp.zeros((8, CH), F32)
            for g in range(4 * colour, 4 * colour + 4):
                part = back[16 * g : 16 * g + 16].astype(F32)
                wide[128 * g : 128 * g + 128, :] = part.reshape(128, CH)
                total = total + jnp.sum(part, axis=0)
            mean = total * (1.0 / 64)
            total = jnp.zeros((8, CH), F32)
            for g in range(4 * colour, 4 * colour + 4):
                part = wide[128 * g : 128 * g + 128, :].reshape(16, 8, CH) - mean[None]
                total = total + jnp.sum(part * part, axis=0)
            halves.append((mean, total))
        (mean0, total0), (mean1, total1) = halves
        apart = 0.5 * (mean0 - mean1)
        means[...] = 0.5 * (mean0 + mean1)
        rstds[...] = lax.rsqrt((total0 + total1) * (1.0 / CH) + apart * apart + 1e-05)

    def updated(layer, t):
        pair_of = [2 * t, 2 * t + 1]
        mixed = jnp.concatenate([wide[pl.ds(s, CH, stride=8), :] for s in pair_of], axis=1)
        mean = jnp.concatenate([means[s : s + 1, :] for s in pair_of], axis=1)
        rstd = jnp.concatenate([rstds[s : s + 1, :] for s in pair_of], axis=1)
        out_normed = (mixed - mean) * rstd * twice(gains[layer, 2]) + twice(gains[layer, 3])
        update = jnp.dot(wot[layer], out_normed.astype(BF16), preferred_element_type=F32)
        return cur[t] + gate[t] * update

    loads[1].wait()
    make_masks()
    for n in (2, 3, 4):
        loads[n].wait()
    prepare(0)
    second_hop()
    loads[0].wait()
    wide[...] = pair_ref[...].astype(F32).reshape(POS, CH)
    for t in range(4):
        rows = [
            wide[pl.ds(256 * g + 16 * e + 2 * s + b, 8, stride=32), :] for s in (2 * t, 2 * t + 1) for b, g, e in order
        ]
        normalize(0, t, jnp.concatenate(rows, axis=0).T)
    pl.semaphore_wait(hop_sem, COLS - 1)
    home1 = scatter(0)
    multiply(0)
    for n in (5, 6, 7, 8):
        loads[n].wait()
    prepare_out(0)
    make_gate(0)
    prepare(1)
    prepare_out(1)
    sent(tile, send_sem.at[0], home1)
    finish(0)
    for t in range(4):
        normalize(1, t, updated(0, t).astype(BF16).astype(F32))
    home2 = scatter(1)
    sent(outgoing, ret_send.at[0], home1)
    multiply(1)
    make_gate(1)
    sent(tile, send_sem.at[1], home2)
    finish(1)
    for t in range(4):
        values = updated(1, t).T
        for n, (s, (b, g, e)) in enumerate([(s, place) for s in (2 * t, 2 * t + 1) for place in order]):
            stage[pl.ds(256 * g + 16 * e + 2 * s + b, 8, stride=32), :] = values[8 * n : 8 * n + 8]
    out_ref[...] = stage[...].reshape(TR, TC, CH).astype(BF16)
    sent(outgoing, ret_send.at[1], home1)


def shards(pair, residue_mask, in_gain, in_bias, proj_weight, gate_weight, out_gain, out_bias, out_weight):
    arguments = (
        pair, residue_mask.reshape(1, 512), in_gain, in_bias, proj_weight, gate_weight, out_gain, out_bias, out_weight
    )
    dma = pltpu.SemaphoreType.DMA
    return pl.pallas_call(
        kernel,
        out_shape=pltpu.VMEM((TR, TC, CH), BF16),
        in_specs=[pl.BlockSpec(memory_space=pltpu.HBM)] * 9,
        out_specs=pl.BlockSpec(memory_space=pltpu.VMEM),
        scratch_shapes=[pltpu.VMEM(value.shape, value.dtype) for value in arguments] + [
            pltpu.VMEM((POS, CH), F32),
            pltpu.VMEM((4, CH, 256), F32),
            pltpu.VMEM((4, CH, 256), F32),
            pltpu.VMEM((POS, CH), F32),
            pltpu.VMEM((8, CH), F32),
            pltpu.VMEM((8, CH), F32),
            pltpu.VMEM((8, CH), F32),
            pltpu.VMEM((CH, POS), BF16),
            pltpu.VMEM((2, 512, CH), BF16),
            pltpu.VMEM((512, POS), F32),
            pltpu.VMEM((2, CH, CH), BF16),
            pltpu.VMEM((2, CH, CH), BF16),
            pltpu.VMEM((2, 4, CH, CH), F32),
            pltpu.VMEM((CH, 16, CH), BF16),
            pltpu.VMEM((CH, 16, CH), BF16),
            pltpu.VMEM((CH, 16, CH), BF16),
            pltpu.VMEM((CH, 8, CH), BF16),
            pltpu.VMEM((CH, 8, CH), BF16),
            pltpu.VMEM((256, 512), BF16),
            pltpu.VMEM((256, 512), BF16),
            pltpu.VMEM((256, 512), BF16),
            pltpu.VMEM((512, 256), BF16),
            pltpu.VMEM((256, 512), BF16),
            pltpu.VMEM((512, 256), F32),
            pltpu.VMEM((CH, 8, CH), BF16),
            dma((9,)),
            pltpu.SemaphoreType.REGULAR,
            dma((2,)), dma((16,)), dma((2,)), dma((2,)), dma((2,)), dma((4,)),
        ],
        compiler_params=pltpu.CompilerParams(
            collective_id=0, has_side_effects=True, vmem_limit_bytes=48 * 1024 * 1024
        ),
        cost_estimate=pl.CostEstimate(flops=700_000_000, bytes_accessed=4_000_000, transcendentals=1_000_000),
    )(*[pltpu.with_memory_space_constraint(value, pltpu.HBM) for value in arguments])


def solution(mesh):
    placed = (P("row", "col", None), P(), P(), P(), P(), P(), P(), P(), P())
    return jax.shard_map(
        shards, mesh=mesh, in_specs=placed, out_specs=P("row", "col", None), check_vma=False
    )
```

```python
import jax
import jax.numpy as jnp
from jax import lax
from jax.experimental import pallas as pl
from jax.experimental.pallas import tpu as pltpu
from jax.sharding import PartitionSpec as P

MESH = pl.DeviceIdType.MESH
F32 = jnp.float32
BF16 = jnp.bfloat16
ROWS, COLS = 8, 32
TR, TC = 64, 16
CH = 128
POS = TR * TC


def sigmoid(values):
    return 0.5 * jnp.tanh(0.5 * values) + 0.5


def kernel(
    pair_hbm, mask_hbm, gain_hbm, bias_hbm, wp_hbm, wg_hbm, ogain_hbm, obias_hbm, wo_hbm,
    out_ref,
    pair_ref, mask_in, gain_ref, bias_ref, wp_ref, wg_ref, ogain_ref, obias_ref, wo_ref,
    wide, cur, gate, stage, masks, means, rstds, normed, wpt, proj_all, wgt, wot, gains,
    tile, recv1, recv2, back1, back2, swap1, swap2, mine_r, mine_l, mine_l2, raw_r, outgoing,
    load_sem, hop_sem, send_sem, in_sem, swap_send, swap_recv, ret_send, ret_recv,
):
    row = lax.axis_index("row")
    col = lax.axis_index("col")
    core = lax.rem(col, 2)
    sibling = col + 1 - 2 * core
    x, y_lo = lax.rem(row, 4), row // 4
    z, y_hi = col // 4, lax.rem(col // 2, 2)

    z_low = lax.rem(z, 4)
    colour_here = lax.rem(x + 4 - z_low, 4)
    own = (colour_here * 4 + z_low) * 8 + z // 4 * 4 + y_hi * 2 + y_lo

    loads = [
        pltpu.make_async_copy(src, dst, load_sem.at[n])
        for n, (src, dst) in enumerate([
            (pair_hbm, pair_ref), (mask_hbm, mask_in), (gain_hbm, gain_ref), (bias_hbm, bias_ref), (wp_hbm, wp_ref),
            (wg_hbm, wg_ref), (ogain_hbm, ogain_ref), (obias_hbm, obias_ref), (wo_hbm, wo_ref),
        ])
    ]
    for load in loads:
        load.start()

    barrier = pltpu.get_barrier_semaphore()

    @pl.loop(1, ROWS)
    def _(d):
        pl.semaphore_signal(barrier, inc=1, device_id=(lax.rem(row + d, ROWS), col), device_id_type=MESH)

    @pl.loop(1, COLS)
    def _(d):
        pl.semaphore_signal(barrier, inc=1, device_id=(row, lax.rem(col + d, COLS)), device_id_type=MESH)

    def second_hop():
        pl.semaphore_wait(barrier, ROWS - 1 + COLS - 1)

        @pl.loop(1, COLS)
        def _(d):
            pl.semaphore_signal(hop_sem, inc=1, device_id=(row, lax.rem(col + d, COLS)), device_id_type=MESH)

    order = [(b, g, e) for b in range(2) for g in range(4) for e in range(2)]

    def make_masks():
        lane = lax.broadcasted_iota(jnp.int32, (8, CH), 1)
        mask = mask_in[...].astype(F32)
        number = lax.broadcasted_iota(jnp.int32, (8, 512), 1)
        sub = lax.broadcasted_iota(jnp.int32, (8, 512), 0)
        even_b = jnp.sum(jnp.where(number == TC * col + 2 * sub, mask, 0.0), axis=1, keepdims=True)
        odd_b = jnp.sum(jnp.where(number == TC * col + 2 * sub + 1, mask, 0.0), axis=1, keepdims=True)
        mask_b = jnp.where(lane < 64, even_b, odd_b)
        place = lax.broadcasted_iota(jnp.int32, (1, CH), 1)
        place = place - jnp.where(place >= 64, 64, 0)
        a_of = 16 * (place // 16) + (place // 8) % 2 + 2 * (place % 8)
        pick = jnp.where(lax.broadcasted_iota(jnp.int32, (512, CH), 0) == TR * row + a_of, 1.0, 0.0).astype(BF16)
        mask_a = jnp.dot(jnp.broadcast_to(mask, (8, 512)).astype(BF16), pick, preferred_element_type=F32)
        masks[...] = mask_a * mask_b

    def spread_out(ref, layer, n):
        gains[layer, n] = jnp.broadcast_to(ref[layer : layer + 1, :], (CH, CH)).T

    def prepare(layer):
        turned = wp_ref[layer].astype(F32).T
        for b in range(16):
            rows = [turned[128 * q + 8 * b : 128 * q + 8 * b + 8] for q in range(4)]
            wpt[layer, 32 * b : 32 * b + 32] = jnp.concatenate(rows, axis=0).astype(BF16)
        spread_out(gain_ref, layer, 0)
        spread_out(bias_ref, layer, 1)

    def prepare_out(layer):
        wgt[layer] = wg_ref[layer].astype(F32).T.astype(BF16)
        wot[layer] = wo_ref[layer].astype(F32).T.astype(BF16)
        spread_out(ogain_ref, layer, 2)
        spread_out(obias_ref, layer, 3)

    def twice(value):
        return jnp.concatenate([value, value], axis=1)

    def normalize(layer, t, values):
        center = values - jnp.mean(values, axis=0, keepdims=True)
        spread = jnp.mean(center * center, axis=0, keepdims=True)
        scaled = center * lax.rsqrt(spread + 1e-05) * twice(gains[layer, 0]) + twice(gains[layer, 1])
        part = scaled.astype(BF16)
        normed[:, 256 * t : 256 * t + 256] = part
        proj_all[:, 256 * t : 256 * t + 256] = jnp.dot(wpt[layer], part, preferred_element_type=F32)
        cur[t] = values

    def send(src, dst, to_row, to_col, send_sem, recv_sem, here):
        def local():
            pltpu.make_async_copy(src, dst, recv_sem).start()

        def remote():
            pltpu.make_async_remote_copy(
                src_ref=src, dst_ref=dst, send_sem=send_sem, recv_sem=recv_sem,
                device_id=(to_row, to_col), device_id_type=MESH,
            ).start()

        if here is None:
            remote()
        else:
            pl.when(here)(local)
            pl.when(jnp.logical_not(here))(remote)

    def sent(buffer, sem, home):
        count = buffer.shape[0]

        @pl.when(home)
        def _():
            part = buffer.at[pl.ds(0, count - 1)]
            pltpu.make_async_copy(part, part, sem).wait()

        @pl.when(jnp.logical_not(home))
        def _():
            pltpu.make_async_copy(buffer, buffer, sem).wait()

    def arrived(buffer, sem):
        pltpu.make_async_copy(buffer, buffer, sem).wait()

    def scatter(layer):
        to_core = y_lo if layer == 0 else col // 16
        corner = y_hi * 2 + core
        slot = z * 16 + x * 4 + corner if layer == 0 else z_low * 32 + row * 4 + corner
        dst = (recv1 if layer == 0 else recv2).at[slot]
        lows = [y_lo, 1 - y_lo]
        highs = [y_hi, 1 - y_hi]
        sides = [z // 4, 1 - z // 4]

        @pl.loop(0, 8)
        def _(g):
            colour, step = g // 2, lax.rem(g, 2)
            depths = [lax.rem(z_low + 3 - step, 4), lax.rem(z_low + step, 4)]
            blocks = [colour * 4 + depth for depth in depths]
            for n, block in enumerate(blocks):
                for s in range(8):
                    part = proj_all[pl.ds(pl.multiple_of(block * 32, 32), 32), CH * s : CH * s + CH]
                    keep = masks[s : s + 1, :]
                    stage[pl.ds(128 * n + s, 8, stride=16), :] = sigmoid(part[0:8]) * part[8:16] * keep
                    stage[pl.ds(128 * n + s + 8, 8, stride=16), :] = sigmoid(part[16:24]) * part[24:32] * keep
                tile[pl.ds(block * 8, 8)] = stage[128 * n : 128 * n + 128, :].reshape(8, 16, CH).astype(BF16)
            if layer == 0:
                @pl.when(g == 0)
                def _():
                    pl.semaphore_wait(hop_sem, COLS - 1)

            columns = [lax.rem(colour + depth, 4) for depth in depths]
            for dz in (1, 0):
                for dh in (1, 0):
                    for dl in (1, 0):
                        for n in range(2):
                            here = None
                            if n == 1 and dz + dh + dl == 0:
                                here = jnp.logical_and(g == 2 * colour_here, to_core == core)
                            send(
                                tile.at[blocks[n] * 8 + sides[dz] * 4 + highs[dh] * 2 + lows[dl]], dst,
                                lows[dl] * 4 + columns[n], (sides[dz] * 4 + depths[n]) * 4 + highs[dh] * 2 + to_core,
                                send_sem.at[layer], in_sem.at[8 * layer + z], here,
                            )

        return to_core == core

    def make_gate(layer):
        for t in range(4):
            part = jnp.dot(wgt[layer], normed[:, 256 * t : 256 * t + 256], preferred_element_type=F32)
            gate[t] = sigmoid(part)

    def merge(first, second):
        low = lax.broadcasted_iota(jnp.int32, first.shape, 2) < 64
        even = jnp.where(low, first, pltpu.roll(second, 64, 2))
        odd = jnp.where(low, pltpu.roll(first, 64, 2), second)
        return even, odd

    def far_first(step, same):
        falling = (z_low < 2) == same
        return jnp.where(falling, 3 - step, step)

    def gather(layer):
        for step in range(8 if layer == 0 else 4):
            if layer == 0:
                recv, width, pairs = recv1, 16, 2
                place = lax.rem(z + (5, 1, 4, 0, 6, 2, 7, 3)[step], 8)
                sem = in_sem.at[place]
            else:
                recv, width, pairs = recv2, 32, 4
                place = lax.rem(z_low + (1, 0, 2, 3)[step], 4)
                sem = in_sem.at[8 + core * 4 + place]
            arrived(recv.at[pl.ds(place * width, width)], sem)
            rows = pl.ds(64 * step if layer == 0 else pl.multiple_of(place * 64, 64), 64)
            for p in range(pairs):
                first = recv[pl.ds(place * width + 8 * p, 4)].astype(F32)
                second = recv[pl.ds(place * width + 8 * p + 4, 4)].astype(F32)
                even, odd = merge(first, second)
                left = jnp.concatenate([even[:, :8], odd[:, :8]], axis=1).reshape(64, CH)
                right = jnp.concatenate([even[:, 8:], odd[:, 8:]], axis=1).reshape(64, CH)
                lanes = slice(128 * p, 128 * p + 128)
                if layer == 0:
                    mine_l[rows, lanes] = left.astype(BF16)
                    raw_r[rows, lanes] = right
                else:
                    mine_l2[rows, lanes] = left.astype(BF16)
                    mine_r[rows, lanes] = right.astype(BF16)
                if layer == 0 and step % 2 == 1:
                    block = slice(64 * step - 64, 64 * step + 64)
                    mine_r[lanes, block] = raw_r[block, lanes].T.astype(BF16)

    def quadrant(layer, q, right, dst):
        side = core if q == 0 else 1 - core
        lines = [lax.rem(x + n, 4) for n in range(4)]
        corners = [(y_hi if dy == 0 else 1 - y_hi) * 2 + (core if dc == 0 else 1 - core) for dy in range(2) for dc in range(2)]

        @pl.loop(0, 4)
        def _(step):
            depth = far_first(step, z // 4 == side)
            rows = right[pl.ds(pl.multiple_of(depth * 64, 64), 64), :]
            if layer == 0:
                mixed = jnp.dot(rows, mine_l[...], preferred_element_type=F32)
            else:
                mixed = lax.dot_general(rows, mine_l2[...], (((1,), (1,)), ((), ())), preferred_element_type=F32)
            base = q * 64 + depth * 16
            for p in range(2):
                block = mixed[:, 128 * p : 128 * p + 128].reshape(4, 16, CH)
                even, odd = merge(block[:, :8], block[:, 8:])
                outgoing[pl.ds(base + 8 * p, 4)] = even.astype(BF16)
                outgoing[pl.ds(base + 8 * p + 4, 4)] = odd.astype(BF16)
            for corner in (3, 2, 1, 0):
                for dx in (2, 1, 3, 0):
                    here = None
                    if corner == 0 and dx == 0:
                        here = jnp.logical_and(y_lo == core, side * 4 + depth == z)
                    send(
                        outgoing.at[base + lines[dx] * 4 + corners[corner]], dst,
                        core * 4 + lines[dx], (side * 4 + depth) * 4 + corners[corner],
                        ret_send.at[layer], ret_recv.at[2 * layer + colour_here // 2], here,
                    )

    def multiply(layer):
        back = (back1 if layer == 0 else back2).at[own]
        swap = swap1 if layer == 0 else swap2
        gather(layer)
        exchange = pltpu.make_async_remote_copy(
            src_ref=mine_r, dst_ref=swap, send_sem=swap_send.at[layer], recv_sem=swap_recv.at[layer],
            device_id=(row, sibling), device_id_type=MESH,
        )
        exchange.start()
        quadrant(layer, 0, mine_r, back)
        exchange.wait_recv()
        quadrant(layer, 1, swap, back)
        exchange.wait_send()

    def finish(layer):
        back = back1 if layer == 0 else back2
        halves = []
        for colour in range(2):
            arrived(back.at[pl.ds(64 * colour, 64)], ret_recv.at[2 * layer + colour])
            total = jnp.zeros((8, CH), F32)
            for g in range(4 * colour, 4 * colour + 4):
                part = back[16 * g : 16 * g + 16].astype(F32)
                wide[128 * g : 128 * g + 128, :] = part.reshape(128, CH)
                total = total + jnp.sum(part, axis=0)
            mean = total * (1.0 / 64)
            total = jnp.zeros((8, CH), F32)
            for g in range(4 * colour, 4 * colour + 4):
                part = wide[128 * g : 128 * g + 128, :].reshape(16, 8, CH) - mean[None]
                total = total + jnp.sum(part * part, axis=0)
            halves.append((mean, total))
        (mean0, total0), (mean1, total1) = halves
        apart = 0.5 * (mean0 - mean1)
        means[...] = 0.5 * (mean0 + mean1)
        rstds[...] = lax.rsqrt((total0 + total1) * (1.0 / CH) + apart * apart + 1e-05)

    def updated(layer, t):
        pair_of = [2 * t, 2 * t + 1]
        mixed = jnp.concatenate([wide[pl.ds(s, CH, stride=8), :] for s in pair_of], axis=1)
        mean = jnp.concatenate([means[s : s + 1, :] for s in pair_of], axis=1)
        rstd = jnp.concatenate([rstds[s : s + 1, :] for s in pair_of], axis=1)
        out_normed = (mixed - mean) * rstd * twice(gains[layer, 2]) + twice(gains[layer, 3])
        update = jnp.dot(wot[layer], out_normed.astype(BF16), preferred_element_type=F32)
        return cur[t] + gate[t] * update

    loads[1].wait()
    make_masks()
    for n in (2, 3, 4):
        loads[n].wait()
    prepare(0)
    loads[0].wait()
    wide[...] = pair_ref[...].astype(F32).reshape(POS, CH)
    for t in range(4):
        rows = [
            wide[pl.ds(256 * g + 16 * e + 2 * s + b, 8, stride=32), :] for s in (2 * t, 2 * t + 1) for b, g, e in order
        ]
        normalize(0, t, jnp.concatenate(rows, axis=0).T)
        if t == 0:
            second_hop()
    home1 = scatter(0)
    multiply(0)
    for n in (5, 6, 7, 8):
        loads[n].wait()
    prepare_out(0)
    make_gate(0)
    prepare(1)
    prepare_out(1)
    sent(tile, send_sem.at[0], home1)
    finish(0)
    for t in range(4):
        normalize(1, t, updated(0, t).astype(BF16).astype(F32))
    home2 = scatter(1)
    sent(outgoing, ret_send.at[0], home1)
    multiply(1)
    make_gate(1)
    sent(tile, send_sem.at[1], home2)
    finish(1)
    for t in range(4):
        values = updated(1, t).T
        for n, (s, (b, g, e)) in enumerate([(s, place) for s in (2 * t, 2 * t + 1) for place in order]):
            stage[pl.ds(256 * g + 16 * e + 2 * s + b, 8, stride=32), :] = values[8 * n : 8 * n + 8]
    out_ref[...] = stage[...].reshape(TR, TC, CH).astype(BF16)
    sent(outgoing, ret_send.at[1], home1)


def shards(pair, residue_mask, in_gain, in_bias, proj_weight, gate_weight, out_gain, out_bias, out_weight):
    arguments = (
        pair, residue_mask.reshape(1, 512), in_gain, in_bias, proj_weight, gate_weight, out_gain, out_bias, out_weight
    )
    dma = pltpu.SemaphoreType.DMA
    return pl.pallas_call(
        kernel,
        out_shape=pltpu.VMEM((TR, TC, CH), BF16),
        in_specs=[pl.BlockSpec(memory_space=pltpu.HBM)] * 9,
        out_specs=pl.BlockSpec(memory_space=pltpu.VMEM),
        scratch_shapes=[pltpu.VMEM(value.shape, value.dtype) for value in arguments] + [
            pltpu.VMEM((POS, CH), F32),
            pltpu.VMEM((4, CH, 256), F32),
            pltpu.VMEM((4, CH, 256), F32),
            pltpu.VMEM((POS, CH), F32),
            pltpu.VMEM((8, CH), F32),
            pltpu.VMEM((8, CH), F32),
            pltpu.VMEM((8, CH), F32),
            pltpu.VMEM((CH, POS), BF16),
            pltpu.VMEM((2, 512, CH), BF16),
            pltpu.VMEM((512, POS), F32),
            pltpu.VMEM((2, CH, CH), BF16),
            pltpu.VMEM((2, CH, CH), BF16),
            pltpu.VMEM((2, 4, CH, CH), F32),
            pltpu.VMEM((CH, 16, CH), BF16),
            pltpu.VMEM((CH, 16, CH), BF16),
            pltpu.VMEM((CH, 16, CH), BF16),
            pltpu.VMEM((CH, 8, CH), BF16),
            pltpu.VMEM((CH, 8, CH), BF16),
            pltpu.VMEM((256, 512), BF16),
            pltpu.VMEM((256, 512), BF16),
            pltpu.VMEM((256, 512), BF16),
            pltpu.VMEM((512, 256), BF16),
            pltpu.VMEM((256, 512), BF16),
            pltpu.VMEM((512, 256), F32),
            pltpu.VMEM((CH, 8, CH), BF16),
            dma((9,)),
            pltpu.SemaphoreType.REGULAR,
            dma((2,)), dma((16,)), dma((2,)), dma((2,)), dma((2,)), dma((4,)),
        ],
        compiler_params=pltpu.CompilerParams(
            collective_id=0, has_side_effects=True, vmem_limit_bytes=48 * 1024 * 1024
        ),
        cost_estimate=pl.CostEstimate(flops=700_000_000, bytes_accessed=4_000_000, transcendentals=1_000_000),
    )(*[pltpu.with_memory_space_constraint(value, pltpu.HBM) for value in arguments])


def solution(mesh):
    placed = (P("row", "col", None), P(), P(), P(), P(), P(), P(), P(), P())
    return jax.shard_map(
        shards, mesh=mesh, in_specs=placed, out_specs=P("row", "col", None), check_vma=False
    )
```

```python
import jax
import jax.numpy as jnp
from jax import lax
from jax.experimental import pallas as pl
from jax.experimental.pallas import tpu as pltpu
from jax.sharding import PartitionSpec as P

MESH = pl.DeviceIdType.MESH
F32 = jnp.float32
BF16 = jnp.bfloat16
ROWS, COLS = 8, 32
TR, TC = 64, 16
CH = 128
POS = TR * TC


def sigmoid(values):
    return 0.5 * jnp.tanh(0.5 * values) + 0.5


def kernel(
    pair_hbm, mask_hbm, gain_hbm, bias_hbm, wp_hbm, wg_hbm, ogain_hbm, obias_hbm, wo_hbm,
    out_ref,
    pair_ref, mask_in, gain_ref, bias_ref, wp_ref, wg_ref, ogain_ref, obias_ref, wo_ref,
    wide, cur, gate, stage, masks, means, rstds, normed, wpt, proj_all, wgt, wot, gains,
    tile, recv1, recv2, back1, back2, swap1, swap2, mine_r, mine_l, mine_l2, raw_r, outgoing,
    load_sem, hop_sem, send_sem, in_sem, swap_send, swap_recv, ret_send, ret_recv,
):
    row = lax.axis_index("row")
    col = lax.axis_index("col")
    core = lax.rem(col, 2)
    sibling = col + 1 - 2 * core
    x, y_lo = lax.rem(row, 4), row // 4
    z, y_hi = col // 4, lax.rem(col // 2, 2)

    colour_here = lax.rem(x + z, 2)
    own = (colour_here * 8 + z) * 8 + x // 2 * 4 + y_hi * 2 + y_lo
    z_low = lax.rem(z, 4)

    loads = [
        pltpu.make_async_copy(src, dst, load_sem.at[n])
        for n, (src, dst) in enumerate([
            (pair_hbm, pair_ref), (mask_hbm, mask_in), (gain_hbm, gain_ref), (bias_hbm, bias_ref), (wp_hbm, wp_ref),
            (wg_hbm, wg_ref), (ogain_hbm, ogain_ref), (obias_hbm, obias_ref), (wo_hbm, wo_ref),
        ])
    ]
    for load in loads:
        load.start()

    barrier = pltpu.get_barrier_semaphore()

    @pl.loop(1, ROWS)
    def _(d):
        pl.semaphore_signal(barrier, inc=1, device_id=(lax.rem(row + d, ROWS), col), device_id_type=MESH)

    @pl.loop(1, COLS)
    def _(d):
        pl.semaphore_signal(barrier, inc=1, device_id=(row, lax.rem(col + d, COLS)), device_id_type=MESH)

    def second_hop():
        pl.semaphore_wait(barrier, ROWS - 1 + COLS - 1)

        @pl.loop(1, COLS)
        def _(d):
            pl.semaphore_signal(hop_sem, inc=1, device_id=(row, lax.rem(col + d, COLS)), device_id_type=MESH)

    order = [(b, g, e) for b in range(2) for g in range(4) for e in range(2)]

    def make_masks():
        lane = lax.broadcasted_iota(jnp.int32, (8, CH), 1)
        mask = mask_in[...].astype(F32)
        number = lax.broadcasted_iota(jnp.int32, (8, 512), 1)
        sub = lax.broadcasted_iota(jnp.int32, (8, 512), 0)
        even_b = jnp.sum(jnp.where(number == TC * col + 2 * sub, mask, 0.0), axis=1, keepdims=True)
        odd_b = jnp.sum(jnp.where(number == TC * col + 2 * sub + 1, mask, 0.0), axis=1, keepdims=True)
        mask_b = jnp.where(lane < 64, even_b, odd_b)
        place = lax.broadcasted_iota(jnp.int32, (1, CH), 1)
        place = place - jnp.where(place >= 64, 64, 0)
        a_of = 16 * (place // 16) + (place // 8) % 2 + 2 * (place % 8)
        pick = jnp.where(lax.broadcasted_iota(jnp.int32, (512, CH), 0) == TR * row + a_of, 1.0, 0.0).astype(BF16)
        mask_a = jnp.dot(jnp.broadcast_to(mask, (8, 512)).astype(BF16), pick, preferred_element_type=F32)
        masks[...] = mask_a * mask_b

    def spread_out(ref, layer, n):
        gains[layer, n] = jnp.broadcast_to(ref[layer : layer + 1, :], (CH, CH)).T

    def prepare(layer):
        turned = wp_ref[layer].astype(F32).T
        for b in range(16):
            rows = [turned[128 * q + 8 * b : 128 * q + 8 * b + 8] for q in range(4)]
            wpt[layer, 32 * b : 32 * b + 32] = jnp.concatenate(rows, axis=0).astype(BF16)
        spread_out(gain_ref, layer, 0)
        spread_out(bias_ref, layer, 1)

    def prepare_out(layer):
        wgt[layer] = wg_ref[layer].astype(F32).T.astype(BF16)
        wot[layer] = wo_ref[layer].astype(F32).T.astype(BF16)
        spread_out(ogain_ref, layer, 2)
        spread_out(obias_ref, layer, 3)

    def twice(value):
        return jnp.concatenate([value, value], axis=1)

    def normalize(layer, t, values):
        center = values - jnp.mean(values, axis=0, keepdims=True)
        spread = jnp.mean(center * center, axis=0, keepdims=True)
        scaled = center * lax.rsqrt(spread + 1e-05) * twice(gains[layer, 0]) + twice(gains[layer, 1])
        part = scaled.astype(BF16)
        normed[:, 256 * t : 256 * t + 256] = part
        proj_all[:, 256 * t : 256 * t + 256] = jnp.dot(wpt[layer], part, preferred_element_type=F32)
        cur[t] = values

    def send(src, dst, to_row, to_col, send_sem, recv_sem, here):
        def local():
            pltpu.make_async_copy(src, dst, recv_sem).start()

        def remote():
            pltpu.make_async_remote_copy(
                src_ref=src, dst_ref=dst, send_sem=send_sem, recv_sem=recv_sem,
                device_id=(to_row, to_col), device_id_type=MESH,
            ).start()

        if here is None:
            remote()
        else:
            pl.when(here)(local)
            pl.when(jnp.logical_not(here))(remote)

    def sent(buffer, sem, home):
        count = buffer.shape[0]

        @pl.when(home)
        def _():
            part = buffer.at[pl.ds(0, count - 1)]
            pltpu.make_async_copy(part, part, sem).wait()

        @pl.when(jnp.logical_not(home))
        def _():
            pltpu.make_async_copy(buffer, buffer, sem).wait()

    def arrived(buffer, sem):
        pltpu.make_async_copy(buffer, buffer, sem).wait()

    def scatter(layer):
        to_core = y_lo if layer == 0 else col // 16
        corner = y_hi * 2 + core
        slot = z * 16 + x * 4 + corner if layer == 0 else z_low * 32 + row * 4 + corner
        dst = (recv1 if layer == 0 else recv2).at[slot]
        lows = [y_lo, 1 - y_lo]
        highs = [y_hi, 1 - y_hi]
        halves = [x // 2, 1 - x // 2]

        @pl.loop(0, 8)
        def _(g):
            colour, step = g // 4, lax.rem(g, 4)
            depths = [lax.rem(z + 4 + step, 8), lax.rem(z + 3 - step, 8)]
            blocks = [colour * 8 + depth for depth in depths]
            for n, block in enumerate(blocks):
                for s in range(8):
                    part = proj_all[pl.ds(pl.multiple_of(block * 32, 32), 32), CH * s : CH * s + CH]
                    keep = masks[s : s + 1, :]
                    stage[pl.ds(128 * n + s, 8, stride=16), :] = sigmoid(part[0:8]) * part[8:16] * keep
                    stage[pl.ds(128 * n + s + 8, 8, stride=16), :] = sigmoid(part[16:24]) * part[24:32] * keep
                tile[pl.ds(block * 8, 8)] = stage[128 * n : 128 * n + 128, :].reshape(8, 16, CH).astype(BF16)
            if layer == 0:
                @pl.when(g == 0)
                def _():
                    pl.semaphore_wait(hop_sem, COLS - 1)

            odd = [lax.rem(colour + depth, 2) for depth in depths]
            for dx in (1, 0):
                for dh in (1, 0):
                    for dl in (1, 0):
                        for n in range(2):
                            here = None
                            if n == 1 and dx + dh + dl == 0:
                                here = jnp.logical_and(g == 4 * colour_here + 3, to_core == core)
                            send(
                                tile.at[blocks[n] * 8 + halves[dx] * 4 + highs[dh] * 2 + lows[dl]], dst,
                                lows[dl] * 4 + halves[dx] * 2 + odd[n], depths[n] * 4 + highs[dh] * 2 + to_core,
                                send_sem.at[layer], in_sem.at[8 * layer + z], here,
                            )

        return to_core == core

    def make_gate(layer):
        for t in range(4):
            part = jnp.dot(wgt[layer], normed[:, 256 * t : 256 * t + 256], preferred_element_type=F32)
            gate[t] = sigmoid(part)

    def merge(first, second):
        low = lax.broadcasted_iota(jnp.int32, first.shape, 2) < 64
        even = jnp.where(low, first, pltpu.roll(second, 64, 2))
        odd = jnp.where(low, pltpu.roll(first, 64, 2), second)
        return even, odd

    def far_first(step, same):
        falling = (z_low < 2) == same
        return jnp.where(falling, 3 - step, step)

    def gather(layer):
        for step in range(8 if layer == 0 else 4):
            if layer == 0:
                recv, width, pairs = recv1, 16, 2
                place = lax.rem(z + (4, 5, 3, 6, 2, 7, 1, 0)[step], 8)
                sem = in_sem.at[place]
            else:
                recv, width, pairs = recv2, 32, 4
                place = far_first(step, z // 4 == core)
                sem = in_sem.at[8 + core * 4 + place]
            arrived(recv.at[pl.ds(place * width, width)], sem)
            rows = pl.ds(64 * step if layer == 0 else pl.multiple_of(place * 64, 64), 64)
            for p in range(pairs):
                first = recv[pl.ds(place * width + 8 * p, 4)].astype(F32)
                second = recv[pl.ds(place * width + 8 * p + 4, 4)].astype(F32)
                even, odd = merge(first, second)
                left = jnp.concatenate([even[:, :8], odd[:, :8]], axis=1).reshape(64, CH)
                right = jnp.concatenate([even[:, 8:], odd[:, 8:]], axis=1).reshape(64, CH)
                lanes = slice(128 * p, 128 * p + 128)
                if layer == 0:
                    mine_l[rows, lanes] = left.astype(BF16)
                    raw_r[rows, lanes] = right
                else:
                    mine_l2[rows, lanes] = left.astype(BF16)
                    mine_r[rows, lanes] = right.astype(BF16)
                if layer == 0 and step % 2 == 1:
                    block = slice(64 * step - 64, 64 * step + 64)
                    mine_r[lanes, block] = raw_r[block, lanes].T.astype(BF16)

    def quadrant(layer, q, right, dst):
        side = core if q == 0 else 1 - core
        lines = [lax.rem(x + n, 4) for n in range(4)]
        corners = [(y_hi if dy == 0 else 1 - y_hi) * 2 + (core if dc == 0 else 1 - core) for dy in range(2) for dc in range(2)]

        @pl.loop(0, 4)
        def _(step):
            depth = far_first(step, z // 4 == side)
            rows = right[pl.ds(pl.multiple_of(depth * 64, 64), 64), :]
            if layer == 0:
                mixed = jnp.dot(rows, mine_l[...], preferred_element_type=F32)
            else:
                mixed = lax.dot_general(rows, mine_l2[...], (((1,), (1,)), ((), ())), preferred_element_type=F32)
            base = q * 64 + depth * 16
            for p in range(2):
                block = mixed[:, 128 * p : 128 * p + 128].reshape(4, 16, CH)
                even, odd = merge(block[:, :8], block[:, 8:])
                outgoing[pl.ds(base + 8 * p, 4)] = even.astype(BF16)
                outgoing[pl.ds(base + 8 * p + 4, 4)] = odd.astype(BF16)
            for corner in (3, 2, 1, 0):
                for dx in (2, 1, 3, 0):
                    here = None
                    if corner == 0 and dx == 0:
                        here = jnp.logical_and(y_lo == core, side * 4 + depth == z)
                    send(
                        outgoing.at[base + lines[dx] * 4 + corners[corner]], dst,
                        core * 4 + lines[dx], (side * 4 + depth) * 4 + corners[corner],
                        ret_send.at[layer], ret_recv.at[2 * layer + colour_here], here,
                    )

    def multiply(layer):
        back = (back1 if layer == 0 else back2).at[own]
        swap = swap1 if layer == 0 else swap2
        gather(layer)
        exchange = pltpu.make_async_remote_copy(
            src_ref=mine_r, dst_ref=swap, send_sem=swap_send.at[layer], recv_sem=swap_recv.at[layer],
            device_id=(row, sibling), device_id_type=MESH,
        )
        exchange.start()
        quadrant(layer, 0, mine_r, back)
        exchange.wait_recv()
        quadrant(layer, 1, swap, back)
        exchange.wait_send()

    def finish(layer):
        back = back1 if layer == 0 else back2
        halves = []
        for colour in range(2):
            arrived(back.at[pl.ds(64 * colour, 64)], ret_recv.at[2 * layer + colour])
            total = jnp.zeros((8, CH), F32)
            for g in range(4 * colour, 4 * colour + 4):
                part = back[16 * g : 16 * g + 16].astype(F32)
                wide[128 * g : 128 * g + 128, :] = part.reshape(128, CH)
                total = total + jnp.sum(part, axis=0)
            mean = total * (1.0 / 64)
            total = jnp.zeros((8, CH), F32)
            for g in range(4 * colour, 4 * colour + 4):
                part = wide[128 * g : 128 * g + 128, :].reshape(16, 8, CH) - mean[None]
                total = total + jnp.sum(part * part, axis=0)
            halves.append((mean, total))
        (mean0, total0), (mean1, total1) = halves
        apart = 0.5 * (mean0 - mean1)
        means[...] = 0.5 * (mean0 + mean1)
        rstds[...] = lax.rsqrt((total0 + total1) * (1.0 / CH) + apart * apart + 1e-05)

    def updated(layer, t):
        pair_of = [2 * t, 2 * t + 1]
        mixed = jnp.concatenate([wide[pl.ds(s, CH, stride=8), :] for s in pair_of], axis=1)
        mean = jnp.concatenate([means[s : s + 1, :] for s in pair_of], axis=1)
        rstd = jnp.concatenate([rstds[s : s + 1, :] for s in pair_of], axis=1)
        out_normed = (mixed - mean) * rstd * twice(gains[layer, 2]) + twice(gains[layer, 3])
        update = jnp.dot(wot[layer], out_normed.astype(BF16), preferred_element_type=F32)
        return cur[t] + gate[t] * update

    loads[1].wait()
    make_masks()
    for n in (2, 3, 4):
        loads[n].wait()
    prepare(0)
    loads[0].wait()
    wide[...] = pair_ref[...].astype(F32).reshape(POS, CH)
    for t in range(4):
        rows = [
            wide[pl.ds(256 * g + 16 * e + 2 * s + b, 8, stride=32), :] for s in (2 * t, 2 * t + 1) for b, g, e in order
        ]
        normalize(0, t, jnp.concatenate(rows, axis=0).T)
        if t == 0:
            second_hop()
    home1 = scatter(0)
    multiply(0)
    for n in (5, 6, 7, 8):
        loads[n].wait()
    prepare_out(0)
    make_gate(0)
    prepare(1)
    prepare_out(1)
    sent(tile, send_sem.at[0], home1)
    finish(0)
    for t in range(4):
        normalize(1, t, updated(0, t).astype(BF16).astype(F32))
    home2 = scatter(1)
    sent(outgoing, ret_send.at[0], home1)
    multiply(1)
    make_gate(1)
    sent(tile, send_sem.at[1], home2)
    finish(1)
    for t in range(4):
        values = updated(1, t).T
        for n, (s, (b, g, e)) in enumerate([(s, place) for s in (2 * t, 2 * t + 1) for place in order]):
            stage[pl.ds(256 * g + 16 * e + 2 * s + b, 8, stride=32), :] = values[8 * n : 8 * n + 8]
    out_ref[...] = stage[...].reshape(TR, TC, CH).astype(BF16)
    sent(outgoing, ret_send.at[1], home1)


def shards(pair, residue_mask, in_gain, in_bias, proj_weight, gate_weight, out_gain, out_bias, out_weight):
    arguments = (
        pair, residue_mask.reshape(1, 512), in_gain, in_bias, proj_weight, gate_weight, out_gain, out_bias, out_weight
    )
    dma = pltpu.SemaphoreType.DMA
    return pl.pallas_call(
        kernel,
        out_shape=pltpu.VMEM((TR, TC, CH), BF16),
        in_specs=[pl.BlockSpec(memory_space=pltpu.HBM)] * 9,
        out_specs=pl.BlockSpec(memory_space=pltpu.VMEM),
        scratch_shapes=[pltpu.VMEM(value.shape, value.dtype) for value in arguments] + [
            pltpu.VMEM((POS, CH), F32),
            pltpu.VMEM((4, CH, 256), F32),
            pltpu.VMEM((4, CH, 256), F32),
            pltpu.VMEM((POS, CH), F32),
            pltpu.VMEM((8, CH), F32),
            pltpu.VMEM((8, CH), F32),
            pltpu.VMEM((8, CH), F32),
            pltpu.VMEM((CH, POS), BF16),
            pltpu.VMEM((2, 512, CH), BF16),
            pltpu.VMEM((512, POS), F32),
            pltpu.VMEM((2, CH, CH), BF16),
            pltpu.VMEM((2, CH, CH), BF16),
            pltpu.VMEM((2, 4, CH, CH), F32),
            pltpu.VMEM((CH, 16, CH), BF16),
            pltpu.VMEM((CH, 16, CH), BF16),
            pltpu.VMEM((CH, 16, CH), BF16),
            pltpu.VMEM((CH, 8, CH), BF16),
            pltpu.VMEM((CH, 8, CH), BF16),
            pltpu.VMEM((256, 512), BF16),
            pltpu.VMEM((256, 512), BF16),
            pltpu.VMEM((256, 512), BF16),
            pltpu.VMEM((512, 256), BF16),
            pltpu.VMEM((256, 512), BF16),
            pltpu.VMEM((512, 256), F32),
            pltpu.VMEM((CH, 8, CH), BF16),
            dma((9,)),
            pltpu.SemaphoreType.REGULAR,
            dma((2,)), dma((16,)), dma((2,)), dma((2,)), dma((2,)), dma((4,)),
        ],
        compiler_params=pltpu.CompilerParams(
            collective_id=0, has_side_effects=True, vmem_limit_bytes=48 * 1024 * 1024
        ),
        cost_estimate=pl.CostEstimate(flops=700_000_000, bytes_accessed=4_000_000, transcendentals=1_000_000),
    )(*[pltpu.with_memory_space_constraint(value, pltpu.HBM) for value in arguments])


def solution(mesh):
    placed = (P("row", "col", None), P(), P(), P(), P(), P(), P(), P(), P())
    return jax.shard_map(
        shards, mesh=mesh, in_specs=placed, out_specs=P("row", "col", None), check_vma=False
    )
```
